256 devices in a mesh: chan: 16 (over z, core), row: 4 (over x), col: 4 (over y).
Axes of the slice: x: 4, y: 4, z: 8, core: 2. Of those that a mesh axis runs over, the one named last changes fastest.
Arguments:
- voltages: bfloat16 [2, 1024, 131072], P(None, 'chan', ('row', 'col')), may hold values from -6 to 6
- input_flags: int32 [1024], P('chan'), may hold values 0 or 1
- channel_order: int32 [128], replicated, may hold values from 0 to 127, each once
- beam_weights: bfloat16 [2, 128, 256, 1024], P(None, 'chan', 'col'), may hold values from -0.1875 to 0.1875
Outputs:
- visibility: float32 [2, 128, 1024, 1024], P(None, 'chan', 'row', 'col')
- beam_power: float32 [128, 256, 128], P('chan', 'col', 'row')
The draws below stay inside these ranges and needn't reach their ends.
Inputs may be any that keep to these rules, and one draw needn't show every extreme that they name: `channel_order`: every fine channel appears exactly once.
All inputs are finite; a program needn't handle non-finite values. No bound on the sum of `input_flags` on one device may be relied on, other than what follows from the above.
Results may differ from the reference program's by a relative error of at most 0.005.
Values may be sent and summed in bfloat16 or wider, within the bound.
No kernel may reach another device: no remote copies, remote signals or barrier semaphores. Data moves between devices by JAX's collectives and lax.ppermute only.
A program may use at most 128 MiB of HBM per device.

```python
import math
import jax
import jax.numpy as jnp
from jax import lax

INPUTS = 1024
NCH = 128
TAPS = 4
BEAMS = 256
INTEG = 8
FRAMES = 1024
BINS = 128


def touch_ends(result, own_key, low, largest):
    index_at = [jax.random.randint(jax.random.fold_in(own_key, axis), (), 0, length) for axis, length in enumerate(result.shape)]
    widest = result.shape.index(max(result.shape))
    neighbour = index_at[:widest] + [(index_at[widest] + 1) % result.shape[widest]] + index_at[widest + 1:]
    return result.at[tuple(index_at)].set(low).at[tuple(neighbour)].set(largest)


def levels(stream_key, shape, pieces, least, largest):
    loudness = 1.0
    for dim, parts in pieces:
        draws = jax.random.uniform(jax.random.fold_in(jax.random.fold_in(stream_key, 6), dim), (parts,), jnp.float32, least / len(pieces), largest / len(pieces))
        loudness = loudness * jnp.repeat(jnp.exp(draws), shape[dim] // parts).reshape((-1,) + (1,) * (len(shape) - 1 - dim))
    return loudness


def normal_values(key, dims, spread, most, pieces=(), kind=jnp.bfloat16):
    level = levels(key, dims, pieces, -0.22, 0.18) if pieces else 1.0
    drawn = jax.random.normal(key, dims, jnp.float32) * spread * level
    return jnp.minimum(jnp.maximum(drawn, -most), most).astype(kind)


def setup_inputs(seed: int = 0) -> dict:
    seeds = jax.random.split(jax.random.key(seed), 5)
    voltages = normal_values(seeds[0], (2, INPUTS, FRAMES * NCH), 1.0, 6.0, ((1, 16), (2, 16)))
    input_flags = touch_ends((jax.random.randint(seeds[1], (INPUTS,), 0, 8) < 7).astype(jnp.int32), jax.random.fold_in(seeds[1], 1), 0, 1)
    channel_order = jax.random.permutation(seeds[2], NCH).astype(jnp.int32)
    beam_weights = normal_values(seeds[3], (2, NCH, BEAMS, INPUTS), INPUTS ** -0.5, 0.1875, ((1, 16), (2, 4)))
    return {"voltages": voltages, "input_flags": input_flags, "channel_order": channel_order, "beam_weights": beam_weights}


def prototype(taps, length):
    position = jnp.arange(taps * length, dtype=jnp.float32) + 0.5
    offset = position / length - taps / 2.0
    window = 0.5 - 0.5 * jnp.cos(2.0 * math.pi * position / (taps * length))
    return (jnp.sin(math.pi * offset) / (math.pi * offset) * window).reshape(taps, length)

def dft_tables(channel_rows, length):
    sample_index = jnp.arange(length, dtype=jnp.int32)
    product = channel_rows[:, None] * sample_index[None, :] % length
    angle = 2.0 * math.pi / length * product.astype(jnp.float32)
    factor = 1.0 / math.sqrt(length)
    cosine = jnp.cos(angle) * factor
    sine = jnp.sin(angle) * factor
    real_rows = jnp.stack([cosine, sine], axis=1)
    imag_rows = jnp.stack([-sine, cosine], axis=1)
    return jnp.stack([real_rows, imag_rows], axis=1).astype(jnp.bfloat16)

def reference(voltages, input_flags, channel_order, beam_weights):
    masked = voltages * input_flags.astype(jnp.bfloat16)[None, :, None]
    padded = jnp.concatenate([jnp.zeros((2, INPUTS, (TAPS - 1) * NCH), jnp.bfloat16), masked], axis=2)
    blocks = padded.reshape(2, INPUTS, FRAMES + TAPS - 1, NCH)
    coeffs = prototype(TAPS, NCH)
    filtered = jnp.zeros((2, INPUTS, FRAMES, NCH), jnp.float32)
    for tap_index in range(TAPS):
        filtered = filtered + coeffs[tap_index] * blocks[:, :, tap_index:tap_index + FRAMES].astype(jnp.float32)
    filtered = filtered.astype(jnp.bfloat16)
    tables = dft_tables(jnp.arange(NCH, dtype=jnp.int32), NCH)
    spectrum = jnp.einsum('kqpn,pifn->kiqf', tables.astype(jnp.float32), filtered.astype(jnp.float32), precision=lax.Precision.HIGHEST).astype(jnp.bfloat16)
    ordered = spectrum[channel_order]
    weights_by_channel = jnp.transpose(beam_weights, (1, 0, 2, 3))

    def per_channel(items):
        block, weights = items
        real_part = block[:, 0].astype(jnp.float32)
        imag_part = block[:, 1].astype(jnp.float32)
        vis_re = (jnp.dot(real_part, real_part.T, precision=lax.Precision.HIGHEST) + jnp.dot(imag_part, imag_part.T, precision=lax.Precision.HIGHEST)) / FRAMES
        vis_im = (jnp.dot(imag_part, real_part.T, precision=lax.Precision.HIGHEST) - jnp.dot(real_part, imag_part.T, precision=lax.Precision.HIGHEST)) / FRAMES
        w_real = weights[0].astype(jnp.float32)
        w_imag = weights[1].astype(jnp.float32)
        beam_re = jnp.dot(w_real, real_part, precision=lax.Precision.HIGHEST) - jnp.dot(w_imag, imag_part, precision=lax.Precision.HIGHEST)
        beam_im = jnp.dot(w_real, imag_part, precision=lax.Precision.HIGHEST) + jnp.dot(w_imag, real_part, precision=lax.Precision.HIGHEST)
        power = beam_re * beam_re + beam_im * beam_im
        binned = power.reshape(BEAMS, BINS, INTEG).mean(axis=-1)
        return (jnp.stack([vis_re, vis_im]), binned)
    vis_all, beam_power = lax.map(per_channel, (ordered, weights_by_channel))
    visibility = jnp.transpose(vis_all, (1, 0, 2, 3))
    return (visibility, beam_power)
```

```python
import functools
import math

import jax
import jax.numpy as jnp
import numpy as np
from jax import lax
from jax.experimental import pallas as pl
from jax.experimental.pallas import tpu as pltpu
from jax.sharding import PartitionSpec as P

NCH = 128
TAPS = 4
INTEG = 8
CHUNKS = (4, 4)

F32 = jnp.float32
BF16 = jnp.bfloat16


def prototype(taps, length):
    position = np.arange(taps * length, dtype=np.float32) + np.float32(0.5)
    offset = position / np.float32(length) - np.float32(taps / 2.0)
    window = 0.5 - 0.5 * np.cos(2.0 * math.pi * position.astype(np.float64) / (taps * length))
    sinc = np.sin(math.pi * offset.astype(np.float64)) / (math.pi * offset.astype(np.float64))
    return (sinc * window).astype(np.float32).reshape(taps, length)


def dft_table(length):
    index = np.arange(length)
    angle = 2.0 * math.pi / length * (index[:, None] * index[None, :] % length)
    factor = 1.0 / math.sqrt(length)
    table = np.concatenate([np.cos(angle) * factor, np.sin(angle) * factor], axis=1)
    return table.astype(np.float32).astype(jnp.bfloat16)


def passed_along(value, axis, steps):
    count = lax.axis_size(axis)
    initial, last = (max(0, -steps), min(count, count - steps))
    return lax.ppermute(value, axis, [(source, source + steps) for source in range(initial, last)])


def spectrum_kernel(chunks, v_ref, halo_ref, flags_ref, order_ref, coeff_ref, table_ref, *rest):
    outs, (filt_ref, spec_ref) = rest[: len(chunks)], rest[len(chunks) :]
    inputs = v_ref.shape[1]
    frames = v_ref.shape[2] // NCH
    eye = lax.broadcasted_iota(jnp.int32, (inputs, inputs), 0) == lax.broadcasted_iota(
        jnp.int32, (inputs, inputs), 1
    )
    flags = jnp.where(eye, flags_ref[...].astype(F32), 0.0)
    mask = jnp.broadcast_to(jnp.sum(flags, axis=1, keepdims=True), (inputs, NCH))
    taps = [jnp.broadcast_to(coeff_ref[t : t + 1, :], (inputs, NCH)) for t in range(TAPS)]

    for part in range(2):
        past = tuple(
            halo_ref[part, :, t * NCH : (t + 1) * NCH].astype(F32) * mask for t in range(TAPS - 1)
        )

        def frame_step(f, past, part=part):
            lanes = pl.ds(pl.multiple_of(f * NCH, NCH), NCH)
            now = v_ref[part, :, lanes].astype(F32) * mask
            window = past + (now,)
            total = taps[0] * window[0]
            for t in range(1, TAPS):
                total = total + taps[t] * window[t]
            filt_ref[part, pl.ds(f, inputs, stride=frames), :] = total
            return window[1:]

        lax.fori_loop(0, frames, frame_step, past, unroll=4)

    onehot = (
        lax.broadcasted_iota(jnp.int32, (NCH, NCH), 0) == jnp.broadcast_to(order_ref[...], (NCH, NCH))
    )
    rows = lax.dot_general(
        onehot.astype(BF16), table_ref[...], (((0,), (0,)), ((), ())), preferred_element_type=F32
    ).astype(BF16)

    def input_step(pair, carry):
        blocks = []
        for which in range(2):
            i = pair * 2 + which
            at = pl.ds(pl.multiple_of(i * frames, frames), frames)
            re = filt_ref[0, at, :].astype(BF16)
            im = filt_ref[1, at, :].astype(BF16)
            blocks.append(jnp.concatenate([re, im], axis=1))
            blocks.append(jnp.concatenate([im, -re], axis=1))
        right = jnp.concatenate(blocks, axis=0)
        result = lax.dot_general(
            rows, right, (((1,), (1,)), ((), ())), preferred_element_type=F32
        )
        for which in range(2):
            spec_ref[pl.ds(pair * 2 + which, NCH, stride=inputs), :] = result[
                :, which * NCH : (which + 1) * NCH
            ]
        return carry

    lax.fori_loop(0, inputs // 2, input_step, 0, unroll=2)

    per_block = sum(chunks)
    blocks = NCH // per_block

    def copy_step(block, carry):
        first = 0
        for out, size in zip(outs, chunks):
            for k in range(size):
                at = pl.multiple_of((block * per_block + first + k) * inputs, inputs)
                out[block, k] = spec_ref[pl.ds(at, inputs), :].astype(BF16)
            first += size
        return carry

    lax.fori_loop(0, blocks, copy_step, 0)


def spectra(voltages, halo, flags, order, chunks):
    inputs = voltages.shape[1]
    frames = voltages.shape[2] // NCH
    blocks = NCH // sum(chunks)
    vmem = pl.BlockSpec(memory_space=pltpu.VMEM)
    return pl.pallas_call(
        functools.partial(spectrum_kernel, chunks),
        out_shape=[jax.ShapeDtypeStruct((blocks, size, inputs, 2 * frames), BF16) for size in chunks],
        in_specs=[vmem] * 6,
        out_specs=[vmem] * len(chunks),
        scratch_shapes=[
            pltpu.VMEM((2, inputs * frames, NCH), F32),
            pltpu.VMEM((NCH * inputs, 2 * frames), F32),
        ],
        compiler_params=pltpu.CompilerParams(vmem_limit_bytes=40 * 2**20),
        cost_estimate=pl.CostEstimate(
            flops=2 * 2 * NCH * NCH * 2 * inputs * frames,
            bytes_accessed=8 * 2**20,
            transcendentals=0,
        ),
    )(
        voltages,
        halo,
        flags.reshape(1, inputs),
        order.reshape(1, NCH),
        jnp.asarray(prototype(TAPS, NCH)),
        jnp.asarray(dft_table(NCH)),
    )


def product_kernel(col_ref, own_ref, prev_ref, next_ref, far_lo_ref, far_hi_ref, w_ref, vis_ref, beam_ref, x_ref, r_ref):
    col = col_ref[0]
    blocks, _, inputs, lanes = own_ref.shape
    half = blocks // 2
    total = blocks * inputs
    groups = vis_ref.shape[0]
    panel = total // groups
    for s, ref in enumerate((own_ref, prev_ref, next_ref)):
        x_ref[:, s * lanes : (s + 1) * lanes] = ref[:, 0].reshape(total, lanes)
    x_ref[: half * inputs, 3 * lanes :] = far_lo_ref[:, 0].reshape(half * inputs, lanes)
    x_ref[half * inputs :, 3 * lanes :] = far_hi_ref[:, 0].reshape(half * inputs, lanes)
    mine = x_ref[pl.ds(pl.multiple_of(col * panel, panel), panel), :]
    r_ref[:panel] = mine
    first = lax.broadcasted_iota(jnp.int32, (panel, lanes), 1) < lanes // 2
    for s in range(4):
        turned = pltpu.roll(mine[:, s * lanes : (s + 1) * lanes].astype(F32), lanes // 2, axis=1)
        r_ref[panel:, s * lanes : (s + 1) * lanes] = jnp.where(first, -turned, turned).astype(BF16)
    scale = 1.0 / (NCH * 8)
    for g in range(groups):
        result = lax.dot_general(
            x_ref[g * panel : (g + 1) * panel],
            r_ref[...],
            (((1,), (1,)), ((), ())),
            preferred_element_type=F32,
        )
        result = (result * scale).astype(BF16)
        vis_ref[g, 0, 0] = result[:, :panel]
        vis_ref[g, 1, 0] = result[:, panel:]
    beams = w_ref.shape[2]
    weights = w_ref[:, 0].reshape(2 * beams, total)
    parts = lax.dot_general(
        weights, x_ref[...], (((1,), (0,)), ((), ())), preferred_element_type=F32
    )
    first = lax.broadcasted_iota(jnp.int32, (beams, lanes), 1) < lanes // 2
    bins = lanes // 2 // INTEG
    power = jnp.zeros((beams, 4 * bins), F32)
    for s, shift in enumerate((0, 3, 1, 2)):
        piece = parts[:, s * lanes : (s + 1) * lanes]
        turned = pltpu.roll(piece[beams:], lanes // 2, axis=1)
        value = piece[:beams] + jnp.where(first, -turned, turned)
        lane = lax.broadcasted_iota(jnp.int32, (lanes, 4 * bins), 0)
        place = lax.broadcasted_iota(jnp.int32, (lanes, 4 * bins), 1)
        source = lax.rem(col + shift, 4)
        wanted = source * bins + lax.rem(lane, lanes // 2) // INTEG
        pool = jnp.where(place == wanted, 1.0 / INTEG, 0.0).astype(F32)
        power = power + lax.dot_general(
            value * value,
            pool,
            (((1,), (0,)), ((), ())),
            precision=lax.Precision.HIGHEST,
            preferred_element_type=F32,
        )
    beam_ref[0] = power


def products(col, slots, weights, first):
    own = slots[0]
    blocks, size, inputs, lanes = own.shape
    beams = weights.shape[2]
    total = blocks * inputs
    panel = total // 4
    bins = 4 * (lanes // 2 // INTEG)

    def data(count):
        return pl.BlockSpec((count, 1, inputs, lanes), lambda k, c: (0, k, 0, 0))

    return pl.pallas_call(
        product_kernel,
        out_shape=[
            jax.ShapeDtypeStruct((4, 2, size, panel, panel), BF16),
            jax.ShapeDtypeStruct((size, beams, bins), F32),
        ],
        grid_spec=pltpu.PrefetchScalarGridSpec(
            num_scalar_prefetch=1,
            grid=(size,),
            in_specs=[
                data(blocks),
                data(blocks),
                data(blocks),
                data(blocks // 2),
                data(blocks // 2),
                pl.BlockSpec((2, 1, beams, total), lambda k, c: (0, first + k, 0, 0)),
            ],
            out_specs=[
                pl.BlockSpec((4, 2, 1, panel, panel), lambda k, c: (0, 0, k, 0, 0)),
                pl.BlockSpec((1, beams, bins), lambda k, c: (k, 0, 0)),
            ],
            scratch_shapes=[
                pltpu.VMEM((total, 4 * lanes), BF16),
                pltpu.VMEM((2 * panel, 4 * lanes), BF16),
            ],
        ),
        compiler_params=pltpu.CompilerParams(vmem_limit_bytes=40 * 2**20),
        cost_estimate=pl.CostEstimate(
            flops=2 * size * total * 4 * lanes * (2 * panel + 2 * beams),
            bytes_accessed=size * (2 * total * 4 * lanes + 4 * total * panel * 2),
            transcendentals=0,
        ),
    )(col, *slots, weights)


def gathered(block):
    count = lax.axis_size("col")
    up = [(i, (i + 1) % count) for i in range(count)]
    down = [(i, (i - 1) % count) for i in range(count)]
    half = block.shape[0] // 2
    from_prev = lax.ppermute(block, "col", up)
    from_next = lax.ppermute(block, "col", down)
    far_lo = lax.ppermute(from_prev[:half], "col", up)
    far_hi = lax.ppermute(from_next[half:], "col", down)
    return (block, from_prev, from_next, far_lo, far_hi)


def on_device(voltages, input_flags, channel_order, beam_weights):
    history = passed_along(voltages[:, :, voltages.shape[2] - (TAPS - 1) * NCH :], ("row", "col"), 1)
    flags = input_flags
    pieces = spectra(voltages, history, flags, channel_order, CHUNKS)
    col = lax.axis_index("col").astype(jnp.int32).reshape(1)
    vis = []
    power = []
    first = 0
    for piece, size in zip(pieces, CHUNKS):
        turned = lax.all_to_all(piece, "chan", split_axis=0, concat_axis=0, tiled=True)
        partial, beam = products(col, gathered(turned), beam_weights, first)
        summed = lax.psum_scatter(partial, "row", scatter_dimension=0, tiled=True)
        vis.append(summed[0].astype(F32))
        power.append(beam)
        first += size
    return (jnp.concatenate(vis, axis=1), jnp.concatenate(power, axis=0))


def solution(mesh):
    placed = (P(None, "chan", ("row", "col")), P("chan"), P(), P(None, "chan", "col", None))
    return jax.shard_map(
        on_device,
        mesh=mesh,
        in_specs=placed,
        out_specs=(P(None, "chan", "row", "col"), P("chan", "col", "row")),
        check_vma=False,
    )
```

```python
import functools
import math

import jax
import jax.numpy as jnp
import numpy as np
from jax import lax
from jax.experimental import pallas as pl
from jax.experimental.pallas import tpu as pltpu
from jax.sharding import PartitionSpec as P

NCH = 128
TAPS = 4
INTEG = 8
CHUNKS = (2, 2, 2, 2)

F32 = jnp.float32
BF16 = jnp.bfloat16
SMALL = pl.CostEstimate(flops=1, bytes_accessed=1, transcendentals=0)


def prototype(taps, length):
    position = np.arange(taps * length, dtype=np.float32) + np.float32(0.5)
    offset = position / np.float32(length) - np.float32(taps / 2.0)
    window = 0.5 - 0.5 * np.cos(2.0 * math.pi * position.astype(np.float64) / (taps * length))
    sinc = np.sin(math.pi * offset.astype(np.float64)) / (math.pi * offset.astype(np.float64))
    return (sinc * window).astype(np.float32).reshape(taps, length)


def dft_table(length):
    index = np.arange(length)
    angle = 2.0 * math.pi / length * (index[:, None] * index[None, :] % length)
    factor = 1.0 / math.sqrt(length)
    table = np.concatenate([np.cos(angle) * factor, np.sin(angle) * factor], axis=1)
    return table.astype(np.float32).astype(jnp.bfloat16)


def passed_along(value, axis, steps):
    count = lax.axis_size(axis)
    initial, last = (max(0, -steps), min(count, count - steps))
    return lax.ppermute(value, axis, [(source, source + steps) for source in range(initial, last)])


def spectrum_kernel(
    place_ref, v_ref, halo_ref, flags_ref, order_ref, coeff_ref, table_ref, mine_ref, theirs_ref, filt_ref, spec_ref
):
    inputs = v_ref.shape[1]
    frames = v_ref.shape[2] // NCH
    eye = lax.broadcasted_iota(jnp.int32, (inputs, inputs), 0) == lax.broadcasted_iota(
        jnp.int32, (inputs, inputs), 1
    )
    flags = jnp.where(eye, flags_ref[...].astype(F32), 0.0)
    mask = jnp.broadcast_to(jnp.sum(flags, axis=1, keepdims=True), (inputs, NCH))
    taps = [jnp.broadcast_to(coeff_ref[t : t + 1, :], (inputs, NCH)) for t in range(TAPS)]

    for part in range(2):
        past = tuple(
            halo_ref[part, :, t * NCH : (t + 1) * NCH].astype(F32) * mask for t in range(TAPS - 1)
        )

        def frame_step(f, past, part=part):
            lanes = pl.ds(pl.multiple_of(f * NCH, NCH), NCH)
            now = v_ref[part, :, lanes].astype(F32) * mask
            window = past + (now,)
            total = taps[0] * window[0]
            for t in range(1, TAPS):
                total = total + taps[t] * window[t]
            filt_ref[part, pl.ds(f, inputs, stride=frames), :] = total
            return window[1:]

        lax.fori_loop(0, frames, frame_step, past, unroll=4)

    onehot = (
        lax.broadcasted_iota(jnp.int32, (NCH, NCH), 0) == jnp.broadcast_to(order_ref[...], (NCH, NCH))
    )
    rows = lax.dot_general(
        onehot.astype(BF16), table_ref[...], (((0,), (0,)), ((), ())), preferred_element_type=F32
    ).astype(BF16)

    def input_step(pair, carry):
        blocks = []
        for which in range(2):
            i = pair * 2 + which
            at = pl.ds(pl.multiple_of(i * frames, frames), frames)
            re = filt_ref[0, at, :].astype(BF16)
            im = filt_ref[1, at, :].astype(BF16)
            blocks.append(jnp.concatenate([re, im], axis=1))
            blocks.append(jnp.concatenate([im, -re], axis=1))
        right = jnp.concatenate(blocks, axis=0)
        result = lax.dot_general(
            rows, right, (((1,), (1,)), ((), ())), preferred_element_type=F32
        )
        for which in range(2):
            spec_ref[pl.ds(pair * 2 + which, NCH, stride=inputs), :] = result[
                :, which * NCH : (which + 1) * NCH
            ]
        return carry

    lax.fori_loop(0, inputs // 2, input_step, 0, unroll=2)

    chan = place_ref[0]
    core = lax.rem(chan, 2)
    steps, size = mine_ref.shape[:2]

    def copy_step(step, carry):
        target = lax.rem(chan // 2 + step, steps) * 2
        for out, which in ((mine_ref, core), (theirs_ref, 1 - core)):
            for k in range(size):
                at = pl.multiple_of(((target + which) * size + k) * inputs, inputs)
                out[step, k] = spec_ref[pl.ds(at, inputs), :].astype(BF16)
        return carry

    lax.fori_loop(0, steps, copy_step, 0)


def spectra(place, voltages, halo, flags, order, blocks):
    inputs = voltages.shape[1]
    frames = voltages.shape[2] // NCH
    vmem = pl.BlockSpec(memory_space=pltpu.VMEM)
    shape = jax.ShapeDtypeStruct((blocks // 2, NCH // blocks, inputs, 2 * frames), BF16)
    return pl.pallas_call(
        spectrum_kernel,
        out_shape=[shape, shape],
        in_specs=[pl.BlockSpec(memory_space=pltpu.SMEM)] + [vmem] * 6,
        out_specs=[vmem] * 2,
        scratch_shapes=[
            pltpu.VMEM((2, inputs * frames, NCH), F32),
            pltpu.VMEM((NCH * inputs, 2 * frames), F32),
        ],
        compiler_params=pltpu.CompilerParams(vmem_limit_bytes=24 * 2**20),
        cost_estimate=SMALL,
    )(
        place,
        voltages,
        halo,
        flags.reshape(1, inputs),
        order.reshape(1, NCH),
        jnp.asarray(prototype(TAPS, NCH)),
        jnp.asarray(dft_table(NCH)),
    )


def repack_kernel(first, size, place_ref, mine_ref, theirs_ref, *refs):
    core = lax.rem(place_ref[0], 2)
    steps = mine_ref.shape[0]
    for step, out in enumerate(refs[-steps:]):
        out[core] = mine_ref[step, first : first + size]
        out[1 - core] = theirs_ref[step, first : first + size]


def call(kernel, out_shape, args, after, place=None):
    vmem = pl.BlockSpec(memory_space=pltpu.VMEM)
    specs = [vmem] * len(args) + [pl.BlockSpec(memory_space=pl.ANY)] * len(after)
    args = [*args, *after]
    if place is not None:
        specs = [pl.BlockSpec(memory_space=pltpu.SMEM)] + specs
        args = [place] + args
    return pl.pallas_call(
        kernel,
        out_shape=out_shape,
        in_specs=specs,
        out_specs=[vmem] * len(out_shape),
        cost_estimate=SMALL,
    )(*args)


def repacked(place, mine, theirs, first, size, after):
    steps, _, inputs, lanes = mine.shape
    shapes = [jax.ShapeDtypeStruct((2, size, inputs, lanes), BF16)] * steps
    return call(functools.partial(repack_kernel, first, size), shapes, [mine, theirs], after, place)


def pack_kernel(steps, place_ref, *refs):
    out = refs[-1]
    mine = place_ref[0] // 2
    for step, piece in enumerate(refs[:steps]):
        source = lax.rem(mine + steps - step, steps)
        out[pl.ds(source * 2, 2)] = piece[...]


def packed(place, pieces, after):
    steps = len(pieces)
    _, size, inputs, lanes = pieces[0].shape
    shapes = [jax.ShapeDtypeStruct((2 * steps, size, inputs, lanes), BF16)]
    return call(functools.partial(pack_kernel, steps), shapes, pieces, after, place)[0]


def halves_kernel(low_ref, high_ref, *refs):
    low_out, high_out = refs[-2:]
    half = low_out.shape[0]
    low_out[...] = low_ref[:half]
    high_out[...] = high_ref[half:]


def halves(low, high, after):
    shape = jax.ShapeDtypeStruct((low.shape[0] // 2,) + low.shape[1:], BF16)
    return call(halves_kernel, [shape, shape], [low, high], after)


def product_kernel(
    col_ref, own_ref, prev_ref, next_ref, far_lo_ref, far_hi_ref, w_ref, *refs
):
    vis_ref, beam_ref, x_ref, r_ref = refs[-4:]
    col = col_ref[0]
    blocks, _, inputs, lanes = own_ref.shape
    half = blocks // 2
    total = blocks * inputs
    groups = vis_ref.shape[0]
    panel = total // groups
    for s, ref in enumerate((own_ref, prev_ref, next_ref)):
        x_ref[:, s * lanes : (s + 1) * lanes] = ref[:, 0].reshape(total, lanes)
    x_ref[: half * inputs, 3 * lanes :] = far_lo_ref[:, 0].reshape(half * inputs, lanes)
    x_ref[half * inputs :, 3 * lanes :] = far_hi_ref[:, 0].reshape(half * inputs, lanes)
    mine = x_ref[pl.ds(pl.multiple_of(col * panel, panel), panel), :]
    r_ref[:panel] = mine
    first = lax.broadcasted_iota(jnp.int32, (panel, lanes), 1) < lanes // 2
    for s in range(4):
        turned = pltpu.roll(mine[:, s * lanes : (s + 1) * lanes].astype(F32), lanes // 2, axis=1)
        r_ref[panel:, s * lanes : (s + 1) * lanes] = jnp.where(first, -turned, turned).astype(BF16)
    scale = 1.0 / (NCH * 8)
    for g in range(groups):
        result = lax.dot_general(
            x_ref[g * panel : (g + 1) * panel],
            r_ref[...],
            (((1,), (1,)), ((), ())),
            preferred_element_type=F32,
        )
        result = (result * scale).astype(BF16)
        vis_ref[g, 0, 0] = result[:, :panel]
        vis_ref[g, 1, 0] = result[:, panel:]
    beams = w_ref.shape[2]
    weights = w_ref[:, 0].reshape(2 * beams, total)
    parts = lax.dot_general(
        weights, x_ref[...], (((1,), (0,)), ((), ())), preferred_element_type=F32
    )
    first = lax.broadcasted_iota(jnp.int32, (beams, lanes), 1) < lanes // 2
    bins = lanes // 2 // INTEG
    power = jnp.zeros((beams, 4 * bins), F32)
    for s, shift in enumerate((0, 3, 1, 2)):
        piece = parts[:, s * lanes : (s + 1) * lanes]
        turned = pltpu.roll(piece[beams:], lanes // 2, axis=1)
        value = piece[:beams] + jnp.where(first, -turned, turned)
        lane = lax.broadcasted_iota(jnp.int32, (lanes, 4 * bins), 0)
        place = lax.broadcasted_iota(jnp.int32, (lanes, 4 * bins), 1)
        source = lax.rem(col + shift, 4)
        wanted = source * bins + lax.rem(lane, lanes // 2) // INTEG
        pool = jnp.where(place == wanted, 1.0 / INTEG, 0.0).astype(F32)
        power = power + lax.dot_general(
            value * value,
            pool,
            (((1,), (0,)), ((), ())),
            precision=lax.Precision.HIGHEST,
            preferred_element_type=F32,
        )
    beam_ref[0] = power


def products(col, slots, weights, first, after):
    own = slots[0]
    blocks, size, inputs, lanes = own.shape
    beams = weights.shape[2]
    total = blocks * inputs
    panel = total // 4
    bins = 4 * (lanes // 2 // INTEG)

    def data(count):
        return pl.BlockSpec((count, 1, inputs, lanes), lambda k, c: (0, k, 0, 0))

    return pl.pallas_call(
        product_kernel,
        out_shape=[
            jax.ShapeDtypeStruct((4, 2, size, panel, panel), BF16),
            jax.ShapeDtypeStruct((size, beams, bins), F32),
        ],
        grid_spec=pltpu.PrefetchScalarGridSpec(
            num_scalar_prefetch=1,
            grid=(size,),
            in_specs=[
                data(blocks),
                data(blocks),
                data(blocks),
                data(blocks // 2),
                data(blocks // 2),
                pl.BlockSpec((2, 1, beams, total), lambda k, c: (0, first + k, 0, 0)),
            ]
            + [pl.BlockSpec(memory_space=pl.ANY)] * len(after),
            out_specs=[
                pl.BlockSpec((4, 2, 1, panel, panel), lambda k, c: (0, 0, k, 0, 0)),
                pl.BlockSpec((1, beams, bins), lambda k, c: (k, 0, 0)),
            ],
            scratch_shapes=[
                pltpu.VMEM((total, 4 * lanes), BF16),
                pltpu.VMEM((2 * panel, 4 * lanes), BF16),
            ],
        ),
        compiler_params=pltpu.CompilerParams(vmem_limit_bytes=20 * 2**20),
        cost_estimate=pl.CostEstimate(flops=44000000000, bytes_accessed=1, transcendentals=0),
    )(col, *slots, weights, *after)


def along(value, axis, step, steps, inner=1):
    pairs = [
        ((g * inner) + i, ((g + step) % steps) * inner + i) for g in range(steps) for i in range(inner)
    ]
    return lax.ppermute(value, axis, pairs)


def on_device(voltages, input_flags, channel_order, beam_weights):
    count = lax.axis_size("chan")
    cols = lax.axis_size("col")
    steps = count // 2
    early = steps // 2
    history = passed_along(voltages[:, :, voltages.shape[2] - (TAPS - 1) * NCH :], ("row", "col"), 1)
    place = lax.axis_index("chan").astype(jnp.int32).reshape(1)
    col = lax.axis_index("col").astype(jnp.int32).reshape(1)
    mine, theirs = spectra(place, voltages, history, input_flags, channel_order, count)
    theirs = lax.ppermute(theirs, "chan", [(c, c ^ 1) for c in range(count)])
    starts = [sum(CHUNKS[:g]) for g in range(len(CHUNKS))]

    def turn(g, after):
        pieces = repacked(place, mine, theirs, starts[g], CHUNKS[g], after)
        return [pieces[0]] + [along(pieces[d], "chan", d, steps, 2) for d in range(1, steps)]

    vis = []
    power = []

    def finish(g, slots, after):
        partial, beam = products(col, slots, beam_weights, starts[g], after)
        vis.append(lax.psum_scatter(partial, "row", scatter_dimension=0, tiled=True)[0].astype(F32))
        power.append(beam)
        return beam

    own = packed(place, turn(0, []), [])
    waiting = None
    for g in range(len(CHUNKS)):
        from_prev = along(own, "col", 1, cols)
        from_next = along(own, "col", cols - 1, cols)
        after = []
        if g + 1 < len(CHUNKS):
            arriving = turn(g + 1, [own])
            after += arriving[1:early]
        if waiting is not None:
            after.append(finish(g - 1, waiting, [own]))
        low, high = halves(from_prev, from_next, after)
        waiting = (
            own,
            from_prev,
            from_next,
            along(low, "col", 1, cols),
            along(high, "col", cols - 1, cols),
        )
        if g + 1 < len(CHUNKS):
            own = packed(place, arriving, [low])
    finish(len(CHUNKS) - 1, waiting, [])
    return (jnp.concatenate(vis, axis=1), jnp.concatenate(power, axis=0))


def solution(mesh):
    placed = (P(None, "chan", ("row", "col")), P("chan"), P(), P(None, "chan", "col", None))
    return jax.shard_map(
        on_device,
        mesh=mesh,
        in_specs=placed,
        out_specs=(P(None, "chan", "row", "col"), P("chan", "col", "row")),
        check_vma=False,
    )
```

```python
import functools
import math

import jax
import jax.numpy as jnp
import numpy as np
from jax import lax
from jax.experimental import pallas as pl
from jax.experimental.pallas import tpu as pltpu
from jax.sharding import PartitionSpec as P

NCH = 128
TAPS = 4
INTEG = 8
CHUNKS = (4, 4)

F32 = jnp.float32
BF16 = jnp.bfloat16
VMEM = pl.BlockSpec(memory_space=pltpu.VMEM)
SMEM = pl.BlockSpec(memory_space=pltpu.SMEM)
ANY = pl.BlockSpec(memory_space=pl.ANY)


def cost(micros):
    return pl.CostEstimate(flops=int(micros * 1.1e9), bytes_accessed=1, transcendentals=0)


def limit(mebibytes):
    return pltpu.CompilerParams(vmem_limit_bytes=mebibytes * 2**20)


def prototype(taps, length):
    position = np.arange(taps * length, dtype=np.float32) + np.float32(0.5)
    offset = position / np.float32(length) - np.float32(taps / 2.0)
    window = 0.5 - 0.5 * np.cos(2.0 * math.pi * position.astype(np.float64) / (taps * length))
    sinc = np.sin(math.pi * offset.astype(np.float64)) / (math.pi * offset.astype(np.float64))
    return (sinc * window).astype(np.float32).reshape(taps, length)


def dft_table(length):
    index = np.arange(length)
    angle = 2.0 * math.pi / length * (index[:, None] * index[None, :] % length)
    factor = 1.0 / math.sqrt(length)
    table = np.concatenate([np.cos(angle) * factor, np.sin(angle) * factor], axis=1)
    return table.astype(np.float32).astype(jnp.bfloat16)


def passed_along(value, axis, steps):
    count = lax.axis_size(axis)
    initial, last = (max(0, -steps), min(count, count - steps))
    return lax.ppermute(value, axis, [(source, source + steps) for source in range(initial, last)])


def flag_column(flags, inputs):
    eye = lax.broadcasted_iota(jnp.int32, (inputs, inputs), 0) == lax.broadcasted_iota(
        jnp.int32, (inputs, inputs), 1
    )
    held = jnp.where(eye, flags.astype(F32), 0.0)
    return jnp.broadcast_to(jnp.sum(held, axis=1, keepdims=True), (inputs, NCH))


def filter_kernel(v_hbm, flags_hbm, coeff_hbm, filt_ref, v_ref, flags_ref, coeff_ref, sems):
    copies = [
        pltpu.make_async_copy(src, dst, sems.at[n])
        for n, (src, dst) in enumerate(
            ((v_hbm, v_ref), (flags_hbm, flags_ref), (coeff_hbm, coeff_ref))
        )
    ]
    for copy in copies:
        copy.start()
    for copy in copies:
        copy.wait()
    inputs = v_ref.shape[1]
    frames = v_ref.shape[2] // NCH
    mask = flag_column(flags_ref[...], inputs)
    taps = [jnp.broadcast_to(coeff_ref[t : t + 1, :], (inputs, NCH)) * mask for t in range(TAPS)]
    for part in range(2):

        def frame_step(f, past, part=part):
            lanes = pl.ds(pl.multiple_of(f * NCH, NCH), NCH)
            window = past + (v_ref[part, :, lanes].astype(F32),)
            total = taps[0] * window[0]
            for t in range(1, TAPS):
                total = total + taps[t] * window[t]
            filt_ref[part, pl.ds(f, inputs, stride=frames), :] = total
            return window[1:]

        zero = v_ref[part, :, :NCH].astype(F32) * 0.0
        lax.fori_loop(0, frames, frame_step, (zero,) * (TAPS - 1), unroll=4)


def spectrum_kernel(chunks, filt_ref, halo_ref, flags_hbm, order_hbm, coeff_hbm, table_hbm, *rest):
    outs = rest[: len(chunks)]
    flags_ref, order_ref, coeff_ref, table_ref, corr_ref, spec_ref, sems = rest[len(chunks) :]
    copies = [
        pltpu.make_async_copy(src, dst, sems.at[n])
        for n, (src, dst) in enumerate(
            (
                (flags_hbm, flags_ref),
                (order_hbm, order_ref),
                (coeff_hbm, coeff_ref),
                (table_hbm, table_ref),
            )
        )
    ]
    for copy in copies:
        copy.start()
    for copy in copies:
        copy.wait()
    inputs = halo_ref.shape[1]
    frames = filt_ref.shape[1] // inputs
    rows = 8
    mask = flag_column(flags_ref[...], inputs)
    taps = [jnp.broadcast_to(coeff_ref[t : t + 1, :], (inputs, NCH)) * mask for t in range(TAPS)]
    for part in range(2):
        past = [halo_ref[part, :, t * NCH : (t + 1) * NCH].astype(F32) for t in range(TAPS - 1)]
        for f in range(rows):
            total = jnp.zeros((inputs, NCH), F32)
            for t in range(TAPS - 1 - f):
                total = total + taps[t] * past[f + t]
            corr_ref[part, pl.ds(f, inputs, stride=rows), :] = total
    onehot = lax.broadcasted_iota(jnp.int32, (NCH, NCH), 0) == jnp.broadcast_to(
        order_ref[...], (NCH, NCH)
    )
    table = lax.dot_general(
        onehot.astype(BF16), table_ref[...], (((0,), (0,)), ((), ())), preferred_element_type=F32
    ).astype(BF16)

    def input_step(pair, carry):
        blocks = []
        for which in range(2):
            i = pair * 2 + which
            both = []
            for part in range(2):
                block = filt_ref[part, pl.ds(pl.multiple_of(i * frames, frames), frames), :]
                extra = corr_ref[part, pl.ds(pl.multiple_of(i * rows, rows), rows), :]
                both.append(jnp.concatenate([block[:rows] + extra, block[rows:]], axis=0).astype(BF16))
            re, im = both
            blocks.append(jnp.concatenate([re, im], axis=1))
            blocks.append(jnp.concatenate([im, -re], axis=1))
        right = jnp.concatenate(blocks, axis=0)
        result = lax.dot_general(
            table, right, (((1,), (1,)), ((), ())), preferred_element_type=F32
        )
        for which in range(2):
            spec_ref[pl.ds(pair * 2 + which, NCH, stride=inputs), :] = result[
                :, which * NCH : (which + 1) * NCH
            ]
        return carry

    lax.fori_loop(0, inputs // 2, input_step, 0, unroll=2)
    per_block = sum(chunks)

    def copy_step(block, carry):
        first = 0
        for out, size in zip(outs, chunks):
            for k in range(size):
                at = pl.multiple_of((block * per_block + first + k) * inputs, inputs)
                out[block, k] = spec_ref[pl.ds(at, inputs), :].astype(BF16)
            first += size
        return carry

    lax.fori_loop(0, NCH // per_block, copy_step, 0)


def spectra(voltages, history, flags, order, chunks):
    inputs = voltages.shape[1]
    frames = voltages.shape[2] // NCH
    flags = flags.reshape(1, inputs)
    coeff = jnp.asarray(prototype(TAPS, NCH))
    filtered = pl.pallas_call(
        filter_kernel,
        out_shape=jax.ShapeDtypeStruct((2, inputs * frames, NCH), F32),
        in_specs=[ANY] * 3,
        out_specs=VMEM,
        scratch_shapes=[
            pltpu.VMEM(voltages.shape, BF16),
            pltpu.VMEM((1, inputs), jnp.int32),
            pltpu.VMEM((TAPS, NCH), F32),
            pltpu.SemaphoreType.DMA((3,)),
        ],
        compiler_params=limit(16),
        cost_estimate=cost(5),
    )(voltages, flags, coeff)
    blocks = NCH // sum(chunks)
    return pl.pallas_call(
        functools.partial(spectrum_kernel, chunks),
        out_shape=[jax.ShapeDtypeStruct((blocks, size, inputs, 2 * frames), BF16) for size in chunks],
        in_specs=[VMEM, VMEM] + [ANY] * 4,
        out_specs=[VMEM] * len(chunks),
        scratch_shapes=[
            pltpu.VMEM((1, inputs), jnp.int32),
            pltpu.VMEM((1, NCH), jnp.int32),
            pltpu.VMEM((TAPS, NCH), F32),
            pltpu.VMEM((NCH, 2 * NCH), BF16),
            pltpu.VMEM((2, inputs * 8, NCH), F32),
            pltpu.VMEM((NCH * inputs, 2 * frames), F32),
            pltpu.SemaphoreType.DMA((4,)),
        ],
        compiler_params=limit(16),
        cost_estimate=cost(6),
    )(filtered, history, flags, order.reshape(1, NCH), coeff, jnp.asarray(dft_table(NCH)))


def halves_kernel(count, low_ref, high_ref, *refs):
    outs = refs[-2 - count :]
    half = outs[0].shape[0]
    outs[0][...] = low_ref[:half]
    outs[1][...] = high_ref[half:]
    for n in range(count):
        outs[2 + n][...] = refs[n][...]


def halves(low, high, through=()):
    shape = jax.ShapeDtypeStruct((low.shape[0] // 2,) + low.shape[1:], BF16)
    shapes = [shape, shape] + [jax.ShapeDtypeStruct(x.shape, x.dtype) for x in through]
    return pl.pallas_call(
        functools.partial(halves_kernel, len(through)),
        out_shape=shapes,
        in_specs=[VMEM] * (2 + len(through)),
        out_specs=[VMEM] * len(shapes),
        cost_estimate=cost(1),
    )(low, high, *through)


def panel_of(x_ref, index, panel):
    return x_ref[0, pl.ds(pl.multiple_of(index * panel, panel), panel), :]


def turned_panel(panel, lanes, low_sign):
    first = lax.broadcasted_iota(jnp.int32, (panel.shape[0], lanes), 1) < lanes // 2
    parts = []
    for s in range(panel.shape[1] // lanes):
        part = pltpu.roll(panel[:, s * lanes : (s + 1) * lanes].astype(F32), lanes // 2, axis=1)
        parts.append(jnp.where(first, low_sign * part, -low_sign * part).astype(BF16))
    return jnp.concatenate(parts, axis=1)


def correlated(left, right):
    return lax.dot_general(
        left, right, (((1,), (1,)), ((), ())), preferred_element_type=F32
    ) * (1.0 / (NCH * 8))


def far_kernel(place_ref, own_ref, prev_ref, next_ref, lo_ref, hi_ref, re_ref, im_ref, x_ref, r_ref):
    fixed, ring = place_ref[0], place_ref[1]
    blocks, _, inputs, lanes = own_ref.shape
    half = blocks // 2 * inputs
    total = blocks * inputs
    for s, ref in enumerate((own_ref, prev_ref, next_ref)):
        x_ref[0, :, s * lanes : (s + 1) * lanes] = ref[:, 0].reshape(total, lanes)
    x_ref[0, :half, 3 * lanes :] = lo_ref[:, 0].reshape(half, lanes)
    x_ref[0, half:, 3 * lanes :] = hi_ref[:, 0].reshape(half, lanes)
    panel = re_ref.shape[1]
    mine = panel_of(x_ref, fixed, panel)
    r_ref[0, :panel] = mine
    r_ref[0, panel:] = turned_panel(mine, lanes, -1.0)
    result = correlated(panel_of(x_ref, lax.rem(ring + 2, 4), panel), r_ref[0])
    re_ref[0] = result[:, :panel].astype(BF16)
    im_ref[0] = result[:, panel:].astype(BF16)


def far_products(place, slots):
    own = slots[0]
    blocks, size, inputs, lanes = own.shape
    total = blocks * inputs
    panel = total // 4

    def data(count):
        return pl.BlockSpec((count, 1, inputs, lanes), lambda k, c: (0, k, 0, 0))

    def whole(rows, width):
        return pl.BlockSpec((1, rows, width), lambda k, c: (k, 0, 0))

    def shape(rows, width):
        return jax.ShapeDtypeStruct((size, rows, width), BF16)

    return pl.pallas_call(
        far_kernel,
        out_shape=[
            shape(panel, panel),
            shape(panel, panel),
            shape(total, 4 * lanes),
            shape(2 * panel, 4 * lanes),
        ],
        grid_spec=pltpu.PrefetchScalarGridSpec(
            num_scalar_prefetch=1,
            grid=(size,),
            in_specs=[data(blocks)] * 3 + [data(blocks // 2)] * 2,
            out_specs=[
                whole(panel, panel),
                whole(panel, panel),
                whole(total, 4 * lanes),
                whole(2 * panel, 4 * lanes),
            ],
        ),
        compiler_params=limit(20),
        cost_estimate=cost(4),
    )(place, *slots)


def near_kernel(
    first, place_ref, x_ref, r_ref, w_hbm, own_ref, up_ref, down_ref, beam_ref, w_ref, sem
):
    fixed, ring = place_ref[0], place_ref[1]
    k = pl.program_id(0)
    size = w_ref.shape[1]
    copy = pltpu.make_async_copy(w_hbm.at[:, first : first + size], w_ref, sem)

    @pl.when(k == 0)
    def _():
        copy.start()

    panel = own_ref.shape[2]
    lanes = x_ref.shape[2] // 4
    for step, ref in ((1, up_ref), (3, down_ref), (0, own_ref)):
        result = correlated(panel_of(x_ref, lax.rem(ring + step, 4), panel), r_ref[0])
        ref[0, 0] = result[:, :panel].astype(ref.dtype)
        ref[1, 0] = result[:, panel:].astype(ref.dtype)

    @pl.when(k == 0)
    def _():
        copy.wait()

    beams = w_ref.shape[2]
    weights = w_ref[:, k].reshape(2 * beams, w_ref.shape[3])
    parts = lax.dot_general(
        weights, x_ref[0], (((1,), (0,)), ((), ())), preferred_element_type=F32
    )
    low = lax.broadcasted_iota(jnp.int32, (beams, lanes), 1) < lanes // 2
    bins = lanes // 2 // INTEG
    power = jnp.zeros((4 * bins, beams), F32)
    for s, shift in enumerate((0, 3, 1, 2)):
        piece = parts[:, s * lanes : (s + 1) * lanes]
        turned = pltpu.roll(piece[beams:], lanes // 2, axis=1)
        value = piece[:beams] + jnp.where(low, -turned, turned)
        lane = lax.broadcasted_iota(jnp.int32, (4 * bins, lanes), 1)
        place = lax.broadcasted_iota(jnp.int32, (4 * bins, lanes), 0)
        wanted = lax.rem(fixed + shift, 4) * bins + lax.rem(lane, lanes // 2) // INTEG
        pool = jnp.where(place == wanted, 1.0 / INTEG, 0.0).astype(F32)
        power = power + lax.dot_general(
            pool,
            value * value,
            (((1,), (1,)), ((), ())),
            precision=lax.Precision.HIGHEST,
            preferred_element_type=F32,
        )
    beam_ref[0] = power


def near_products(place, x, r, weights, first):
    size, total, width = x.shape
    panel = total // 4
    beams = weights.shape[2]
    bins = width // 2 // INTEG
    block = pl.BlockSpec((2, 1, panel, panel), lambda k, c: (0, k, 0, 0))
    return pl.pallas_call(
        functools.partial(near_kernel, first),
        out_shape=[
            jax.ShapeDtypeStruct((2, size, panel, panel), F32),
            jax.ShapeDtypeStruct((2, size, panel, panel), BF16),
            jax.ShapeDtypeStruct((2, size, panel, panel), BF16),
            jax.ShapeDtypeStruct((size, bins, beams), F32),
        ],
        grid_spec=pltpu.PrefetchScalarGridSpec(
            num_scalar_prefetch=1,
            grid=(size,),
            in_specs=[
                pl.BlockSpec((1, total, width), lambda k, c: (k, 0, 0)),
                pl.BlockSpec((1, 2 * panel, width), lambda k, c: (k, 0, 0)),
                ANY,
            ],
            out_specs=[block] * 3 + [pl.BlockSpec((1, bins, beams), lambda k, c: (k, 0, 0))],
            scratch_shapes=[
                pltpu.VMEM((2, size) + weights.shape[2:], BF16),
                pltpu.SemaphoreType.DMA,
            ],
        ),
        compiler_params=limit(20),
        cost_estimate=cost(7),
    )(place, x, r, weights)


def add_kernel(up_ref, down_ref, low_ref, high_ref, *refs):
    up_out, down_out = refs[-2:]
    up_out[0, 0] = (up_ref[0, 0].astype(F32) + low_ref[0].astype(F32)).astype(BF16)
    down_out[0, 0] = (down_ref[0, 0].astype(F32) + high_ref[0].astype(F32)).astype(BF16)


def added(up, down, low, high, after=()):
    _, size, panel, _ = up.shape
    real = pl.BlockSpec((1, 1, panel, panel), lambda k: (0, k, 0, 0))
    imag = pl.BlockSpec((1, 1, panel, panel), lambda k: (1, k, 0, 0))
    one = pl.BlockSpec((1, panel, panel), lambda k: (k, 0, 0))
    shape = jax.ShapeDtypeStruct(up.shape, BF16)
    return pl.pallas_call(
        add_kernel,
        out_shape=[shape, shape],
        grid=(size,),
        in_specs=[real, imag, one, one] + [ANY] * len(after),
        out_specs=[real, imag],
        input_output_aliases={0: 0, 1: 1},
        cost_estimate=cost(1),
    )(up, down, low, high, *after)


def final_kernel(own_ref, prev_ref, next_ref, *refs):
    refs[-1][...] = own_ref[...] + prev_ref[...].astype(F32) + next_ref[...].astype(F32)


def finished(own, from_prev, from_next, first, channels, out):
    _, size, panel, _ = own.shape
    block = pl.BlockSpec((1, 1, panel, panel), lambda p, k: (p, k, 0, 0))
    extra = [] if out is None else [out]
    return pl.pallas_call(
        final_kernel,
        out_shape=jax.ShapeDtypeStruct((2, channels, panel, panel), F32),
        grid=(2, size),
        in_specs=[block] * 3 + [ANY] * len(extra),
        out_specs=pl.BlockSpec((1, 1, panel, panel), lambda p, k: (p, first + k, 0, 0)),
        input_output_aliases={3: 0} if extra else {},
        cost_estimate=cost(2),
    )(own, from_prev, from_next, *extra)


def along(value, axis, step):
    count = lax.axis_size(axis)
    return lax.ppermute(value, axis, [(i, (i + step) % count) for i in range(count)])


def both_ways(up, down, axis):
    return along(up, axis, 1), along(down, axis, -1)


def on_device(voltages, input_flags, channel_order, beam_weights):
    history = passed_along(voltages[:, :, voltages.shape[2] - (TAPS - 1) * NCH :], ("row", "col"), 1)
    place = jnp.stack([lax.axis_index("col"), lax.axis_index("row")]).astype(jnp.int32)
    pieces = spectra(voltages, history, input_flags, channel_order, CHUNKS)
    channels = sum(CHUNKS)

    def turn(piece):
        return lax.all_to_all(piece, "chan", split_axis=0, concat_axis=0, tiled=True)

    own0 = turn(pieces[0])
    near0 = both_ways(own0, own0, "col")
    own1 = turn(pieces[1])
    low0, high0, own1 = halves(*near0, [own1])
    far0 = both_ways(low0, high0, "col")
    near1 = both_ways(own1, own1, "col")

    re0, im0, x0, r0 = far_products(place, (own0, *near0, *far0))
    got0 = both_ways(re0, im0, "row")
    mine0, up0, down0, beam0 = near_products(place, x0, r0, beam_weights, 0)
    low1, high1 = halves(*near1)
    far1 = both_ways(low1, high1, "col")
    sent0 = both_ways(*added(up0, down0, *got0), "row")

    re1, im1, x1, r1 = far_products(place, (own1, *near1, *far1))
    got1 = both_ways(re1, im1, "row")
    mine1, up1, down1, beam1 = near_products(place, x1, r1, beam_weights, CHUNKS[0])
    sent1 = both_ways(*added(up1, down1, *got1), "row")

    out = finished(mine0, *sent0, 0, channels, None)
    visibility = finished(mine1, *sent1, CHUNKS[0], channels, out)
    power = jnp.concatenate([beam0, beam1], axis=0)
    return (visibility, jnp.transpose(power, (0, 2, 1)))


def solution(mesh):
    placed = (P(None, "chan", ("row", "col")), P("chan"), P(), P(None, "chan", "col", None))
    return jax.shard_map(
        on_device,
        mesh=mesh,
        in_specs=placed,
        out_specs=(P(None, "chan", "row", "col"), P("chan", "col", "row")),
        check_vma=False,
    )
```

```python
import functools
import math

import jax
import jax.numpy as jnp
import numpy as np
from jax import lax
from jax.experimental import pallas as pl
from jax.experimental.pallas import tpu as pltpu
from jax.sharding import PartitionSpec as P

NCH = 128
TAPS = 4
INTEG = 8
CHUNKS = (4, 4)

F32 = jnp.float32
BF16 = jnp.bfloat16
VMEM = pl.BlockSpec(memory_space=pltpu.VMEM)
SMEM = pl.BlockSpec(memory_space=pltpu.SMEM)
ANY = pl.BlockSpec(memory_space=pl.ANY)
HBM = pl.BlockSpec(memory_space=pltpu.HBM)


def cost(micros):
    return pl.CostEstimate(flops=int(micros * 1.1e9), bytes_accessed=1, transcendentals=0)


def in_hbm(value):
    return pltpu.with_memory_space_constraint(value, pltpu.HBM)


def limit(mebibytes):
    return pltpu.CompilerParams(vmem_limit_bytes=mebibytes * 2**20)


def prototype(taps, length):
    position = np.arange(taps * length, dtype=np.float32) + np.float32(0.5)
    offset = position / np.float32(length) - np.float32(taps / 2.0)
    window = 0.5 - 0.5 * np.cos(2.0 * math.pi * position.astype(np.float64) / (taps * length))
    sinc = np.sin(math.pi * offset.astype(np.float64)) / (math.pi * offset.astype(np.float64))
    return (sinc * window).astype(np.float32).reshape(taps, length)


def dft_table(length):
    index = np.arange(length)
    angle = 2.0 * math.pi / length * (index[:, None] * index[None, :] % length)
    factor = 1.0 / math.sqrt(length)
    table = np.concatenate([np.cos(angle) * factor, np.sin(angle) * factor], axis=1)
    return table.astype(np.float32).astype(jnp.bfloat16)


def passed_along(value, axis, steps):
    count = lax.axis_size(axis)
    initial, last = (max(0, -steps), min(count, count - steps))
    return lax.ppermute(value, axis, [(source, source + steps) for source in range(initial, last)])


def flag_column(flags, inputs):
    eye = lax.broadcasted_iota(jnp.int32, (inputs, inputs), 0) == lax.broadcasted_iota(
        jnp.int32, (inputs, inputs), 1
    )
    held = jnp.where(eye, flags.astype(F32), 0.0)
    return jnp.broadcast_to(jnp.sum(held, axis=1, keepdims=True), (inputs, NCH))


def filter_kernel(v_hbm, flags_hbm, coeff_hbm, filt_ref, v_ref, flags_ref, coeff_ref, sems):
    copies = [
        pltpu.make_async_copy(src, dst, sems.at[n])
        for n, (src, dst) in enumerate(
            ((v_hbm, v_ref), (flags_hbm, flags_ref), (coeff_hbm, coeff_ref))
        )
    ]
    for copy in copies:
        copy.start()
    for copy in copies:
        copy.wait()
    inputs = v_ref.shape[1]
    frames = v_ref.shape[2] // NCH
    mask = flag_column(flags_ref[...], inputs)
    taps = [jnp.broadcast_to(coeff_ref[t : t + 1, :], (inputs, NCH)) * mask for t in range(TAPS)]
    for part in range(2):

        def frame_step(f, past, part=part):
            lanes = pl.ds(pl.multiple_of(f * NCH, NCH), NCH)
            window = past + (v_ref[part, :, lanes].astype(F32),)
            total = taps[0] * window[0]
            for t in range(1, TAPS):
                total = total + taps[t] * window[t]
            filt_ref[part, pl.ds(f, inputs, stride=frames), :] = total
            return window[1:]

        zero = v_ref[part, :, :NCH].astype(F32) * 0.0
        lax.fori_loop(0, frames, frame_step, (zero,) * (TAPS - 1), unroll=4)


def spectrum_kernel(chunks, filt_ref, halo_ref, flags_hbm, order_hbm, coeff_hbm, table_hbm, *rest):
    outs = rest[: len(chunks)]
    flags_ref, order_ref, coeff_ref, table_ref, corr_ref, spec_ref, sems = rest[len(chunks) :]
    copies = [
        pltpu.make_async_copy(src, dst, sems.at[n])
        for n, (src, dst) in enumerate(
            (
                (flags_hbm, flags_ref),
                (order_hbm, order_ref),
                (coeff_hbm, coeff_ref),
                (table_hbm, table_ref),
            )
        )
    ]
    for copy in copies:
        copy.start()
    for copy in copies:
        copy.wait()
    inputs = halo_ref.shape[1]
    frames = filt_ref.shape[1] // inputs
    rows = 8
    mask = flag_column(flags_ref[...], inputs)
    taps = [jnp.broadcast_to(coeff_ref[t : t + 1, :], (inputs, NCH)) * mask for t in range(TAPS)]
    for part in range(2):
        past = [halo_ref[part, :, t * NCH : (t + 1) * NCH].astype(F32) for t in range(TAPS - 1)]
        for f in range(rows):
            total = jnp.zeros((inputs, NCH), F32)
            for t in range(TAPS - 1 - f):
                total = total + taps[t] * past[f + t]
            corr_ref[part, pl.ds(f, inputs, stride=rows), :] = total
    onehot = lax.broadcasted_iota(jnp.int32, (NCH, NCH), 0) == jnp.broadcast_to(
        order_ref[...], (NCH, NCH)
    )
    table = lax.dot_general(
        onehot.astype(BF16), table_ref[...], (((0,), (0,)), ((), ())), preferred_element_type=F32
    ).astype(BF16)

    def input_step(pair, carry):
        blocks = []
        for which in range(2):
            i = pair * 2 + which
            both = []
            for part in range(2):
                block = filt_ref[part, pl.ds(pl.multiple_of(i * frames, frames), frames), :]
                extra = corr_ref[part, pl.ds(pl.multiple_of(i * rows, rows), rows), :]
                both.append(jnp.concatenate([block[:rows] + extra, block[rows:]], axis=0).astype(BF16))
            re, im = both
            blocks.append(jnp.concatenate([re, im], axis=1))
            blocks.append(jnp.concatenate([im, -re], axis=1))
        right = jnp.concatenate(blocks, axis=0)
        result = lax.dot_general(
            table, right, (((1,), (1,)), ((), ())), preferred_element_type=F32
        )
        for which in range(2):
            spec_ref[pl.ds(pair * 2 + which, NCH, stride=inputs), :] = result[
                :, which * NCH : (which + 1) * NCH
            ]
        return carry

    lax.fori_loop(0, inputs // 2, input_step, 0, unroll=2)
    per_block = sum(chunks)

    def copy_step(block, carry):
        first = 0
        for out, size in zip(outs, chunks):
            for k in range(size):
                at = pl.multiple_of((block * per_block + first + k) * inputs, inputs)
                out[block, k] = spec_ref[pl.ds(at, inputs), :].astype(BF16)
            first += size
        return carry

    lax.fori_loop(0, NCH // per_block, copy_step, 0)


def spectra(voltages, history, flags, order, chunks):
    inputs = voltages.shape[1]
    frames = voltages.shape[2] // NCH
    flags = flags.reshape(1, inputs)
    coeff = jnp.asarray(prototype(TAPS, NCH))
    filtered = pl.pallas_call(
        filter_kernel,
        out_shape=jax.ShapeDtypeStruct((2, inputs * frames, NCH), F32),
        in_specs=[HBM] * 3,
        out_specs=VMEM,
        scratch_shapes=[
            pltpu.VMEM(voltages.shape, BF16),
            pltpu.VMEM((1, inputs), jnp.int32),
            pltpu.VMEM((TAPS, NCH), F32),
            pltpu.SemaphoreType.DMA((3,)),
        ],
        compiler_params=limit(16),
        cost_estimate=cost(5),
    )(in_hbm(voltages), in_hbm(flags), in_hbm(coeff))
    blocks = NCH // sum(chunks)
    return pl.pallas_call(
        functools.partial(spectrum_kernel, chunks),
        out_shape=[jax.ShapeDtypeStruct((blocks, size, inputs, 2 * frames), BF16) for size in chunks],
        in_specs=[VMEM, VMEM] + [HBM] * 4,
        out_specs=[VMEM] * len(chunks),
        scratch_shapes=[
            pltpu.VMEM((1, inputs), jnp.int32),
            pltpu.VMEM((1, NCH), jnp.int32),
            pltpu.VMEM((TAPS, NCH), F32),
            pltpu.VMEM((NCH, 2 * NCH), BF16),
            pltpu.VMEM((2, inputs * 8, NCH), F32),
            pltpu.VMEM((NCH * inputs, 2 * frames), F32),
            pltpu.SemaphoreType.DMA((4,)),
        ],
        compiler_params=limit(16),
        cost_estimate=cost(6),
    )(
        filtered,
        history,
        *[in_hbm(x) for x in (flags, order.reshape(1, NCH), coeff, jnp.asarray(dft_table(NCH)))],
    )


def halves_kernel(low_ref, high_ref, *refs):
    low_out, high_out, sems = refs[-3:]
    half = low_out.shape[0]
    copies = [
        pltpu.make_async_copy(low_ref.at[:half], low_out, sems.at[0]),
        pltpu.make_async_copy(high_ref.at[half:], high_out, sems.at[1]),
    ]
    for copy in copies:
        copy.start()
    for copy in copies:
        copy.wait()


def halves(low, high, after=()):
    shape = (low.shape[0] // 2,) + low.shape[1:]
    return pl.pallas_call(
        halves_kernel,
        out_shape=[jax.ShapeDtypeStruct(shape, BF16)] * 2,
        in_specs=[ANY] * (2 + len(after)),
        out_specs=[ANY] * 2,
        scratch_shapes=[pltpu.SemaphoreType.DMA((2,))],
        compiler_params=limit(62),
        cost_estimate=cost(1),
    )(in_hbm(low), in_hbm(high), *after)


def panel_of(x_ref, index, panel):
    return x_ref[0, pl.ds(pl.multiple_of(index * panel, panel), panel), :]


def turned_panel(panel, lanes, low_sign):
    first = lax.broadcasted_iota(jnp.int32, (panel.shape[0], lanes), 1) < lanes // 2
    parts = []
    for s in range(panel.shape[1] // lanes):
        part = pltpu.roll(panel[:, s * lanes : (s + 1) * lanes].astype(F32), lanes // 2, axis=1)
        parts.append(jnp.where(first, low_sign * part, -low_sign * part).astype(BF16))
    return jnp.concatenate(parts, axis=1)


def correlated(by_row, moving, fixed):
    panel = moving.shape[0]
    left, right = (fixed, moving) if by_row else (moving, fixed)
    result = lax.dot_general(
        left, right, (((1,), (1,)), ((), ())), preferred_element_type=F32
    ) * (1.0 / (NCH * 8))
    if by_row:
        return result[:panel], result[panel:]
    return result[:, :panel], result[:, panel:]


def far_kernel(by_row, place_ref, own_ref, prev_ref, next_ref, lo_ref, hi_ref, *refs):
    re_ref, im_ref, x_ref, r_ref = refs[-4:]
    fixed, ring = place_ref[0], place_ref[1]
    blocks, _, inputs, lanes = own_ref.shape
    half = blocks // 2 * inputs
    total = blocks * inputs
    for s, ref in enumerate((own_ref, prev_ref, next_ref)):
        x_ref[0, :, s * lanes : (s + 1) * lanes] = ref[:, 0].reshape(total, lanes)
    x_ref[0, :half, 3 * lanes :] = lo_ref[:, 0].reshape(half, lanes)
    x_ref[0, half:, 3 * lanes :] = hi_ref[:, 0].reshape(half, lanes)
    panel = re_ref.shape[1]
    mine = panel_of(x_ref, fixed, panel)
    r_ref[0, :panel] = mine
    r_ref[0, panel:] = turned_panel(mine, lanes, 1.0 if by_row else -1.0)
    re, im = correlated(by_row, panel_of(x_ref, lax.rem(ring + 2, 4), panel), r_ref[0])
    re_ref[0] = re.astype(BF16)
    im_ref[0] = im.astype(BF16)


def far_products(place, slots, by_row, after=()):
    own = slots[0]
    blocks, size, inputs, lanes = own.shape
    total = blocks * inputs
    panel = total // 4

    def data(count):
        return pl.BlockSpec((count, 1, inputs, lanes), lambda k, c: (0, k, 0, 0))

    def whole(rows, width):
        return pl.BlockSpec((1, rows, width), lambda k, c: (k, 0, 0))

    def shape(rows, width):
        return pltpu.HBM((size, rows, width), BF16)

    return pl.pallas_call(
        functools.partial(far_kernel, by_row),
        out_shape=[
            shape(panel, panel),
            shape(panel, panel),
            shape(total, 4 * lanes),
            shape(2 * panel, 4 * lanes),
        ],
        grid_spec=pltpu.PrefetchScalarGridSpec(
            num_scalar_prefetch=1,
            grid=(size,),
            in_specs=[data(blocks)] * 3 + [data(blocks // 2)] * 2 + [ANY] * len(after),
            out_specs=[
                whole(panel, panel),
                whole(panel, panel),
                whole(total, 4 * lanes),
                whole(2 * panel, 4 * lanes),
            ],
        ),
        compiler_params=limit(62),
        cost_estimate=cost(4),
    )(place, *[in_hbm(slot) for slot in slots[:3]], *slots[3:], *after)


def formed(parts, lanes):
    beams = parts.shape[0] // 2
    low = lax.broadcasted_iota(jnp.int32, (beams, lanes), 1) < lanes // 2
    turned = pltpu.roll(parts[beams:], lanes // 2, axis=1)
    value = parts[:beams] + jnp.where(low, -turned, turned)
    return value * value


def pooled(power, bins, first):
    lanes = power.shape[1]
    lane = lax.broadcasted_iota(jnp.int32, (bins, lanes), 1)
    place = lax.broadcasted_iota(jnp.int32, (bins, lanes), 0)
    wanted = first + lax.rem(lane, lanes // 2) // INTEG
    pool = jnp.where(place == wanted, 1.0 / INTEG, 0.0).astype(F32)
    return lax.dot_general(
        pool,
        power,
        (((1,), (1,)), ((), ())),
        precision=lax.Precision.HIGHEST,
        preferred_element_type=F32,
    )


def near_kernel(by_row, place_ref, x_ref, r_ref, *refs):
    fixed, ring = place_ref[0], place_ref[1]
    if by_row:
        own_ref, up_ref, down_ref = refs
    else:
        w_hbm, own_ref, up_ref, down_ref, beam_ref, w_ref, sem = refs
        k = pl.program_id(0)
        copy = pltpu.make_async_copy(w_hbm.at[:, : w_ref.shape[1]], w_ref, sem)

        @pl.when(k == 0)
        def _():
            copy.start()

    panel = own_ref.shape[2]
    lanes = x_ref.shape[2] // 4
    for step, ref in ((1, up_ref), (3, down_ref), (0, own_ref)):
        target = panel_of(x_ref, lax.rem(ring + step, 4), panel)
        re, im = correlated(by_row, target, r_ref[0])
        ref[0, 0] = re.astype(ref.dtype)
        ref[1, 0] = im.astype(ref.dtype)
    if by_row:
        return

    @pl.when(k == 0)
    def _():
        copy.wait()

    beams = w_ref.shape[2]
    weights = w_ref[:, k].reshape(2 * beams, w_ref.shape[3])
    parts = lax.dot_general(
        weights, x_ref[0], (((1,), (0,)), ((), ())), preferred_element_type=F32
    )
    bins = lanes // 2 // INTEG
    power = jnp.zeros((4 * bins, beams), F32)
    for s, shift in enumerate((0, 3, 1, 2)):
        squared = formed(parts[:, s * lanes : (s + 1) * lanes], lanes)
        power = power + pooled(squared, 4 * bins, lax.rem(fixed + shift, 4) * bins)
    beam_ref[0] = power


def near_products(place, x, r, by_row, weights=None):
    size, total, width = x.shape
    panel = total // 4
    block = pl.BlockSpec((2, 1, panel, panel), lambda k, c: (0, k, 0, 0))
    shape = (2, size, panel, panel)
    shapes = [pltpu.HBM(shape, F32), pltpu.HBM(shape, BF16), pltpu.HBM(shape, BF16)]
    specs = [block] * 3
    args = [x, r]
    scratch = []
    if not by_row:
        beams = weights.shape[2]
        bins = width // 2 // INTEG
        shapes.append(jax.ShapeDtypeStruct((size, bins, beams), F32))
        specs.append(pl.BlockSpec((1, bins, beams), lambda k, c: (k, 0, 0)))
        args.append(weights)
        scratch = [pltpu.VMEM((2, size) + weights.shape[2:], BF16), pltpu.SemaphoreType.DMA]
    args = [in_hbm(arg) for arg in args]
    return pl.pallas_call(
        functools.partial(near_kernel, by_row),
        out_shape=shapes,
        grid_spec=pltpu.PrefetchScalarGridSpec(
            num_scalar_prefetch=1,
            grid=(size,),
            in_specs=[
                pl.BlockSpec((1, total, width), lambda k, c: (k, 0, 0)),
                pl.BlockSpec((1, 2 * panel, width), lambda k, c: (k, 0, 0)),
            ]
            + [HBM] * (len(args) - 2),
            out_specs=specs,
            scratch_shapes=scratch,
        ),
        compiler_params=limit(62),
        cost_estimate=cost(7),
    )(place, *args)


def beam_kernel(own_ref, w_ref, out_ref):
    blocks, _, inputs, lanes = own_ref.shape
    owners, _, _, beams, total = w_ref.shape
    x = own_ref[:, 0].reshape(blocks * inputs, lanes)
    weights = w_ref[:, :, 0].reshape(owners * 2 * beams, total)
    parts = lax.dot_general(weights, x, (((1,), (0,)), ((), ())), preferred_element_type=F32)
    for owner in range(owners):
        squared = formed(parts[owner * 2 * beams : (owner + 1) * 2 * beams], lanes)
        out_ref[owner, 0] = pooled(squared, lanes // 2 // INTEG, 0)


def own_beams(own, weights):
    blocks, size, inputs, lanes = own.shape
    owners, _, _, beams, total = weights.shape
    bins = lanes // 2 // INTEG
    return pl.pallas_call(
        beam_kernel,
        out_shape=jax.ShapeDtypeStruct((owners, size, bins, beams), F32),
        grid=(size,),
        in_specs=[
            pl.BlockSpec((blocks, 1, inputs, lanes), lambda k: (0, k, 0, 0)),
            pl.BlockSpec((owners, 2, 1, beams, total), lambda k: (0, 0, k, 0, 0)),
        ],
        out_specs=pl.BlockSpec((owners, 1, bins, beams), lambda k: (0, k, 0, 0)),
        compiler_params=limit(62),
        cost_estimate=cost(4),
    )(in_hbm(own), in_hbm(weights))


def add_kernel(up_ref, down_ref, low_ref, high_ref, *refs):
    up_out, down_out = refs[-2:]
    up_out[0] = (up_ref[0].astype(F32) + low_ref[...].astype(F32)).astype(BF16)
    down_out[0] = (down_ref[0].astype(F32) + high_ref[...].astype(F32)).astype(BF16)


def added(up, down, low, high, after=()):
    _, size, panel, _ = up.shape
    real = pl.BlockSpec((1, size, panel, panel), lambda n: (0, 0, 0, 0))
    imag = pl.BlockSpec((1, size, panel, panel), lambda n: (1, 0, 0, 0))
    one = pl.BlockSpec((size, panel, panel), lambda n: (0, 0, 0))
    shape = pltpu.HBM(up.shape, BF16)
    return pl.pallas_call(
        add_kernel,
        out_shape=[shape, shape],
        grid=(1,),
        in_specs=[real, imag, one, one] + [ANY] * len(after),
        out_specs=[real, imag],
        input_output_aliases={0: 0, 1: 1},
        compiler_params=limit(62),
        cost_estimate=cost(1),
    )(up, down, low, high, *after)


def final_kernel(own_ref, prev_ref, next_ref, *refs):
    refs[-1][...] = own_ref[...] + prev_ref[...].astype(F32) + next_ref[...].astype(F32)


def finished(own, from_prev, from_next, first, channels, out):
    _, size, panel, _ = own.shape
    step = math.gcd(first, size) if first else size
    block = pl.BlockSpec((1, step, panel, panel), lambda p, k: (p, k, 0, 0))
    extra = [] if out is None else [out]
    return pl.pallas_call(
        final_kernel,
        out_shape=jax.ShapeDtypeStruct((2, channels, panel, panel), F32),
        grid=(2, size // step),
        in_specs=[block] * 3 + [ANY] * len(extra),
        out_specs=pl.BlockSpec((1, step, panel, panel), lambda p, k: (p, first // step + k, 0, 0)),
        input_output_aliases={3: 0} if extra else {},
        compiler_params=limit(62),
        cost_estimate=cost(2),
    )(in_hbm(own), from_prev, from_next, *extra)


def along(value, axis, step):
    count = lax.axis_size(axis)
    return lax.ppermute(value, axis, [(i, (i + step) % count) for i in range(count)])


def both_ways(up, down, axis):
    return along(up, axis, 1), along(down, axis, -1)


def on_device(voltages, input_flags, channel_order, beam_weights):
    size_a, size_b = CHUNKS
    channels = size_a + size_b
    history = passed_along(voltages[:, :, voltages.shape[2] - (TAPS - 1) * NCH :], ("row", "col"), 1)
    row = lax.axis_index("row").astype(jnp.int32)
    col = lax.axis_index("col").astype(jnp.int32)
    place_a = jnp.stack([col, row])
    place_b = jnp.stack([row, col])
    weights_b = lax.all_gather(beam_weights[:, size_a:], "col", axis=0)
    piece_a, piece_b = spectra(voltages, history, input_flags, channel_order, CHUNKS)

    def turn(piece, axis):
        return lax.all_to_all(piece, axis, split_axis=0, concat_axis=0, tiled=True)

    own_a = turn(piece_a, "chan")
    near_a = both_ways(own_a, own_a, "col")
    own_b = turn(piece_b, "chan")
    near_b = both_ways(own_b, own_b, "row")
    far_b = both_ways(*halves(*near_b, [own_a]), "row")
    far_a = both_ways(*halves(*near_a), "col")
    beam_b = own_beams(own_b, weights_b)

    re_b, im_b, x_b, r_b = far_products(place_b, (own_b, *near_b, *far_b), True, [beam_b])
    got_b = both_ways(re_b, im_b, "col")
    mine_b, up_b, down_b = near_products(place_b, x_b, r_b, True)
    sent_b = both_ways(*added(up_b, down_b, *got_b), "col")

    re_a, im_a, x_a, r_a = far_products(place_a, (own_a, *near_a, *far_a), False, [mine_b])
    got_a = both_ways(re_a, im_a, "row")
    mine_a, up_a, down_a, power_a = near_products(place_a, x_a, r_a, False, beam_weights)
    sent_a = both_ways(*added(up_a, down_a, *got_a), "row")

    power_b = jnp.transpose(turn(beam_b, "col"), (1, 0, 2, 3)).reshape(size_b, -1, beam_b.shape[3])
    out = finished(mine_a, *sent_a, 0, channels, None)
    visibility = finished(mine_b, *sent_b, size_a, channels, out)
    power = jnp.concatenate([power_a, power_b], axis=0)
    return (visibility, jnp.transpose(power, (0, 2, 1)))


def solution(mesh):
    placed = (P(None, "chan", ("row", "col")), P("chan"), P(), P(None, "chan", "col", None))
    return jax.shard_map(
        on_device,
        mesh=mesh,
        in_specs=placed,
        out_specs=(P(None, "chan", "row", "col"), P("chan", "col", "row")),
        check_vma=False,
    )
```

```python
import functools
import math

import jax
import jax.numpy as jnp
import numpy as np
from jax import lax
from jax.experimental import pallas as pl
from jax.experimental.pallas import tpu as pltpu
from jax.sharding import PartitionSpec as P

NCH = 128
TAPS = 4
INTEG = 8
CHUNKS = (5, 3)

F32 = jnp.float32
BF16 = jnp.bfloat16
VMEM = pl.BlockSpec(memory_space=pltpu.VMEM)
SMEM = pl.BlockSpec(memory_space=pltpu.SMEM)
ANY = pl.BlockSpec(memory_space=pl.ANY)
HBM = pl.BlockSpec(memory_space=pltpu.HBM)


def cost(micros):
    return pl.CostEstimate(flops=int(micros * 1.1e9), bytes_accessed=1, transcendentals=0)


def in_hbm(value):
    return pltpu.with_memory_space_constraint(value, pltpu.HBM)


def limit(mebibytes):
    return pltpu.CompilerParams(vmem_limit_bytes=mebibytes * 2**20)


def prototype(taps, length):
    position = np.arange(taps * length, dtype=np.float32) + np.float32(0.5)
    offset = position / np.float32(length) - np.float32(taps / 2.0)
    window = 0.5 - 0.5 * np.cos(2.0 * math.pi * position.astype(np.float64) / (taps * length))
    sinc = np.sin(math.pi * offset.astype(np.float64)) / (math.pi * offset.astype(np.float64))
    return (sinc * window).astype(np.float32).reshape(taps, length)


def dft_table(length):
    index = np.arange(length)
    angle = 2.0 * math.pi / length * (index[:, None] * index[None, :] % length)
    factor = 1.0 / math.sqrt(length)
    table = np.concatenate([np.cos(angle) * factor, np.sin(angle) * factor], axis=1)
    return table.astype(np.float32).astype(jnp.bfloat16)


def passed_along(value, axis, steps):
    count = lax.axis_size(axis)
    initial, last = (max(0, -steps), min(count, count - steps))
    return lax.ppermute(value, axis, [(source, source + steps) for source in range(initial, last)])


def flag_column(flags, inputs):
    eye = lax.broadcasted_iota(jnp.int32, (inputs, inputs), 0) == lax.broadcasted_iota(
        jnp.int32, (inputs, inputs), 1
    )
    held = jnp.where(eye, flags.astype(F32), 0.0)
    return jnp.broadcast_to(jnp.sum(held, axis=1, keepdims=True), (inputs, NCH))


def filter_kernel(v_hbm, flags_hbm, coeff_hbm, filt_ref, v_ref, flags_ref, coeff_ref, sems):
    copies = [
        pltpu.make_async_copy(src, dst, sems.at[n])
        for n, (src, dst) in enumerate(
            ((v_hbm, v_ref), (flags_hbm, flags_ref), (coeff_hbm, coeff_ref))
        )
    ]
    for copy in copies:
        copy.start()
    for copy in copies:
        copy.wait()
    inputs = v_ref.shape[1]
    frames = v_ref.shape[2] // NCH
    mask = flag_column(flags_ref[...], inputs)
    taps = [jnp.broadcast_to(coeff_ref[t : t + 1, :], (inputs, NCH)) * mask for t in range(TAPS)]
    for part in range(2):

        def frame_step(f, past, part=part):
            lanes = pl.ds(pl.multiple_of(f * NCH, NCH), NCH)
            window = past + (v_ref[part, :, lanes].astype(F32),)
            total = taps[0] * window[0]
            for t in range(1, TAPS):
                total = total + taps[t] * window[t]
            filt_ref[part, pl.ds(f, inputs, stride=frames), :] = total
            return window[1:]

        zero = v_ref[part, :, :NCH].astype(F32) * 0.0
        lax.fori_loop(0, frames, frame_step, (zero,) * (TAPS - 1), unroll=4)


def spectrum_kernel(chunks, filt_ref, halo_ref, flags_hbm, order_hbm, coeff_hbm, table_hbm, *rest):
    outs = rest[: len(chunks)]
    flags_ref, order_ref, coeff_ref, table_ref, corr_ref, spec_ref, sems = rest[len(chunks) :]
    copies = [
        pltpu.make_async_copy(src, dst, sems.at[n])
        for n, (src, dst) in enumerate(
            (
                (flags_hbm, flags_ref),
                (order_hbm, order_ref),
                (coeff_hbm, coeff_ref),
                (table_hbm, table_ref),
            )
        )
    ]
    for copy in copies:
        copy.start()
    for copy in copies:
        copy.wait()
    inputs = halo_ref.shape[1]
    frames = filt_ref.shape[1] // inputs
    rows = 8
    mask = flag_column(flags_ref[...], inputs)
    taps = [jnp.broadcast_to(coeff_ref[t : t + 1, :], (inputs, NCH)) * mask for t in range(TAPS)]
    for part in range(2):
        past = [halo_ref[part, :, t * NCH : (t + 1) * NCH].astype(F32) for t in range(TAPS - 1)]
        for f in range(rows):
            total = jnp.zeros((inputs, NCH), F32)
            for t in range(TAPS - 1 - f):
                total = total + taps[t] * past[f + t]
            corr_ref[part, pl.ds(f, inputs, stride=rows), :] = total
    onehot = lax.broadcasted_iota(jnp.int32, (NCH, NCH), 0) == jnp.broadcast_to(
        order_ref[...], (NCH, NCH)
    )
    table = lax.dot_general(
        onehot.astype(BF16), table_ref[...], (((0,), (0,)), ((), ())), preferred_element_type=F32
    ).astype(BF16)

    def input_step(pair, carry):
        blocks = []
        for which in range(2):
            i = pair * 2 + which
            both = []
            for part in range(2):
                block = filt_ref[part, pl.ds(pl.multiple_of(i * frames, frames), frames), :]
                extra = corr_ref[part, pl.ds(pl.multiple_of(i * rows, rows), rows), :]
                both.append(jnp.concatenate([block[:rows] + extra, block[rows:]], axis=0).astype(BF16))
            re, im = both
            blocks.append(jnp.concatenate([re, im], axis=1))
            blocks.append(jnp.concatenate([im, -re], axis=1))
        right = jnp.concatenate(blocks, axis=0)
        result = lax.dot_general(
            table, right, (((1,), (1,)), ((), ())), preferred_element_type=F32
        )
        for which in range(2):
            spec_ref[pl.ds(pair * 2 + which, NCH, stride=inputs), :] = result[
                :, which * NCH : (which + 1) * NCH
            ]
        return carry

    lax.fori_loop(0, inputs // 2, input_step, 0, unroll=2)
    per_block = sum(chunks)

    def copy_step(block, carry):
        first = 0
        for out, size in zip(outs, chunks):
            for k in range(size):
                at = pl.multiple_of((block * per_block + first + k) * inputs, inputs)
                out[block, k] = spec_ref[pl.ds(at, inputs), :].astype(BF16)
            first += size
        return carry

    lax.fori_loop(0, NCH // per_block, copy_step, 0)


def spectra(voltages, history, flags, order, chunks):
    inputs = voltages.shape[1]
    frames = voltages.shape[2] // NCH
    flags = flags.reshape(1, inputs)
    coeff = jnp.asarray(prototype(TAPS, NCH))
    filtered = pl.pallas_call(
        filter_kernel,
        out_shape=jax.ShapeDtypeStruct((2, inputs * frames, NCH), F32),
        in_specs=[HBM] * 3,
        out_specs=VMEM,
        scratch_shapes=[
            pltpu.VMEM(voltages.shape, BF16),
            pltpu.VMEM((1, inputs), jnp.int32),
            pltpu.VMEM((TAPS, NCH), F32),
            pltpu.SemaphoreType.DMA((3,)),
        ],
        compiler_params=limit(16),
        cost_estimate=cost(5),
    )(in_hbm(voltages), in_hbm(flags), in_hbm(coeff))
    blocks = NCH // sum(chunks)
    return pl.pallas_call(
        functools.partial(spectrum_kernel, chunks),
        out_shape=[jax.ShapeDtypeStruct((blocks, size, inputs, 2 * frames), BF16) for size in chunks],
        in_specs=[VMEM, VMEM] + [HBM] * 4,
        out_specs=[VMEM] * len(chunks),
        scratch_shapes=[
            pltpu.VMEM((1, inputs), jnp.int32),
            pltpu.VMEM((1, NCH), jnp.int32),
            pltpu.VMEM((TAPS, NCH), F32),
            pltpu.VMEM((NCH, 2 * NCH), BF16),
            pltpu.VMEM((2, inputs * 8, NCH), F32),
            pltpu.VMEM((NCH * inputs, 2 * frames), F32),
            pltpu.SemaphoreType.DMA((4,)),
        ],
        compiler_params=limit(16),
        cost_estimate=cost(6),
    )(
        filtered,
        history,
        *[in_hbm(x) for x in (flags, order.reshape(1, NCH), coeff, jnp.asarray(dft_table(NCH)))],
    )


def halves_kernel(low_ref, high_ref, *refs):
    low_out, high_out = refs[-2:]
    low_out[...] = low_ref[...]
    high_out[...] = high_ref[...]


def halves(low, high, after=()):
    blocks = low.shape[0] // 2
    block = (blocks // 2,) + low.shape[1:]
    first = pl.BlockSpec(block, lambda n: (n, 0, 0, 0))
    second = pl.BlockSpec(block, lambda n: (2 + n, 0, 0, 0))
    return pl.pallas_call(
        halves_kernel,
        out_shape=[pltpu.HBM((blocks,) + low.shape[1:], BF16)] * 2,
        grid=(2,),
        in_specs=[first, second] + [ANY] * len(after),
        out_specs=[first, first],
        compiler_params=limit(62),
        cost_estimate=cost(1),
    )(low, high, *after)


def turned_panel(panel, lanes, low_sign):
    first = lax.broadcasted_iota(jnp.int32, (panel.shape[0], lanes), 1) < lanes // 2
    parts = []
    for s in range(panel.shape[1] // lanes):
        part = pltpu.roll(panel[:, s * lanes : (s + 1) * lanes].astype(F32), lanes // 2, axis=1)
        parts.append(jnp.where(first, low_sign * part, -low_sign * part).astype(BF16))
    return jnp.concatenate(parts, axis=1)


def correlated(by_row, moving, fixed):
    panel = moving.shape[0]
    left, right = (fixed, moving) if by_row else (moving, fixed)
    result = lax.dot_general(
        left, right, (((1,), (1,)), ((), ())), preferred_element_type=F32
    ) * (1.0 / (NCH * 8))
    if by_row:
        return result[:panel], result[panel:]
    return result[:, :panel], result[:, panel:]


def stacked(by_row, panel, lanes):
    return jnp.concatenate([panel, turned_panel(panel, lanes, 1.0 if by_row else -1.0)], axis=0)


def far_kernel(by_row, place_ref, *refs):
    re_ref, im_ref = refs[-2:]
    lanes = refs[0].shape[3]

    def panel(parts, index):
        near = [part[:, 0].reshape(-1, lanes) for part in parts[:3]]
        low, high = [part[:, 0].reshape(-1, lanes) for part in parts[3:]]
        return jnp.concatenate(near + [jnp.where(index < 2, low, high)], axis=1)

    mine = panel(refs[:5], place_ref[0])
    other = panel(refs[5:10], lax.rem(place_ref[1] + 2, 4))
    re, im = correlated(by_row, other, stacked(by_row, mine, lanes))
    re_ref[0] = re.astype(BF16)
    im_ref[0] = im.astype(BF16)


def far_products(place, slots, by_row, after=()):
    own = slots[0]
    blocks, size, inputs, lanes = own.shape
    quarter = blocks // 4
    panel = quarter * inputs

    def fixed(k, c):
        return (c[0], k, 0, 0)

    def fixed_half(k, c):
        return (lax.rem(c[0], 2), k, 0, 0)

    def other(k, c):
        return (lax.rem(c[1] + 2, 4), k, 0, 0)

    def other_half(k, c):
        return (lax.rem(c[1], 2), k, 0, 0)

    def data(index):
        return pl.BlockSpec((quarter, 1, inputs, lanes), index)

    whole = pl.BlockSpec((1, panel, panel), lambda k, c: (k, 0, 0))
    slots = [in_hbm(slot) for slot in slots[:3]] + list(slots[3:])
    return pl.pallas_call(
        functools.partial(far_kernel, by_row),
        out_shape=[pltpu.HBM((size, panel, panel), BF16)] * 2,
        grid_spec=pltpu.PrefetchScalarGridSpec(
            num_scalar_prefetch=1,
            grid=(size,),
            in_specs=[data(fixed)] * 3
            + [data(fixed_half)] * 2
            + [data(other)] * 3
            + [data(other_half)] * 2
            + [ANY] * len(after),
            out_specs=[whole, whole],
        ),
        compiler_params=limit(62),
        cost_estimate=cost(4),
    )(place, *slots, *slots, *after)


def formed(parts, lanes):
    beams = parts.shape[0] // 2
    low = lax.broadcasted_iota(jnp.int32, (beams, lanes), 1) < lanes // 2
    turned = pltpu.roll(parts[beams:], lanes // 2, axis=1)
    value = parts[:beams] + jnp.where(low, -turned, turned)
    return value * value


def pooled(power, bins, first):
    lanes = power.shape[1]
    lane = lax.broadcasted_iota(jnp.int32, (bins, lanes), 1)
    place = lax.broadcasted_iota(jnp.int32, (bins, lanes), 0)
    wanted = first + lax.rem(lane, lanes // 2) // INTEG
    pool = jnp.where(place == wanted, 1.0 / INTEG, 0.0).astype(F32)
    return lax.dot_general(
        pool,
        power,
        (((1,), (1,)), ((), ())),
        precision=lax.Precision.HIGHEST,
        preferred_element_type=F32,
    )


def near_kernel(by_row, first, place_ref, own_ref, prev_ref, next_ref, low_ref, high_ref, *refs):
    fixed, ring = place_ref[0], place_ref[1]
    if by_row:
        out_ref, up_ref, down_ref, x_ref = refs[-4:]
    else:
        w_hbm = refs[0]
        out_ref, up_ref, down_ref, beam_ref, x_ref, w_ref, sem = refs[-7:]
        k = pl.program_id(0)
        copy = pltpu.make_async_copy(w_hbm.at[:, first : first + w_ref.shape[1]], w_ref, sem)

        @pl.when(k == 0)
        def _():
            copy.start()

    blocks, _, inputs, lanes = own_ref.shape
    half = blocks // 2 * inputs
    total = blocks * inputs
    panel = total // 4
    for s, ref in enumerate((own_ref, prev_ref, next_ref)):
        x_ref[:, s * lanes : (s + 1) * lanes] = ref[:, 0].reshape(total, lanes)
    x_ref[:half, 3 * lanes :] = low_ref[:, 0].reshape(half, lanes)
    x_ref[half:, 3 * lanes :] = high_ref[:, 0].reshape(half, lanes)

    def panel_of(index):
        return x_ref[pl.ds(pl.multiple_of(index * panel, panel), panel), :]

    stack = stacked(by_row, panel_of(fixed), lanes)
    for step, ref in ((1, up_ref), (3, down_ref), (0, out_ref)):
        re, im = correlated(by_row, panel_of(lax.rem(ring + step, 4)), stack)
        ref[0, 0] = re.astype(ref.dtype)
        ref[1, 0] = im.astype(ref.dtype)
    if by_row:
        return

    @pl.when(k == 0)
    def _():
        copy.wait()

    beams = w_ref.shape[2]
    weights = w_ref[:, k].reshape(2 * beams, total)
    parts = lax.dot_general(
        weights, x_ref[...], (((1,), (0,)), ((), ())), preferred_element_type=F32
    )
    bins = lanes // 2 // INTEG
    power = jnp.zeros((4 * bins, beams), F32)
    for s, shift in enumerate((0, 3, 1, 2)):
        squared = formed(parts[:, s * lanes : (s + 1) * lanes], lanes)
        power = power + pooled(squared, 4 * bins, lax.rem(fixed + shift, 4) * bins)
    beam_ref[0] = power


def near_products(place, slots, by_row, first=0, weights=None, after=()):
    blocks, size, inputs, lanes = slots[0].shape
    total = blocks * inputs
    panel = total // 4

    def data(count):
        return pl.BlockSpec((count, 1, inputs, lanes), lambda k, c: (0, k, 0, 0))

    block = pl.BlockSpec((2, 1, panel, panel), lambda k, c: (0, k, 0, 0))
    shape = (2, size, panel, panel)
    shapes = [pltpu.HBM(shape, F32), pltpu.HBM(shape, BF16), pltpu.HBM(shape, BF16)]
    specs = [block] * 3
    args = [in_hbm(slot) for slot in slots[:3]] + list(slots[3:])
    scratch = [pltpu.VMEM((total, 4 * lanes), BF16)]
    if not by_row:
        beams = weights.shape[2]
        bins = 4 * (lanes // 2 // INTEG)
        shapes.append(jax.ShapeDtypeStruct((size, bins, beams), F32))
        specs.append(pl.BlockSpec((1, bins, beams), lambda k, c: (k, 0, 0)))
        args.append(in_hbm(weights))
        scratch += [pltpu.VMEM((2, size) + weights.shape[2:], BF16), pltpu.SemaphoreType.DMA]
    args += after
    return pl.pallas_call(
        functools.partial(near_kernel, by_row, first),
        out_shape=shapes,
        grid_spec=pltpu.PrefetchScalarGridSpec(
            num_scalar_prefetch=1,
            grid=(size,),
            in_specs=[data(blocks)] * 3 + [data(blocks // 2)] * 2 + [ANY] * (len(args) - 5),
            out_specs=specs,
            scratch_shapes=scratch,
        ),
        compiler_params=limit(62),
        cost_estimate=cost(7),
    )(place, *args)


def beam_kernel(own_ref, w_ref, out_ref):
    blocks, _, inputs, lanes = own_ref.shape
    owners, _, _, beams, total = w_ref.shape
    x = own_ref[:, 0].reshape(blocks * inputs, lanes)
    weights = w_ref[:, :, 0].reshape(owners * 2 * beams, total)
    parts = lax.dot_general(weights, x, (((1,), (0,)), ((), ())), preferred_element_type=F32)
    for owner in range(owners):
        squared = formed(parts[owner * 2 * beams : (owner + 1) * 2 * beams], lanes)
        out_ref[owner, 0] = pooled(squared, lanes // 2 // INTEG, 0)


def own_beams(own, weights):
    blocks, size, inputs, lanes = own.shape
    owners, _, _, beams, total = weights.shape
    bins = lanes // 2 // INTEG
    return pl.pallas_call(
        beam_kernel,
        out_shape=jax.ShapeDtypeStruct((owners, size, bins, beams), F32),
        grid=(size,),
        in_specs=[
            pl.BlockSpec((blocks, 1, inputs, lanes), lambda k: (0, k, 0, 0)),
            pl.BlockSpec((owners, 2, 1, beams, total), lambda k: (0, 0, k, 0, 0)),
        ],
        out_specs=pl.BlockSpec((owners, 1, bins, beams), lambda k: (0, k, 0, 0)),
        compiler_params=limit(62),
        cost_estimate=cost(4),
    )(in_hbm(own), in_hbm(weights))


def add_kernel(up_ref, down_ref, low_ref, high_ref, *refs):
    up_out, down_out = refs[-2:]
    up_out[0] = (up_ref[0].astype(F32) + low_ref[...].astype(F32)).astype(BF16)
    down_out[0] = (down_ref[0].astype(F32) + high_ref[...].astype(F32)).astype(BF16)


def added(up, down, low, high, after=()):
    _, size, panel, _ = up.shape
    real = pl.BlockSpec((1, size, panel, panel), lambda n: (0, 0, 0, 0))
    imag = pl.BlockSpec((1, size, panel, panel), lambda n: (1, 0, 0, 0))
    one = pl.BlockSpec((size, panel, panel), lambda n: (0, 0, 0))
    shape = pltpu.HBM(up.shape, BF16)
    return pl.pallas_call(
        add_kernel,
        out_shape=[shape, shape],
        grid=(1,),
        in_specs=[real, imag, one, one] + [ANY] * len(after),
        out_specs=[real, imag],
        input_output_aliases={0: 0, 1: 1},
        compiler_params=limit(62),
        cost_estimate=cost(1),
    )(up, down, low, high, *after)


def final_kernel(own_ref, prev_ref, next_ref, *refs):
    refs[-1][...] = own_ref[...] + prev_ref[...].astype(F32) + next_ref[...].astype(F32)


def finished(own, from_prev, from_next, first, channels, out):
    _, size, panel, _ = own.shape
    step = math.gcd(first, size) if first else size
    block = pl.BlockSpec((1, step, panel, panel), lambda p, k: (p, k, 0, 0))
    extra = [] if out is None else [out]
    return pl.pallas_call(
        final_kernel,
        out_shape=jax.ShapeDtypeStruct((2, channels, panel, panel), F32),
        grid=(2, size // step),
        in_specs=[block] * 3 + [ANY] * len(extra),
        out_specs=pl.BlockSpec((1, step, panel, panel), lambda p, k: (p, first // step + k, 0, 0)),
        input_output_aliases={3: 0} if extra else {},
        compiler_params=limit(62),
        cost_estimate=cost(2),
    )(in_hbm(own), from_prev, from_next, *extra)


def along(value, axis, step):
    count = lax.axis_size(axis)
    return lax.ppermute(value, axis, [(i, (i + step) % count) for i in range(count)])


def both_ways(up, down, axis):
    return along(up, axis, 1), along(down, axis, -1)


def on_device(voltages, input_flags, channel_order, beam_weights):
    size_b, size_a = CHUNKS
    channels = size_a + size_b
    history = passed_along(voltages[:, :, voltages.shape[2] - (TAPS - 1) * NCH :], ("row", "col"), 1)
    row = lax.axis_index("row").astype(jnp.int32)
    col = lax.axis_index("col").astype(jnp.int32)
    place_a = jnp.stack([col, row])
    place_b = jnp.stack([row, col])
    weights = lax.all_gather(beam_weights, "col", axis=0)
    piece_b, piece_a = spectra(voltages, history, input_flags, channel_order, CHUNKS)

    def turn(piece, axis):
        return lax.all_to_all(piece, axis, split_axis=0, concat_axis=0, tiled=True)

    own_b = turn(piece_b, "chan")
    near_b = both_ways(own_b, own_b, "row")
    own_a = turn(piece_a, "chan")
    near_a = both_ways(own_a, own_a, "col")
    far_b = both_ways(*halves(*near_b, [own_a]), "row")
    beam_b = own_beams(own_b, weights)
    slots_b = (own_b, *near_b, *far_b)
    re_b, im_b = far_products(place_b, slots_b, True, [beam_b])
    got_b = both_ways(re_b, im_b, "col")
    half_a = halves(*near_a, [re_b])
    far_a = both_ways(*half_a, "col")
    slots_a = (own_a, *near_a, *far_a)
    mine_b, up_b, down_b = near_products(place_b, slots_b, True, after=[half_a[0]])
    sum_b = added(up_b, down_b, *got_b)
    sent_b = both_ways(*sum_b, "col")
    re_a, im_a = far_products(place_a, slots_a, False, [sum_b[0]])
    got_a = both_ways(re_a, im_a, "row")
    mine_a, up_a, down_a, power_a = near_products(place_a, slots_a, False, size_b, beam_weights)
    sum_a = added(up_a, down_a, *got_a)
    sent_a = both_ways(*sum_a, "row")

    power_b = jnp.transpose(turn(beam_b, "col"), (1, 0, 2, 3)).reshape(size_b, -1, beam_b.shape[3])
    out = finished(mine_b, *sent_b, 0, channels, None)
    visibility = finished(mine_a, *sent_a, size_b, channels, out)
    power = jnp.concatenate([power_b, power_a], axis=0)
    return (visibility, jnp.transpose(power, (0, 2, 1)))


def solution(mesh):
    placed = (P(None, "chan", ("row", "col")), P("chan"), P(), P(None, "chan", "col", None))
    return jax.shard_map(
        on_device,
        mesh=mesh,
        in_specs=placed,
        out_specs=(P(None, "chan", "row", "col"), P("chan", "col", "row")),
        check_vma=False,
    )
```

```python
import functools
import math

import jax
import jax.numpy as jnp
import numpy as np
from jax import lax
from jax.experimental import pallas as pl
from jax.experimental.pallas import tpu as pltpu
from jax.sharding import PartitionSpec as P

NCH = 128
TAPS = 4
INTEG = 8
CHUNKS = (5, 3)

F32 = jnp.float32
BF16 = jnp.bfloat16
VMEM = pl.BlockSpec(memory_space=pltpu.VMEM)
SMEM = pl.BlockSpec(memory_space=pltpu.SMEM)
ANY = pl.BlockSpec(memory_space=pl.ANY)
HBM = pl.BlockSpec(memory_space=pltpu.HBM)


def cost(micros):
    return pl.CostEstimate(flops=int(micros * 1.1e9), bytes_accessed=1, transcendentals=0)


def in_hbm(value):
    return pltpu.with_memory_space_constraint(value, pltpu.HBM)


def limit(mebibytes):
    return pltpu.CompilerParams(vmem_limit_bytes=mebibytes * 2**20)


def prototype(taps, length):
    position = np.arange(taps * length, dtype=np.float32) + np.float32(0.5)
    offset = position / np.float32(length) - np.float32(taps / 2.0)
    window = 0.5 - 0.5 * np.cos(2.0 * math.pi * position.astype(np.float64) / (taps * length))
    sinc = np.sin(math.pi * offset.astype(np.float64)) / (math.pi * offset.astype(np.float64))
    return (sinc * window).astype(np.float32).reshape(taps, length)


def dft_table(length):
    index = np.arange(length)
    angle = 2.0 * math.pi / length * (index[:, None] * index[None, :] % length)
    factor = 1.0 / math.sqrt(length)
    table = np.concatenate([np.cos(angle) * factor, np.sin(angle) * factor], axis=1)
    return table.astype(np.float32).astype(jnp.bfloat16)


def passed_along(value, axis, steps):
    count = lax.axis_size(axis)
    initial, last = (max(0, -steps), min(count, count - steps))
    return lax.ppermute(value, axis, [(source, source + steps) for source in range(initial, last)])


def flag_column(flags, inputs):
    eye = lax.broadcasted_iota(jnp.int32, (inputs, inputs), 0) == lax.broadcasted_iota(
        jnp.int32, (inputs, inputs), 1
    )
    held = jnp.where(eye, flags.astype(F32), 0.0)
    return jnp.broadcast_to(jnp.sum(held, axis=1, keepdims=True), (inputs, NCH))


def filter_kernel(v_hbm, flags_hbm, coeff_hbm, filt_ref, v_ref, flags_ref, coeff_ref, sems):
    copies = [
        pltpu.make_async_copy(src, dst, sems.at[n])
        for n, (src, dst) in enumerate(
            ((v_hbm, v_ref), (flags_hbm, flags_ref), (coeff_hbm, coeff_ref))
        )
    ]
    for copy in copies:
        copy.start()
    for copy in copies:
        copy.wait()
    inputs = v_ref.shape[1]
    frames = v_ref.shape[2] // NCH
    mask = flag_column(flags_ref[...], inputs)
    taps = [jnp.broadcast_to(coeff_ref[t : t + 1, :], (inputs, NCH)) * mask for t in range(TAPS)]
    for part in range(2):

        def frame_step(f, past, part=part):
            lanes = pl.ds(pl.multiple_of(f * NCH, NCH), NCH)
            window = past + (v_ref[part, :, lanes].astype(F32),)
            total = taps[0] * window[0]
            for t in range(1, TAPS):
                total = total + taps[t] * window[t]
            filt_ref[part, pl.ds(f, inputs, stride=frames), :] = total
            return window[1:]

        zero = v_ref[part, :, :NCH].astype(F32) * 0.0
        lax.fori_loop(0, frames, frame_step, (zero,) * (TAPS - 1), unroll=8)


def spectrum_kernel(chunks, filt_ref, halo_ref, flags_hbm, order_hbm, coeff_hbm, table_hbm, *rest):
    outs = rest[: len(chunks)]
    flags_ref, order_ref, coeff_ref, table_ref, corr_ref, spec_ref, sems = rest[len(chunks) :]
    copies = [
        pltpu.make_async_copy(src, dst, sems.at[n])
        for n, (src, dst) in enumerate(
            (
                (flags_hbm, flags_ref),
                (order_hbm, order_ref),
                (coeff_hbm, coeff_ref),
                (table_hbm, table_ref),
            )
        )
    ]
    for copy in copies:
        copy.start()
    for copy in copies:
        copy.wait()
    inputs = halo_ref.shape[1]
    frames = filt_ref.shape[1] // inputs
    rows = 8
    mask = flag_column(flags_ref[...], inputs)
    taps = [jnp.broadcast_to(coeff_ref[t : t + 1, :], (inputs, NCH)) * mask for t in range(TAPS)]
    for part in range(2):
        past = [halo_ref[part, :, t * NCH : (t + 1) * NCH].astype(F32) for t in range(TAPS - 1)]
        for f in range(rows):
            total = jnp.zeros((inputs, NCH), F32)
            for t in range(TAPS - 1 - f):
                total = total + taps[t] * past[f + t]
            corr_ref[part, pl.ds(f, inputs, stride=rows), :] = total
    onehot = lax.broadcasted_iota(jnp.int32, (NCH, NCH), 0) == jnp.broadcast_to(
        order_ref[...], (NCH, NCH)
    )
    table = lax.dot_general(
        onehot.astype(BF16), table_ref[...], (((0,), (0,)), ((), ())), preferred_element_type=F32
    ).astype(BF16)

    def input_step(pair, carry):
        blocks = []
        for which in range(2):
            i = pair * 2 + which
            both = []
            for part in range(2):
                block = filt_ref[part, pl.ds(pl.multiple_of(i * frames, frames), frames), :]
                extra = corr_ref[part, pl.ds(pl.multiple_of(i * rows, rows), rows), :]
                both.append(jnp.concatenate([block[:rows] + extra, block[rows:]], axis=0).astype(BF16))
            re, im = both
            blocks.append(jnp.concatenate([re, im], axis=1))
            blocks.append(jnp.concatenate([im, -re], axis=1))
        right = jnp.concatenate(blocks, axis=0)
        result = lax.dot_general(
            table, right, (((1,), (1,)), ((), ())), preferred_element_type=F32
        )
        for which in range(2):
            spec_ref[pl.ds(pair * 2 + which, NCH, stride=inputs), :] = result[
                :, which * NCH : (which + 1) * NCH
            ]
        return carry

    lax.fori_loop(0, inputs // 2, input_step, 0, unroll=4)
    per_block = sum(chunks)

    def copy_step(block, carry):
        first = 0
        for out, size in zip(outs, chunks):
            for k in range(size):
                at = pl.multiple_of((block * per_block + first + k) * inputs, inputs)
                out[block, k] = spec_ref[pl.ds(at, inputs), :].astype(BF16)
            first += size
        return carry

    lax.fori_loop(0, NCH // per_block, copy_step, 0)


def spectra(voltages, history, flags, order, chunks):
    inputs = voltages.shape[1]
    frames = voltages.shape[2] // NCH
    flags = flags.reshape(1, inputs)
    coeff = jnp.asarray(prototype(TAPS, NCH))
    filtered = pl.pallas_call(
        filter_kernel,
        out_shape=jax.ShapeDtypeStruct((2, inputs * frames, NCH), F32),
        in_specs=[HBM] * 3,
        out_specs=VMEM,
        scratch_shapes=[
            pltpu.VMEM(voltages.shape, BF16),
            pltpu.VMEM((1, inputs), jnp.int32),
            pltpu.VMEM((TAPS, NCH), F32),
            pltpu.SemaphoreType.DMA((3,)),
        ],
        compiler_params=limit(16),
        cost_estimate=cost(5),
    )(in_hbm(voltages), in_hbm(flags), in_hbm(coeff))
    blocks = NCH // sum(chunks)
    return pl.pallas_call(
        functools.partial(spectrum_kernel, chunks),
        out_shape=[jax.ShapeDtypeStruct((blocks, size, inputs, 2 * frames), BF16) for size in chunks],
        in_specs=[VMEM, VMEM] + [HBM] * 4,
        out_specs=[VMEM] * len(chunks),
        scratch_shapes=[
            pltpu.VMEM((1, inputs), jnp.int32),
            pltpu.VMEM((1, NCH), jnp.int32),
            pltpu.VMEM((TAPS, NCH), F32),
            pltpu.VMEM((NCH, 2 * NCH), BF16),
            pltpu.VMEM((2, inputs * 8, NCH), F32),
            pltpu.VMEM((NCH * inputs, 2 * frames), F32),
            pltpu.SemaphoreType.DMA((4,)),
        ],
        compiler_params=limit(16),
        cost_estimate=cost(6),
    )(
        filtered,
        history,
        *[in_hbm(x) for x in (flags, order.reshape(1, NCH), coeff, jnp.asarray(dft_table(NCH)))],
    )


def halves_kernel(low_ref, high_ref, *refs):
    low_out, high_out = refs[-2:]
    low_out[...] = low_ref[...]
    high_out[...] = high_ref[...]


def halves(low, high, after=()):
    blocks = low.shape[0] // 2
    block = (blocks // 2,) + low.shape[1:]
    first = pl.BlockSpec(block, lambda n: (n, 0, 0, 0))
    second = pl.BlockSpec(block, lambda n: (2 + n, 0, 0, 0))
    return pl.pallas_call(
        halves_kernel,
        out_shape=[pltpu.HBM((blocks,) + low.shape[1:], BF16)] * 2,
        grid=(2,),
        in_specs=[first, second] + [ANY] * len(after),
        out_specs=[first, first],
        compiler_params=limit(62),
        cost_estimate=cost(0.1),
    )(low, high, *after)


def turned_panel(panel, lanes, low_sign):
    first = lax.broadcasted_iota(jnp.int32, (panel.shape[0], lanes), 1) < lanes // 2
    parts = []
    for s in range(panel.shape[1] // lanes):
        part = pltpu.roll(panel[:, s * lanes : (s + 1) * lanes].astype(F32), lanes // 2, axis=1)
        parts.append(jnp.where(first, low_sign * part, -low_sign * part).astype(BF16))
    return jnp.concatenate(parts, axis=1)


def correlated(by_row, moving, fixed):
    panel = moving.shape[0]
    left, right = (fixed, moving) if by_row else (moving, fixed)
    result = lax.dot_general(
        left, right, (((1,), (1,)), ((), ())), preferred_element_type=F32
    ) * (1.0 / (NCH * 8))
    if by_row:
        return result[:panel], result[panel:]
    return result[:, :panel], result[:, panel:]


def stacked(by_row, panel, lanes):
    return jnp.concatenate([panel, turned_panel(panel, lanes, 1.0 if by_row else -1.0)], axis=0)


def far_kernel(by_row, place_ref, *refs):
    re_ref, im_ref = refs[-2:]
    lanes = refs[0].shape[3]

    def panel(parts, index):
        near = [part[:, 0].reshape(-1, lanes) for part in parts[:3]]
        low, high = [part[:, 0].reshape(-1, lanes) for part in parts[3:]]
        return jnp.concatenate(near + [jnp.where(index < 2, low, high)], axis=1)

    mine = panel(refs[:5], place_ref[0])
    other = panel(refs[5:10], lax.rem(place_ref[1] + 2, 4))
    re, im = correlated(by_row, other, stacked(by_row, mine, lanes))
    re_ref[0] = re.astype(BF16)
    im_ref[0] = im.astype(BF16)


def far_products(place, slots, by_row, after=()):
    own = slots[0]
    blocks, size, inputs, lanes = own.shape
    quarter = blocks // 4
    panel = quarter * inputs

    def fixed(k, c):
        return (c[0], k, 0, 0)

    def fixed_half(k, c):
        return (lax.rem(c[0], 2), k, 0, 0)

    def other(k, c):
        return (lax.rem(c[1] + 2, 4), k, 0, 0)

    def other_half(k, c):
        return (lax.rem(c[1], 2), k, 0, 0)

    def data(index):
        return pl.BlockSpec((quarter, 1, inputs, lanes), index)

    whole = pl.BlockSpec((1, panel, panel), lambda k, c: (k, 0, 0))
    slots = [in_hbm(slot) for slot in slots[:3]] + list(slots[3:])
    return pl.pallas_call(
        functools.partial(far_kernel, by_row),
        out_shape=[pltpu.HBM((size, panel, panel), BF16)] * 2,
        grid_spec=pltpu.PrefetchScalarGridSpec(
            num_scalar_prefetch=1,
            grid=(size,),
            in_specs=[data(fixed)] * 3
            + [data(fixed_half)] * 2
            + [data(other)] * 3
            + [data(other_half)] * 2
            + [ANY] * len(after),
            out_specs=[whole, whole],
        ),
        compiler_params=limit(62),
        cost_estimate=cost(0.1),
    )(place, *slots, *slots, *after)


def formed(parts, lanes):
    beams = parts.shape[0] // 2
    values = []
    low = lax.broadcasted_iota(jnp.int32, (beams, lanes), 1) < lanes // 2
    for s in range(parts.shape[1] // lanes):
        piece = parts[:, s * lanes : (s + 1) * lanes]
        turned = pltpu.roll(piece[beams:], lanes // 2, axis=1)
        value = piece[:beams] + jnp.where(low, -turned, turned)
        values.append(value * value)
    return jnp.concatenate(values, axis=1) if len(values) > 1 else values[0]


def pooled(power, lanes, bins, sources):
    width = power.shape[1]
    pools = []
    for source in sources:
        lane = lax.broadcasted_iota(jnp.int32, (bins, lanes), 1)
        place = lax.broadcasted_iota(jnp.int32, (bins, lanes), 0)
        wanted = source * (lanes // 2 // INTEG) + lax.rem(lane, lanes // 2) // INTEG
        pools.append(jnp.where(place == wanted, 1.0 / INTEG, 0.0).astype(BF16))
    pool = jnp.concatenate(pools, axis=1) if len(pools) > 1 else pools[0]
    high = power.astype(BF16)
    rest = power - high.astype(F32)
    middle = rest.astype(BF16)
    low = (rest - middle.astype(F32)).astype(BF16)
    total = jnp.zeros((bins, power.shape[0]), F32)
    for term in (low, middle, high):
        total = total + lax.dot_general(
            pool, term, (((1,), (1,)), ((), ())), preferred_element_type=F32
        )
    return total


def near_kernel(by_row, first, place_ref, own_ref, prev_ref, next_ref, low_ref, high_ref, *refs):
    fixed, ring = place_ref[0], place_ref[1]
    if by_row:
        out_ref, up_ref, down_ref, x_ref = refs[-4:]
    else:
        w_hbm = refs[0]
        out_ref, up_ref, down_ref, beam_ref, x_ref, w_ref, sem = refs[-7:]
        k = pl.program_id(0)
        copy = pltpu.make_async_copy(w_hbm.at[:, first : first + w_ref.shape[1]], w_ref, sem)

        @pl.when(k == 0)
        def _():
            copy.start()

    blocks, _, inputs, lanes = own_ref.shape
    half = blocks // 2 * inputs
    total = blocks * inputs
    panel = total // 4
    for s, ref in enumerate((own_ref, prev_ref, next_ref)):
        x_ref[:, s * lanes : (s + 1) * lanes] = ref[:, 0].reshape(total, lanes)
    x_ref[:half, 3 * lanes :] = low_ref[:, 0].reshape(half, lanes)
    x_ref[half:, 3 * lanes :] = high_ref[:, 0].reshape(half, lanes)

    def panel_of(index):
        return x_ref[pl.ds(pl.multiple_of(index * panel, panel), panel), :]

    stack = stacked(by_row, panel_of(fixed), lanes)
    for step, ref in ((1, up_ref), (3, down_ref), (0, out_ref)):
        re, im = correlated(by_row, panel_of(lax.rem(ring + step, 4)), stack)
        ref[0, 0] = re.astype(ref.dtype)
        ref[1, 0] = im.astype(ref.dtype)
    if by_row:
        return

    @pl.when(k == 0)
    def _():
        copy.wait()

    beams = w_ref.shape[2]
    weights = w_ref[:, k].reshape(2 * beams, total)
    parts = lax.dot_general(
        weights, x_ref[...], (((1,), (0,)), ((), ())), preferred_element_type=F32
    )
    bins = lanes // 2 // INTEG
    sources = [lax.rem(fixed + shift, 4) for shift in (0, 3, 1, 2)]
    beam_ref[0] = pooled(formed(parts, lanes), lanes, 4 * bins, sources)


def near_products(place, slots, by_row, first=0, weights=None, after=()):
    blocks, size, inputs, lanes = slots[0].shape
    total = blocks * inputs
    panel = total // 4

    def data(count):
        return pl.BlockSpec((count, 1, inputs, lanes), lambda k, c: (0, k, 0, 0))

    block = pl.BlockSpec((2, 1, panel, panel), lambda k, c: (0, k, 0, 0))
    shape = (2, size, panel, panel)
    shapes = [pltpu.HBM(shape, F32), pltpu.HBM(shape, BF16), pltpu.HBM(shape, BF16)]
    specs = [block] * 3
    args = [in_hbm(slot) for slot in slots[:3]] + list(slots[3:])
    scratch = [pltpu.VMEM((total, 4 * lanes), BF16)]
    if not by_row:
        beams = weights.shape[2]
        bins = 4 * (lanes // 2 // INTEG)
        shapes.append(jax.ShapeDtypeStruct((size, bins, beams), F32))
        specs.append(pl.BlockSpec((1, bins, beams), lambda k, c: (k, 0, 0)))
        args.append(in_hbm(weights))
        scratch += [pltpu.VMEM((2, size) + weights.shape[2:], BF16), pltpu.SemaphoreType.DMA]
    args += after
    return pl.pallas_call(
        functools.partial(near_kernel, by_row, first),
        out_shape=shapes,
        grid_spec=pltpu.PrefetchScalarGridSpec(
            num_scalar_prefetch=1,
            grid=(size,),
            in_specs=[data(blocks)] * 3 + [data(blocks // 2)] * 2 + [ANY] * (len(args) - 5),
            out_specs=specs,
            scratch_shapes=scratch,
        ),
        compiler_params=limit(62),
        cost_estimate=cost(0.1),
    )(place, *args)


def beam_kernel(own_ref, w_ref, out_ref):
    blocks, _, inputs, lanes = own_ref.shape
    owners, _, _, beams, total = w_ref.shape
    x = own_ref[:, 0].reshape(blocks * inputs, lanes)
    weights = jnp.concatenate(
        [w_ref[:, part, 0].reshape(owners * beams, total) for part in range(2)], axis=0
    )
    parts = lax.dot_general(weights, x, (((1,), (0,)), ((), ())), preferred_element_type=F32)
    power = pooled(formed(parts, lanes), lanes, lanes // 2 // INTEG, [0])
    for owner in range(owners):
        out_ref[owner, 0] = power[:, owner * beams : (owner + 1) * beams]


def own_beams(own, weights, first=0):
    blocks, size, inputs, lanes = own.shape
    owners, _, _, beams, total = weights.shape
    bins = lanes // 2 // INTEG
    return pl.pallas_call(
        beam_kernel,
        out_shape=jax.ShapeDtypeStruct((owners, size, bins, beams), F32),
        grid=(size,),
        in_specs=[
            pl.BlockSpec((blocks, 1, inputs, lanes), lambda k: (0, k, 0, 0)),
            pl.BlockSpec((owners, 2, 1, beams, total), lambda k: (0, 0, first + k, 0, 0)),
        ],
        out_specs=pl.BlockSpec((owners, 1, bins, beams), lambda k: (0, k, 0, 0)),
        compiler_params=limit(62),
        cost_estimate=cost(0.1),
    )(in_hbm(own), in_hbm(weights))


def add_kernel(up_ref, down_ref, low_ref, high_ref, *refs):
    up_out, down_out = refs[-2:]
    up_out[0] = (up_ref[0].astype(F32) + low_ref[...].astype(F32)).astype(BF16)
    down_out[0] = (down_ref[0].astype(F32) + high_ref[...].astype(F32)).astype(BF16)


def added(up, down, low, high, after=()):
    _, size, panel, _ = up.shape
    real = pl.BlockSpec((1, size, panel, panel), lambda n: (0, 0, 0, 0))
    imag = pl.BlockSpec((1, size, panel, panel), lambda n: (1, 0, 0, 0))
    one = pl.BlockSpec((size, panel, panel), lambda n: (0, 0, 0))
    shape = pltpu.HBM(up.shape, BF16)
    return pl.pallas_call(
        add_kernel,
        out_shape=[shape, shape],
        grid=(1,),
        in_specs=[real, imag, one, one] + [ANY] * len(after),
        out_specs=[real, imag],
        input_output_aliases={0: 0, 1: 1},
        compiler_params=limit(62),
        cost_estimate=cost(0.1),
    )(up, down, low, high, *after)


def final_kernel(first, own_ref, prev_ref, next_ref, *refs):
    out_hbm, held, sems = refs[-3:]
    size = own_ref.shape[1]
    p = pl.program_id(0)

    def copy(part):
        return pltpu.make_async_copy(
            held.at[part], out_hbm.at[part, first : first + size], sems.at[part]
        )

    for part in range(2):

        @pl.when(p == part)
        def _(part=part):
            held[part] = own_ref[0] + prev_ref[0].astype(F32) + next_ref[0].astype(F32)
            copy(part).start()

    @pl.when(p == 1)
    def _():
        copy(0).wait()
        copy(1).wait()


def finished(own, from_prev, from_next, first, channels, out):
    _, size, panel, _ = own.shape
    block = pl.BlockSpec((1, size, panel, panel), lambda p: (p, 0, 0, 0))
    extra = [] if out is None else [out]
    return pl.pallas_call(
        functools.partial(final_kernel, first),
        out_shape=jax.ShapeDtypeStruct((2, channels, panel, panel), F32),
        grid=(2,),
        in_specs=[block] * 3 + [ANY] * len(extra),
        out_specs=HBM,
        input_output_aliases={3: 0} if extra else {},
        scratch_shapes=[
            pltpu.VMEM((2, size, panel, panel), F32),
            pltpu.SemaphoreType.DMA((2,)),
        ],
        compiler_params=limit(62),
        cost_estimate=cost(0.1),
    )(in_hbm(own), from_prev, from_next, *extra)


def along(value, axis, step):
    count = lax.axis_size(axis)
    return lax.ppermute(value, axis, [(i, (i + step) % count) for i in range(count)])


def both_ways(up, down, axis):
    return along(up, axis, 1), along(down, axis, -1)


def on_device(voltages, input_flags, channel_order, beam_weights):
    size_b, size_a = CHUNKS
    channels = size_a + size_b
    history = passed_along(voltages[:, :, voltages.shape[2] - (TAPS - 1) * NCH :], ("row", "col"), 1)
    row = lax.axis_index("row").astype(jnp.int32)
    col = lax.axis_index("col").astype(jnp.int32)
    place_a = jnp.stack([col, row])
    place_b = jnp.stack([row, col])
    weights = lax.all_gather(beam_weights, "col", axis=0)
    piece_b, piece_a = spectra(voltages, history, input_flags, channel_order, CHUNKS)

    def turn(piece, axis):
        return lax.all_to_all(piece, axis, split_axis=0, concat_axis=0, tiled=True)

    own_b = turn(piece_b, "chan")
    near_b = both_ways(own_b, own_b, "row")
    own_a = turn(piece_a, "chan")
    near_a = both_ways(own_a, own_a, "col")
    beam_b = own_beams(own_b, weights)
    far_b = both_ways(*halves(*near_b, [own_a, beam_b]), "row")
    slots_b = (own_b, *near_b, *far_b)
    re_b, im_b = far_products(place_b, slots_b, True)
    got_b = both_ways(re_b, im_b, "col")
    half_a = halves(*near_a, [re_b])
    far_a = both_ways(*half_a, "col")
    slots_a = (own_a, *near_a, *far_a)
    mine_b, up_b, down_b = near_products(place_b, slots_b, True, after=[half_a[0]])
    sum_b = added(up_b, down_b, *got_b)
    sent_b = both_ways(*sum_b, "col")
    re_a, im_a = far_products(place_a, slots_a, False, [sum_b[0]])
    got_a = both_ways(re_a, im_a, "row")
    mine_a, up_a, down_a, power_a = near_products(place_a, slots_a, False, size_b, beam_weights)
    sum_a = added(up_a, down_a, *got_a)
    sent_a = both_ways(*sum_a, "row")

    power_b = jnp.transpose(turn(beam_b, "col"), (1, 0, 2, 3)).reshape(size_b, -1, beam_b.shape[3])
    out = finished(mine_b, *sent_b, 0, channels, None)
    visibility = finished(mine_a, *sent_a, size_b, channels, out)
    power = jnp.concatenate([power_b, power_a], axis=0)
    return (visibility, jnp.transpose(power, (0, 2, 1)))


def solution(mesh):
    placed = (P(None, "chan", ("row", "col")), P("chan"), P(), P(None, "chan", "col", None))
    return jax.shard_map(
        on_device,
        mesh=mesh,
        in_specs=placed,
        out_specs=(P(None, "chan", "row", "col"), P("chan", "col", "row")),
        check_vma=False,
    )
```

```python
import functools
import math

import jax
import jax.numpy as jnp
import numpy as np
from jax import lax
from jax.experimental import pallas as pl
from jax.experimental.pallas import tpu as pltpu
from jax.sharding import PartitionSpec as P

NCH = 128
TAPS = 4
INTEG = 8
CHUNKS = (3, 3, 2)

F32 = jnp.float32
BF16 = jnp.bfloat16
VMEM = pl.BlockSpec(memory_space=pltpu.VMEM)
SMEM = pl.BlockSpec(memory_space=pltpu.SMEM)
ANY = pl.BlockSpec(memory_space=pl.ANY)
HBM = pl.BlockSpec(memory_space=pltpu.HBM)


def cost(micros):
    return pl.CostEstimate(flops=int(micros * 1.1e9), bytes_accessed=1, transcendentals=0)


def in_hbm(value):
    return pltpu.with_memory_space_constraint(value, pltpu.HBM)


def limit(mebibytes):
    return pltpu.CompilerParams(vmem_limit_bytes=mebibytes * 2**20)


def prototype(taps, length):
    position = np.arange(taps * length, dtype=np.float32) + np.float32(0.5)
    offset = position / np.float32(length) - np.float32(taps / 2.0)
    window = 0.5 - 0.5 * np.cos(2.0 * math.pi * position.astype(np.float64) / (taps * length))
    sinc = np.sin(math.pi * offset.astype(np.float64)) / (math.pi * offset.astype(np.float64))
    return (sinc * window).astype(np.float32).reshape(taps, length)


def dft_table(length):
    index = np.arange(length)
    angle = 2.0 * math.pi / length * (index[:, None] * index[None, :] % length)
    factor = 1.0 / math.sqrt(length)
    table = np.concatenate([np.cos(angle) * factor, np.sin(angle) * factor], axis=1)
    return table.astype(np.float32).astype(jnp.bfloat16)


def passed_along(value, axis, steps):
    count = lax.axis_size(axis)
    initial, last = (max(0, -steps), min(count, count - steps))
    return lax.ppermute(value, axis, [(source, source + steps) for source in range(initial, last)])


def flag_column(flags, inputs):
    eye = lax.broadcasted_iota(jnp.int32, (inputs, inputs), 0) == lax.broadcasted_iota(
        jnp.int32, (inputs, inputs), 1
    )
    held = jnp.where(eye, flags.astype(F32), 0.0)
    return jnp.broadcast_to(jnp.sum(held, axis=1, keepdims=True), (inputs, NCH))


def filter_kernel(
    first, v_hbm, flags_hbm, coeff_hbm, w_hbm, filt_ref, cut_hbm, v_ref, flags_ref, coeff_ref, w_ref, sems
):
    pairs = (
        (v_hbm.at[0], v_ref.at[0]),
        (flags_hbm, flags_ref),
        (coeff_hbm, coeff_ref),
        (v_hbm.at[1], v_ref.at[1]),
        (w_hbm.at[:, first : first + w_ref.shape[1]], w_ref),
        (w_ref, cut_hbm),
    )
    copies = [pltpu.make_async_copy(src, dst, sems.at[n]) for n, (src, dst) in enumerate(pairs)]
    for copy in copies[:5]:
        copy.start()
    for copy in copies[:3]:
        copy.wait()
    inputs = v_ref.shape[1]
    frames = v_ref.shape[2] // NCH
    mask = flag_column(flags_ref[...], inputs)
    taps = [jnp.broadcast_to(coeff_ref[t : t + 1, :], (inputs, NCH)) * mask for t in range(TAPS)]
    for part in range(2):
        if part == 1:
            copies[3].wait()
            copies[4].wait()
            copies[5].start()

        def frame_step(f, past, part=part):
            lanes = pl.ds(pl.multiple_of(f * NCH, NCH), NCH)
            window = past + (v_ref[part, :, lanes].astype(F32),)
            total = taps[0] * window[0]
            for t in range(1, TAPS):
                total = total + taps[t] * window[t]
            filt_ref[part, pl.ds(f, inputs, stride=frames), :] = total
            return window[1:]

        zero = v_ref[part, :, :NCH].astype(F32) * 0.0
        lax.fori_loop(0, frames, frame_step, (zero,) * (TAPS - 1), unroll=8)
    copies[5].wait()


def spectrum_kernel(chunks, filt_ref, halo_ref, flags_hbm, order_hbm, coeff_hbm, table_hbm, *rest):
    outs = rest[: len(chunks)]
    flags_ref, order_ref, coeff_ref, table_ref, corr_ref, spec_ref, sems = rest[len(chunks) :]
    copies = [
        pltpu.make_async_copy(src, dst, sems.at[n])
        for n, (src, dst) in enumerate(
            (
                (flags_hbm, flags_ref),
                (order_hbm, order_ref),
                (coeff_hbm, coeff_ref),
                (table_hbm, table_ref),
            )
        )
    ]
    for copy in copies:
        copy.start()
    for copy in copies:
        copy.wait()
    inputs = halo_ref.shape[1]
    frames = filt_ref.shape[1] // inputs
    rows = 8
    mask = flag_column(flags_ref[...], inputs)
    taps = [jnp.broadcast_to(coeff_ref[t : t + 1, :], (inputs, NCH)) * mask for t in range(TAPS)]
    for part in range(2):
        past = [halo_ref[part, :, t * NCH : (t + 1) * NCH].astype(F32) for t in range(TAPS - 1)]
        for f in range(rows):
            total = jnp.zeros((inputs, NCH), F32)
            for t in range(TAPS - 1 - f):
                total = total + taps[t] * past[f + t]
            corr_ref[part, pl.ds(f, inputs, stride=rows), :] = total
    onehot = lax.broadcasted_iota(jnp.int32, (NCH, NCH), 0) == jnp.broadcast_to(
        order_ref[...], (NCH, NCH)
    )
    table = lax.dot_general(
        onehot.astype(BF16), table_ref[...], (((0,), (0,)), ((), ())), preferred_element_type=F32
    ).astype(BF16)

    def input_step(pair, carry):
        blocks = []
        for which in range(2):
            i = pair * 2 + which
            both = []
            for part in range(2):
                block = filt_ref[part, pl.ds(pl.multiple_of(i * frames, frames), frames), :]
                extra = corr_ref[part, pl.ds(pl.multiple_of(i * rows, rows), rows), :]
                both.append(jnp.concatenate([block[:rows] + extra, block[rows:]], axis=0).astype(BF16))
            re, im = both
            blocks.append(jnp.concatenate([re, im], axis=1))
            blocks.append(jnp.concatenate([im, -re], axis=1))
        right = jnp.concatenate(blocks, axis=0)
        result = lax.dot_general(
            table, right, (((1,), (1,)), ((), ())), preferred_element_type=F32
        )
        for which in range(2):
            spec_ref[pl.ds(pair * 2 + which, NCH, stride=inputs), :] = result[
                :, which * NCH : (which + 1) * NCH
            ]
        return carry

    lax.fori_loop(0, inputs // 2, input_step, 0, unroll=4)
    per_block = sum(chunks)

    def copy_step(block, carry):
        first = 0
        for out, size in zip(outs, chunks):
            for k in range(size):
                at = pl.multiple_of((block * per_block + first + k) * inputs, inputs)
                out[block, k] = spec_ref[pl.ds(at, inputs), :].astype(BF16)
            first += size
        return carry

    lax.fori_loop(0, NCH // per_block, copy_step, 0)


def spectra(voltages, history, flags, order, weights, chunks):
    inputs = voltages.shape[1]
    frames = voltages.shape[2] // NCH
    flags = flags.reshape(1, inputs)
    coeff = jnp.asarray(prototype(TAPS, NCH))
    held = (2, chunks[1]) + weights.shape[2:]
    filtered, cut = pl.pallas_call(
        functools.partial(filter_kernel, chunks[0]),
        out_shape=[jax.ShapeDtypeStruct((2, inputs * frames, NCH), F32), pltpu.HBM(held, BF16)],
        in_specs=[HBM] * 4,
        out_specs=[VMEM, HBM],
        scratch_shapes=[
            pltpu.VMEM(voltages.shape, BF16),
            pltpu.VMEM((1, inputs), jnp.int32),
            pltpu.VMEM((TAPS, NCH), F32),
            pltpu.VMEM(held, BF16),
            pltpu.SemaphoreType.DMA((6,)),
        ],
        compiler_params=limit(16),
        cost_estimate=cost(5),
    )(in_hbm(voltages), in_hbm(flags), in_hbm(coeff), in_hbm(weights))
    blocks = NCH // sum(chunks)
    pieces = pl.pallas_call(
        functools.partial(spectrum_kernel, chunks),
        out_shape=[jax.ShapeDtypeStruct((blocks, size, inputs, 2 * frames), BF16) for size in chunks],
        in_specs=[VMEM, VMEM] + [HBM] * 4,
        out_specs=[VMEM] * len(chunks),
        scratch_shapes=[
            pltpu.VMEM((1, inputs), jnp.int32),
            pltpu.VMEM((1, NCH), jnp.int32),
            pltpu.VMEM((TAPS, NCH), F32),
            pltpu.VMEM((NCH, 2 * NCH), BF16),
            pltpu.VMEM((2, inputs * 8, NCH), F32),
            pltpu.VMEM((NCH * inputs, 2 * frames), F32),
            pltpu.SemaphoreType.DMA((4,)),
        ],
        compiler_params=limit(16),
        cost_estimate=cost(6),
    )(
        filtered,
        history,
        *[in_hbm(x) for x in (flags, order.reshape(1, NCH), coeff, jnp.asarray(dft_table(NCH)))],
    )
    return pieces, cut


def halves_kernel(low_ref, high_ref, *refs):
    low_out, high_out = refs[-2:]
    low_out[...] = low_ref[...]
    high_out[...] = high_ref[...]


def halves(low, high, after=()):
    blocks = low.shape[0] // 2
    block = (blocks // 2,) + low.shape[1:]
    first = pl.BlockSpec(block, lambda n: (n, 0, 0, 0))
    second = pl.BlockSpec(block, lambda n: (2 + n, 0, 0, 0))
    return pl.pallas_call(
        halves_kernel,
        out_shape=[pltpu.HBM((blocks,) + low.shape[1:], BF16)] * 2,
        grid=(2,),
        in_specs=[first, second] + [ANY] * len(after),
        out_specs=[first, first],
        compiler_params=limit(62),
        cost_estimate=cost(0.1),
    )(low, high, *after)


def turned_panel(panel, lanes, low_sign):
    first = lax.broadcasted_iota(jnp.int32, (panel.shape[0], lanes), 1) < lanes // 2
    parts = []
    for s in range(panel.shape[1] // lanes):
        part = pltpu.roll(panel[:, s * lanes : (s + 1) * lanes].astype(F32), lanes // 2, axis=1)
        parts.append(jnp.where(first, low_sign * part, -low_sign * part).astype(BF16))
    return jnp.concatenate(parts, axis=1)


def correlated(by_row, moving, fixed):
    panel = moving.shape[0]
    left, right = (fixed, moving) if by_row else (moving, fixed)
    result = lax.dot_general(
        left, right, (((1,), (1,)), ((), ())), preferred_element_type=F32
    ) * (1.0 / (NCH * 8))
    if by_row:
        return result[:panel], result[panel:]
    return result[:, :panel], result[:, panel:]


def stacked(by_row, panel, lanes):
    return jnp.concatenate([panel, turned_panel(panel, lanes, 1.0 if by_row else -1.0)], axis=0)


def far_kernel(by_row, place_ref, *refs):
    re_ref, im_ref = refs[-2:]
    lanes = refs[0].shape[3]

    def panel(parts, index):
        near = [part[:, 0].reshape(-1, lanes) for part in parts[:3]]
        low, high = [part[:, 0].reshape(-1, lanes) for part in parts[3:]]
        return jnp.concatenate(near + [jnp.where(index < 2, low, high)], axis=1)

    mine = panel(refs[:5], place_ref[0])
    other = panel(refs[5:10], lax.rem(place_ref[1] + 2, 4))
    re, im = correlated(by_row, other, stacked(by_row, mine, lanes))
    re_ref[0] = re.astype(BF16)
    im_ref[0] = im.astype(BF16)


def far_products(place, slots, by_row, after=()):
    own = slots[0]
    blocks, size, inputs, lanes = own.shape
    quarter = blocks // 4
    panel = quarter * inputs

    def fixed(k, c):
        return (c[0], k, 0, 0)

    def fixed_half(k, c):
        return (lax.rem(c[0], 2), k, 0, 0)

    def other(k, c):
        return (lax.rem(c[1] + 2, 4), k, 0, 0)

    def other_half(k, c):
        return (lax.rem(c[1], 2), k, 0, 0)

    def data(index):
        return pl.BlockSpec((quarter, 1, inputs, lanes), index)

    whole = pl.BlockSpec((1, panel, panel), lambda k, c: (k, 0, 0))
    slots = [in_hbm(slot) for slot in slots[:3]] + list(slots[3:])
    return pl.pallas_call(
        functools.partial(far_kernel, by_row),
        out_shape=[pltpu.HBM((size, panel, panel), BF16)] * 2,
        grid_spec=pltpu.PrefetchScalarGridSpec(
            num_scalar_prefetch=1,
            grid=(size,),
            in_specs=[data(fixed)] * 3
            + [data(fixed_half)] * 2
            + [data(other)] * 3
            + [data(other_half)] * 2
            + [ANY] * len(after),
            out_specs=[whole, whole],
        ),
        compiler_params=limit(62),
        cost_estimate=cost(0.1),
    )(place, *slots, *slots, *after)


def formed(parts, lanes):
    beams = parts.shape[0] // 2
    values = []
    low = lax.broadcasted_iota(jnp.int32, (beams, lanes), 1) < lanes // 2
    for s in range(parts.shape[1] // lanes):
        piece = parts[:, s * lanes : (s + 1) * lanes]
        turned = pltpu.roll(piece[beams:], lanes // 2, axis=1)
        value = piece[:beams] + jnp.where(low, -turned, turned)
        values.append(value * value)
    return jnp.concatenate(values, axis=1) if len(values) > 1 else values[0]


def pooled(power, lanes, bins, sources):
    width = power.shape[1]
    pools = []
    for source in sources:
        lane = lax.broadcasted_iota(jnp.int32, (bins, lanes), 1)
        place = lax.broadcasted_iota(jnp.int32, (bins, lanes), 0)
        wanted = source * (lanes // 2 // INTEG) + lax.rem(lane, lanes // 2) // INTEG
        pools.append(jnp.where(place == wanted, 1.0 / INTEG, 0.0).astype(BF16))
    pool = jnp.concatenate(pools, axis=1) if len(pools) > 1 else pools[0]
    high = power.astype(BF16)
    rest = power - high.astype(F32)
    middle = rest.astype(BF16)
    low = (rest - middle.astype(F32)).astype(BF16)
    total = jnp.zeros((bins, power.shape[0]), F32)
    for term in (low, middle, high):
        total = total + lax.dot_general(
            pool, term, (((1,), (1,)), ((), ())), preferred_element_type=F32
        )
    return total


def near_kernel(by_row, first, place_ref, own_ref, prev_ref, next_ref, low_ref, high_ref, *refs):
    fixed, ring = place_ref[0], place_ref[1]
    if by_row:
        out_ref, up_ref, down_ref, x_ref = refs[-4:]
    else:
        w_hbm = refs[0]
        out_ref, up_ref, down_ref, beam_ref, x_ref, w_ref, sem = refs[-7:]
        k = pl.program_id(0)
        copy = pltpu.make_async_copy(w_hbm.at[:, first : first + w_ref.shape[1]], w_ref, sem)

        @pl.when(k == 0)
        def _():
            copy.start()

    blocks, _, inputs, lanes = own_ref.shape
    half = blocks // 2 * inputs
    total = blocks * inputs
    panel = total // 4
    for s, ref in enumerate((own_ref, prev_ref, next_ref)):
        x_ref[:, s * lanes : (s + 1) * lanes] = ref[:, 0].reshape(total, lanes)
    x_ref[:half, 3 * lanes :] = low_ref[:, 0].reshape(half, lanes)
    x_ref[half:, 3 * lanes :] = high_ref[:, 0].reshape(half, lanes)

    def panel_of(index):
        return x_ref[pl.ds(pl.multiple_of(index * panel, panel), panel), :]

    stack = stacked(by_row, panel_of(fixed), lanes)
    for step, ref in ((1, up_ref), (3, down_ref), (0, out_ref)):
        re, im = correlated(by_row, panel_of(lax.rem(ring + step, 4)), stack)
        ref[0, 0] = re.astype(ref.dtype)
        ref[1, 0] = im.astype(ref.dtype)
    if by_row:
        return

    @pl.when(k == 0)
    def _():
        copy.wait()

    beams = w_ref.shape[2]
    weights = w_ref[:, k].reshape(2 * beams, total)
    parts = lax.dot_general(
        weights, x_ref[...], (((1,), (0,)), ((), ())), preferred_element_type=F32
    )
    bins = lanes // 2 // INTEG
    sources = [lax.rem(fixed + shift, 4) for shift in (0, 3, 1, 2)]
    beam_ref[0] = pooled(formed(parts, lanes), lanes, 4 * bins, sources)


def near_products(place, slots, by_row, first=0, weights=None, after=()):
    blocks, size, inputs, lanes = slots[0].shape
    total = blocks * inputs
    panel = total // 4

    def data(count):
        return pl.BlockSpec((count, 1, inputs, lanes), lambda k, c: (0, k, 0, 0))

    block = pl.BlockSpec((2, 1, panel, panel), lambda k, c: (0, k, 0, 0))
    shape = (2, size, panel, panel)
    shapes = [pltpu.HBM(shape, F32), pltpu.HBM(shape, BF16), pltpu.HBM(shape, BF16)]
    specs = [block] * 3
    args = [in_hbm(slot) for slot in slots[:3]] + list(slots[3:])
    scratch = [pltpu.VMEM((total, 4 * lanes), BF16)]
    if not by_row:
        beams = weights.shape[2]
        bins = 4 * (lanes // 2 // INTEG)
        shapes.append(jax.ShapeDtypeStruct((size, bins, beams), F32))
        specs.append(pl.BlockSpec((1, bins, beams), lambda k, c: (k, 0, 0)))
        args.append(in_hbm(weights))
        scratch += [pltpu.VMEM((2, size) + weights.shape[2:], BF16), pltpu.SemaphoreType.DMA]
    args += after
    return pl.pallas_call(
        functools.partial(near_kernel, by_row, first),
        out_shape=shapes,
        grid_spec=pltpu.PrefetchScalarGridSpec(
            num_scalar_prefetch=1,
            grid=(size,),
            in_specs=[data(blocks)] * 3 + [data(blocks // 2)] * 2 + [ANY] * (len(args) - 5),
            out_specs=specs,
            scratch_shapes=scratch,
        ),
        compiler_params=limit(62),
        cost_estimate=cost(0.1),
    )(place, *args)


def beam_kernel(own_ref, w_ref, *refs):
    out_ref = refs[-1]
    blocks, _, inputs, lanes = own_ref.shape
    owners, _, _, beams, total = w_ref.shape
    x = own_ref[:, 0].reshape(blocks * inputs, lanes)
    weights = jnp.concatenate(
        [w_ref[:, part, 0].reshape(owners * beams, total) for part in range(2)], axis=0
    )
    parts = lax.dot_general(weights, x, (((1,), (0,)), ((), ())), preferred_element_type=F32)
    power = pooled(formed(parts, lanes), lanes, lanes // 2 // INTEG, [0])
    for owner in range(owners):
        out_ref[owner, 0] = power[:, owner * beams : (owner + 1) * beams]


def own_beams(own, weights, first=0, after=()):
    blocks, size, inputs, lanes = own.shape
    owners, _, _, beams, total = weights.shape
    bins = lanes // 2 // INTEG
    return pl.pallas_call(
        beam_kernel,
        out_shape=jax.ShapeDtypeStruct((owners, size, bins, beams), F32),
        grid=(size,),
        in_specs=[
            pl.BlockSpec((blocks, 1, inputs, lanes), lambda k: (0, k, 0, 0)),
            pl.BlockSpec((owners, 2, 1, beams, total), lambda k: (0, 0, first + k, 0, 0)),
        ]
        + [ANY] * len(after),
        out_specs=pl.BlockSpec((owners, 1, bins, beams), lambda k: (0, k, 0, 0)),
        compiler_params=limit(62),
        cost_estimate=cost(0.1),
    )(in_hbm(own), in_hbm(weights), *after)


def add_kernel(up_ref, down_ref, low_ref, high_ref, *refs):
    up_out, down_out = refs[-2:]
    up_out[0] = (up_ref[0].astype(F32) + low_ref[...].astype(F32)).astype(BF16)
    down_out[0] = (down_ref[0].astype(F32) + high_ref[...].astype(F32)).astype(BF16)


def added(up, down, low, high, after=()):
    _, size, panel, _ = up.shape
    real = pl.BlockSpec((1, size, panel, panel), lambda n: (0, 0, 0, 0))
    imag = pl.BlockSpec((1, size, panel, panel), lambda n: (1, 0, 0, 0))
    one = pl.BlockSpec((size, panel, panel), lambda n: (0, 0, 0))
    shape = pltpu.HBM(up.shape, BF16)
    return pl.pallas_call(
        add_kernel,
        out_shape=[shape, shape],
        grid=(1,),
        in_specs=[real, imag, one, one] + [ANY] * len(after),
        out_specs=[real, imag],
        input_output_aliases={0: 0, 1: 1},
        compiler_params=limit(62),
        cost_estimate=cost(0.1),
    )(up, down, low, high, *after)


def final_kernel(first, own_ref, prev_ref, next_ref, *refs):
    out_hbm, token_ref, held, sems = refs[-4:]
    token_ref[...] = jnp.zeros_like(token_ref)
    size = own_ref.shape[1]
    p = pl.program_id(0)

    def copy(part):
        return pltpu.make_async_copy(
            held.at[part], out_hbm.at[part, first : first + size], sems.at[part]
        )

    for part in range(2):

        @pl.when(p == part)
        def _(part=part):
            held[part] = own_ref[0] + prev_ref[0].astype(F32) + next_ref[0].astype(F32)
            copy(part).start()

    @pl.when(p == 1)
    def _():
        copy(0).wait()
        copy(1).wait()


def finished(own, from_prev, from_next, first, channels, out, after=()):
    _, size, panel, _ = own.shape
    block = pl.BlockSpec((1, size, panel, panel), lambda p: (p, 0, 0, 0))
    extra = [] if out is None else [out]
    return pl.pallas_call(
        functools.partial(final_kernel, first),
        out_shape=[
            jax.ShapeDtypeStruct((2, channels, panel, panel), F32),
            jax.ShapeDtypeStruct((8, NCH), F32),
        ],
        grid=(2,),
        in_specs=[block] * 3 + [ANY] * (len(extra) + len(after)),
        out_specs=[HBM, pl.BlockSpec((8, NCH), lambda p: (0, 0))],
        input_output_aliases={3: 0} if extra else {},
        scratch_shapes=[
            pltpu.VMEM((2, size, panel, panel), F32),
            pltpu.SemaphoreType.DMA((2,)),
        ],
        compiler_params=limit(62),
        cost_estimate=cost(0.1),
    )(in_hbm(own), from_prev, from_next, *extra, *after)


def along(value, axis, step):
    count = lax.axis_size(axis)
    return lax.ppermute(value, axis, [(i, (i + step) % count) for i in range(count)])


def both_ways(up, down, axis):
    return along(up, axis, 1), along(down, axis, -1)


def on_device(voltages, input_flags, channel_order, beam_weights):
    firsts = [sum(CHUNKS[:n]) for n in range(len(CHUNKS))]
    history = passed_along(voltages[:, :, voltages.shape[2] - (TAPS - 1) * NCH :], ("row", "col"), 1)
    row = lax.axis_index("row").astype(jnp.int32)
    col = lax.axis_index("col").astype(jnp.int32)
    by_row = (False, True, False)
    places = [jnp.stack([row, col]) if turned else jnp.stack([col, row]) for turned in by_row]
    gather = [("row" if turned else "col") for turned in by_row]
    reduce = [("col" if turned else "row") for turned in by_row]
    pieces, cut = spectra(voltages, history, input_flags, channel_order, beam_weights, CHUNKS)
    weights = lax.all_gather(cut, "col", axis=0)

    def turn(piece, axis):
        return lax.all_to_all(piece, axis, split_axis=0, concat_axis=0, tiled=True)

    own = [turn(piece, "chan") for piece in pieces]
    near = [both_ways(x, x, axis) for x, axis in zip(own, gather)]

    def spread(n, after):
        half = halves(*near[n], after)
        return half, (own[n], *near[n], *both_ways(*half, gather[n]))

    def far(n, slots, after):
        sides = far_products(places[n], slots, by_row[n], after)
        return sides, both_ways(*sides, reduce[n])

    def near_by(n, slots, after):
        given = None if by_row[n] else beam_weights
        return near_products(places[n], slots, by_row[n], firsts[n], given, after)

    def send(n, results, got, after):
        sums = added(results[1], results[2], *got, after)
        return sums, both_ways(*sums, reduce[n])

    def close(n, result, sent, out, after):
        return finished(result[0], *sent, firsts[n], sum(CHUNKS), out, after)

    half, slots0 = spread(0, [])
    sides, got0 = far(0, slots0, [])
    result0 = near_by(0, slots0, [sides[0]])
    half, slots1 = spread(1, [result0[0]])
    sums, sent0 = send(0, result0, got0, [half[0]])
    beam1 = own_beams(own[1], weights, after=[sums[0]])
    sides, got1 = far(1, slots1, [beam1])
    half, slots2 = spread(2, [sides[0]])
    result1 = near_by(1, slots1, [half[0]])
    sums, sent1 = send(1, result1, got1, [])
    out, token = close(0, result0, sent0, None, [sums[0]])
    sides, got2 = far(2, slots2, [token])
    result2 = near_by(2, slots2, [sides[0]])
    sums, sent2 = send(2, result2, got2, [])
    power1 = jnp.transpose(turn(beam1, "col"), (1, 0, 2, 3)).reshape(CHUNKS[1], -1, beam1.shape[3])
    out, token = close(1, result1, sent1, out, [sums[0]])
    out, token = close(2, result2, sent2, out, [])
    power = jnp.concatenate([result0[3], power1, result2[3]], axis=0)
    return (out, jnp.transpose(power, (0, 2, 1)))


def solution(mesh):
    placed = (P(None, "chan", ("row", "col")), P("chan"), P(), P(None, "chan", "col", None))
    return jax.shard_map(
        on_device,
        mesh=mesh,
        in_specs=placed,
        out_specs=(P(None, "chan", "row", "col"), P("chan", "col", "row")),
        check_vma=False,
    )
```

```python
import functools
import math

import jax
import jax.numpy as jnp
import numpy as np
from jax import lax
from jax.experimental import pallas as pl
from jax.experimental.pallas import tpu as pltpu
from jax.sharding import PartitionSpec as P

NCH = 128
TAPS = 4
INTEG = 8
CHUNKS = (4, 4)

F32 = jnp.float32
BF16 = jnp.bfloat16
VMEM = pl.BlockSpec(memory_space=pltpu.VMEM)
SMEM = pl.BlockSpec(memory_space=pltpu.SMEM)
ANY = pl.BlockSpec(memory_space=pl.ANY)
HBM = pl.BlockSpec(memory_space=pltpu.HBM)


def cost(micros):
    return pl.CostEstimate(flops=int(micros * 1.1e9), bytes_accessed=1, transcendentals=0)


def in_hbm(value):
    return pltpu.with_memory_space_constraint(value, pltpu.HBM)


def limit(mebibytes):
    return pltpu.CompilerParams(vmem_limit_bytes=mebibytes * 2**20)


def prototype(taps, length):
    position = np.arange(taps * length, dtype=np.float32) + np.float32(0.5)
    offset = position / np.float32(length) - np.float32(taps / 2.0)
    window = 0.5 - 0.5 * np.cos(2.0 * math.pi * position.astype(np.float64) / (taps * length))
    sinc = np.sin(math.pi * offset.astype(np.float64)) / (math.pi * offset.astype(np.float64))
    return (sinc * window).astype(np.float32).reshape(taps, length)


def dft_table(length):
    index = np.arange(length)
    angle = 2.0 * math.pi / length * (index[:, None] * index[None, :] % length)
    factor = 1.0 / math.sqrt(length)
    table = np.concatenate([np.cos(angle) * factor, np.sin(angle) * factor], axis=1)
    return table.astype(np.float32).astype(jnp.bfloat16)


def passed_along(value, axis, steps):
    count = lax.axis_size(axis)
    initial, last = (max(0, -steps), min(count, count - steps))
    return lax.ppermute(value, axis, [(source, source + steps) for source in range(initial, last)])


def flag_column(flags, inputs):
    eye = lax.broadcasted_iota(jnp.int32, (inputs, inputs), 0) == lax.broadcasted_iota(
        jnp.int32, (inputs, inputs), 1
    )
    held = jnp.where(eye, flags.astype(F32), 0.0)
    return jnp.broadcast_to(jnp.sum(held, axis=1, keepdims=True), (inputs, NCH))


def filter_kernel(v_hbm, flags_hbm, coeff_hbm, filt_ref, v_ref, flags_ref, coeff_ref, sems):
    copies = [
        pltpu.make_async_copy(src, dst, sems.at[n])
        for n, (src, dst) in enumerate(
            ((v_hbm, v_ref), (flags_hbm, flags_ref), (coeff_hbm, coeff_ref))
        )
    ]
    for copy in copies:
        copy.start()
    for copy in copies:
        copy.wait()
    inputs = v_ref.shape[1]
    frames = v_ref.shape[2] // NCH
    mask = flag_column(flags_ref[...], inputs)
    taps = [jnp.broadcast_to(coeff_ref[t : t + 1, :], (inputs, NCH)) * mask for t in range(TAPS)]
    for part in range(2):

        def frame_step(f, past, part=part):
            lanes = pl.ds(pl.multiple_of(f * NCH, NCH), NCH)
            window = past + (v_ref[part, :, lanes].astype(F32),)
            total = taps[0] * window[0]
            for t in range(1, TAPS):
                total = total + taps[t] * window[t]
            filt_ref[part, pl.ds(f, inputs, stride=frames), :] = total
            return window[1:]

        zero = v_ref[part, :, :NCH].astype(F32) * 0.0
        lax.fori_loop(0, frames, frame_step, (zero,) * (TAPS - 1), unroll=8)


def spectrum_kernel(chunks, filt_ref, halo_ref, flags_hbm, order_hbm, coeff_hbm, table_hbm, *rest):
    outs = rest[: len(chunks)]
    flags_ref, order_ref, coeff_ref, table_ref, corr_ref, spec_ref, sems = rest[len(chunks) :]
    copies = [
        pltpu.make_async_copy(src, dst, sems.at[n])
        for n, (src, dst) in enumerate(
            (
                (flags_hbm, flags_ref),
                (order_hbm, order_ref),
                (coeff_hbm, coeff_ref),
                (table_hbm, table_ref),
            )
        )
    ]
    for copy in copies:
        copy.start()
    for copy in copies:
        copy.wait()
    inputs = halo_ref.shape[1]
    frames = filt_ref.shape[1] // inputs
    rows = 8
    mask = flag_column(flags_ref[...], inputs)
    taps = [jnp.broadcast_to(coeff_ref[t : t + 1, :], (inputs, NCH)) * mask for t in range(TAPS)]
    for part in range(2):
        past = [halo_ref[part, :, t * NCH : (t + 1) * NCH].astype(F32) for t in range(TAPS - 1)]
        for f in range(rows):
            total = jnp.zeros((inputs, NCH), F32)
            for t in range(TAPS - 1 - f):
                total = total + taps[t] * past[f + t]
            corr_ref[part, pl.ds(f, inputs, stride=rows), :] = total
    onehot = lax.broadcasted_iota(jnp.int32, (NCH, NCH), 0) == jnp.broadcast_to(
        order_ref[...], (NCH, NCH)
    )
    table = lax.dot_general(
        onehot.astype(BF16), table_ref[...], (((0,), (0,)), ((), ())), preferred_element_type=F32
    ).astype(BF16)

    def input_step(pair, carry):
        blocks = []
        for which in range(2):
            i = pair * 2 + which
            both = []
            for part in range(2):
                block = filt_ref[part, pl.ds(pl.multiple_of(i * frames, frames), frames), :]
                extra = corr_ref[part, pl.ds(pl.multiple_of(i * rows, rows), rows), :]
                both.append(jnp.concatenate([block[:rows] + extra, block[rows:]], axis=0).astype(BF16))
            re, im = both
            blocks.append(jnp.concatenate([re, im], axis=1))
            blocks.append(jnp.concatenate([im, -re], axis=1))
        right = jnp.concatenate(blocks, axis=0)
        result = lax.dot_general(
            table, right, (((1,), (1,)), ((), ())), preferred_element_type=F32
        )
        for which in range(2):
            spec_ref[pl.ds(pair * 2 + which, NCH, stride=inputs), :] = result[
                :, which * NCH : (which + 1) * NCH
            ]
        return carry

    lax.fori_loop(0, inputs // 2, input_step, 0, unroll=4)
    per_block = sum(chunks)

    def copy_step(block, carry):
        first = 0
        for out, size in zip(outs, chunks):
            for k in range(size):
                at = pl.multiple_of((block * per_block + first + k) * inputs, inputs)
                out[block, k] = spec_ref[pl.ds(at, inputs), :].astype(BF16)
            first += size
        return carry

    lax.fori_loop(0, NCH // per_block, copy_step, 0)


def spectra(voltages, history, flags, order, chunks):
    inputs = voltages.shape[1]
    frames = voltages.shape[2] // NCH
    flags = flags.reshape(1, inputs)
    coeff = jnp.asarray(prototype(TAPS, NCH))
    filtered = pl.pallas_call(
        filter_kernel,
        out_shape=jax.ShapeDtypeStruct((2, inputs * frames, NCH), F32),
        in_specs=[HBM] * 3,
        out_specs=VMEM,
        scratch_shapes=[
            pltpu.VMEM(voltages.shape, BF16),
            pltpu.VMEM((1, inputs), jnp.int32),
            pltpu.VMEM((TAPS, NCH), F32),
            pltpu.SemaphoreType.DMA((3,)),
        ],
        compiler_params=limit(16),
        cost_estimate=cost(5),
    )(in_hbm(voltages), in_hbm(flags), in_hbm(coeff))
    blocks = NCH // sum(chunks)
    return pl.pallas_call(
        functools.partial(spectrum_kernel, chunks),
        out_shape=[jax.ShapeDtypeStruct((blocks, size, inputs, 2 * frames), BF16) for size in chunks],
        in_specs=[VMEM, VMEM] + [HBM] * 4,
        out_specs=[VMEM] * len(chunks),
        scratch_shapes=[
            pltpu.VMEM((1, inputs), jnp.int32),
            pltpu.VMEM((1, NCH), jnp.int32),
            pltpu.VMEM((TAPS, NCH), F32),
            pltpu.VMEM((NCH, 2 * NCH), BF16),
            pltpu.VMEM((2, inputs * 8, NCH), F32),
            pltpu.VMEM((NCH * inputs, 2 * frames), F32),
            pltpu.SemaphoreType.DMA((4,)),
        ],
        compiler_params=limit(16),
        cost_estimate=cost(6),
    )(
        filtered,
        history,
        *[in_hbm(x) for x in (flags, order.reshape(1, NCH), coeff, jnp.asarray(dft_table(NCH)))],
    )


def halves_kernel(low_ref, high_ref, *refs):
    low_out, high_out = refs[-2:]
    low_out[...] = low_ref[...]
    high_out[...] = high_ref[...]


def halves(low, high, after=()):
    blocks = low.shape[0] // 2
    block = (blocks // 2,) + low.shape[1:]
    first = pl.BlockSpec(block, lambda n: (n, 0, 0, 0))
    second = pl.BlockSpec(block, lambda n: (2 + n, 0, 0, 0))
    return pl.pallas_call(
        halves_kernel,
        out_shape=[pltpu.HBM((blocks,) + low.shape[1:], BF16)] * 2,
        grid=(2,),
        in_specs=[first, second] + [ANY] * len(after),
        out_specs=[first, first],
        compiler_params=limit(62),
        cost_estimate=cost(0.1),
    )(low, high, *after)


def turned_panel(panel, lanes, low_sign):
    first = lax.broadcasted_iota(jnp.int32, (panel.shape[0], lanes), 1) < lanes // 2
    parts = []
    for s in range(panel.shape[1] // lanes):
        part = pltpu.roll(panel[:, s * lanes : (s + 1) * lanes].astype(F32), lanes // 2, axis=1)
        parts.append(jnp.where(first, low_sign * part, -low_sign * part).astype(BF16))
    return jnp.concatenate(parts, axis=1)


def correlated(by_row, moving, fixed):
    panel = moving.shape[0]
    left, right = (fixed, moving) if by_row else (moving, fixed)
    result = lax.dot_general(
        left, right, (((1,), (1,)), ((), ())), preferred_element_type=F32
    ) * (1.0 / (NCH * 8))
    if by_row:
        return result[:panel], result[panel:]
    return result[:, :panel], result[:, panel:]


def stacked(by_row, panel, lanes):
    return jnp.concatenate([panel, turned_panel(panel, lanes, 1.0 if by_row else -1.0)], axis=0)


def far_kernel(by_row, place_ref, *refs):
    re_ref, im_ref = refs[-2:]
    lanes = refs[0].shape[3]

    def panel(parts, index):
        near = [part[:, 0].reshape(-1, lanes) for part in parts[:3]]
        low, high = [part[:, 0].reshape(-1, lanes) for part in parts[3:]]
        return jnp.concatenate(near + [jnp.where(index < 2, low, high)], axis=1)

    mine = panel(refs[:5], place_ref[0])
    other = panel(refs[5:10], lax.rem(place_ref[1] + 2, 4))
    re, im = correlated(by_row, other, stacked(by_row, mine, lanes))
    re_ref[0] = re.astype(BF16)
    im_ref[0] = im.astype(BF16)


def far_products(place, slots, by_row, after=()):
    own = slots[0]
    blocks, size, inputs, lanes = own.shape
    quarter = blocks // 4
    panel = quarter * inputs

    def fixed(k, c):
        return (c[0], k, 0, 0)

    def fixed_half(k, c):
        return (lax.rem(c[0], 2), k, 0, 0)

    def other(k, c):
        return (lax.rem(c[1] + 2, 4), k, 0, 0)

    def other_half(k, c):
        return (lax.rem(c[1], 2), k, 0, 0)

    def data(index):
        return pl.BlockSpec((quarter, 1, inputs, lanes), index)

    whole = pl.BlockSpec((1, panel, panel), lambda k, c: (k, 0, 0))
    slots = [in_hbm(slot) for slot in slots[:3]] + list(slots[3:])
    return pl.pallas_call(
        functools.partial(far_kernel, by_row),
        out_shape=[pltpu.HBM((size, panel, panel), BF16)] * 2,
        grid_spec=pltpu.PrefetchScalarGridSpec(
            num_scalar_prefetch=1,
            grid=(size,),
            in_specs=[data(fixed)] * 3
            + [data(fixed_half)] * 2
            + [data(other)] * 3
            + [data(other_half)] * 2
            + [ANY] * len(after),
            out_specs=[whole, whole],
        ),
        compiler_params=limit(62),
        cost_estimate=cost(0.1),
    )(place, *slots, *slots, *after)


def formed(parts, lanes):
    beams = parts.shape[0] // 2
    values = []
    low = lax.broadcasted_iota(jnp.int32, (beams, lanes), 1) < lanes // 2
    for s in range(parts.shape[1] // lanes):
        piece = parts[:, s * lanes : (s + 1) * lanes]
        turned = pltpu.roll(piece[beams:], lanes // 2, axis=1)
        value = piece[:beams] + jnp.where(low, -turned, turned)
        values.append(value * value)
    return jnp.concatenate(values, axis=1) if len(values) > 1 else values[0]


def pooled(power, lanes, bins, sources):
    width = power.shape[1]
    pools = []
    for source in sources:
        lane = lax.broadcasted_iota(jnp.int32, (bins, lanes), 1)
        place = lax.broadcasted_iota(jnp.int32, (bins, lanes), 0)
        wanted = source * (lanes // 2 // INTEG) + lax.rem(lane, lanes // 2) // INTEG
        pools.append(jnp.where(place == wanted, 1.0 / INTEG, 0.0).astype(BF16))
    pool = jnp.concatenate(pools, axis=1) if len(pools) > 1 else pools[0]
    high = power.astype(BF16)
    rest = power - high.astype(F32)
    middle = rest.astype(BF16)
    low = (rest - middle.astype(F32)).astype(BF16)
    total = jnp.zeros((bins, power.shape[0]), F32)
    for term in (low, middle, high):
        total = total + lax.dot_general(
            pool, term, (((1,), (1,)), ((), ())), preferred_element_type=F32
        )
    return total


def near_kernel(by_row, first, place_ref, own_ref, prev_ref, next_ref, low_ref, high_ref, *refs):
    fixed, ring = place_ref[0], place_ref[1]
    if by_row:
        out_ref, up_ref, down_ref, x_ref = refs[-4:]
    else:
        w_hbm = refs[0]
        out_ref, up_ref, down_ref, beam_ref, x_ref, w_ref, sem = refs[-7:]
        k = pl.program_id(0)
        copy = pltpu.make_async_copy(w_hbm.at[:, first : first + w_ref.shape[1]], w_ref, sem)

        @pl.when(k == 0)
        def _():
            copy.start()

    blocks, _, inputs, lanes = own_ref.shape
    half = blocks // 2 * inputs
    total = blocks * inputs
    panel = total // 4
    for s, ref in enumerate((own_ref, prev_ref, next_ref)):
        x_ref[:, s * lanes : (s + 1) * lanes] = ref[:, 0].reshape(total, lanes)
    x_ref[:half, 3 * lanes :] = low_ref[:, 0].reshape(half, lanes)
    x_ref[half:, 3 * lanes :] = high_ref[:, 0].reshape(half, lanes)

    def panel_of(index):
        return x_ref[pl.ds(pl.multiple_of(index * panel, panel), panel), :]

    stack = stacked(by_row, panel_of(fixed), lanes)
    for step, ref in ((1, up_ref), (3, down_ref), (0, out_ref)):
        re, im = correlated(by_row, panel_of(lax.rem(ring + step, 4)), stack)
        ref[0, 0] = re.astype(ref.dtype)
        ref[1, 0] = im.astype(ref.dtype)
    if by_row:
        return

    @pl.when(k == 0)
    def _():
        copy.wait()

    beams = w_ref.shape[2]
    weights = w_ref[:, k].reshape(2 * beams, total)
    parts = lax.dot_general(
        weights, x_ref[...], (((1,), (0,)), ((), ())), preferred_element_type=F32
    )
    bins = lanes // 2 // INTEG
    sources = [lax.rem(fixed + shift, 4) for shift in (0, 3, 1, 2)]
    beam_ref[0] = pooled(formed(parts, lanes), lanes, 4 * bins, sources)


def near_products(place, slots, by_row, first=0, weights=None, after=()):
    blocks, size, inputs, lanes = slots[0].shape
    total = blocks * inputs
    panel = total // 4

    def data(count):
        return pl.BlockSpec((count, 1, inputs, lanes), lambda k, c: (0, k, 0, 0))

    block = pl.BlockSpec((2, 1, panel, panel), lambda k, c: (0, k, 0, 0))
    shape = (2, size, panel, panel)
    shapes = [pltpu.HBM(shape, F32), pltpu.HBM(shape, BF16), pltpu.HBM(shape, BF16)]
    specs = [block] * 3
    args = [in_hbm(slot) for slot in slots[:3]] + list(slots[3:])
    scratch = [pltpu.VMEM((total, 4 * lanes), BF16)]
    if not by_row:
        beams = weights.shape[2]
        bins = 4 * (lanes // 2 // INTEG)
        shapes.append(jax.ShapeDtypeStruct((size, bins, beams), F32))
        specs.append(pl.BlockSpec((1, bins, beams), lambda k, c: (k, 0, 0)))
        args.append(in_hbm(weights))
        scratch += [pltpu.VMEM((2, size) + weights.shape[2:], BF16), pltpu.SemaphoreType.DMA]
    args += after
    return pl.pallas_call(
        functools.partial(near_kernel, by_row, first),
        out_shape=shapes,
        grid_spec=pltpu.PrefetchScalarGridSpec(
            num_scalar_prefetch=1,
            grid=(size,),
            in_specs=[data(blocks)] * 3 + [data(blocks // 2)] * 2 + [ANY] * (len(args) - 5),
            out_specs=specs,
            scratch_shapes=scratch,
        ),
        compiler_params=limit(62),
        cost_estimate=cost(0.1),
    )(place, *args)


def beam_kernel(own_ref, w_ref, *refs):
    out_ref = refs[-1]
    blocks, _, inputs, lanes = own_ref.shape
    owners, _, _, beams, total = w_ref.shape
    x = own_ref[:, 0].reshape(blocks * inputs, lanes)
    weights = jnp.concatenate(
        [w_ref[:, part, 0].reshape(owners * beams, total) for part in range(2)], axis=0
    )
    parts = lax.dot_general(weights, x, (((1,), (0,)), ((), ())), preferred_element_type=F32)
    power = pooled(formed(parts, lanes), lanes, lanes // 2 // INTEG, [0])
    for owner in range(owners):
        out_ref[owner, 0] = power[:, owner * beams : (owner + 1) * beams]


def own_beams(own, weights, after):
    blocks, size, inputs, lanes = own.shape
    owners, _, _, beams, total = weights.shape
    bins = lanes // 2 // INTEG
    return pl.pallas_call(
        beam_kernel,
        out_shape=jax.ShapeDtypeStruct((owners, size, bins, beams), F32),
        grid=(size,),
        in_specs=[
            pl.BlockSpec((blocks, 1, inputs, lanes), lambda k: (0, k, 0, 0)),
            pl.BlockSpec((owners, 2, 1, beams, total), lambda k: (0, 0, k, 0, 0)),
        ]
        + [ANY] * len(after),
        out_specs=pl.BlockSpec((owners, 1, bins, beams), lambda k: (0, k, 0, 0)),
        compiler_params=limit(62),
        cost_estimate=cost(0.1),
    )(in_hbm(own), in_hbm(weights), *after)


def add_kernel(up_ref, down_ref, low_ref, high_ref, *refs):
    up_out, down_out = refs[-2:]
    up_out[0] = (up_ref[0].astype(F32) + low_ref[...].astype(F32)).astype(BF16)
    down_out[0] = (down_ref[0].astype(F32) + high_ref[...].astype(F32)).astype(BF16)


def added(up, down, low, high, after=()):
    _, size, panel, _ = up.shape
    real = pl.BlockSpec((1, size, panel, panel), lambda n: (0, 0, 0, 0))
    imag = pl.BlockSpec((1, size, panel, panel), lambda n: (1, 0, 0, 0))
    one = pl.BlockSpec((size, panel, panel), lambda n: (0, 0, 0))
    shape = pltpu.HBM(up.shape, BF16)
    return pl.pallas_call(
        add_kernel,
        out_shape=[shape, shape],
        grid=(1,),
        in_specs=[real, imag, one, one] + [ANY] * len(after),
        out_specs=[real, imag],
        input_output_aliases={0: 0, 1: 1},
        compiler_params=limit(62),
        cost_estimate=cost(0.1),
    )(up, down, low, high, *after)


def final_kernel(first, own_ref, prev_ref, next_ref, *refs):
    out_hbm, held, sems = refs[-3:]
    size = own_ref.shape[1]
    p = pl.program_id(0)

    def copy(part):
        return pltpu.make_async_copy(
            held.at[part], out_hbm.at[part, first : first + size], sems.at[part]
        )

    for part in range(2):

        @pl.when(p == part)
        def _(part=part):
            held[part] = own_ref[0] + prev_ref[0].astype(F32) + next_ref[0].astype(F32)
            copy(part).start()

    @pl.when(p == 1)
    def _():
        copy(0).wait()
        copy(1).wait()


def finished(own, from_prev, from_next, first, channels, out):
    _, size, panel, _ = own.shape
    block = pl.BlockSpec((1, size, panel, panel), lambda p: (p, 0, 0, 0))
    extra = [] if out is None else [out]
    return pl.pallas_call(
        functools.partial(final_kernel, first),
        out_shape=jax.ShapeDtypeStruct((2, channels, panel, panel), F32),
        grid=(2,),
        in_specs=[block] * 3 + [ANY] * len(extra),
        out_specs=HBM,
        input_output_aliases={3: 0} if extra else {},
        scratch_shapes=[
            pltpu.VMEM((2, size, panel, panel), F32),
            pltpu.SemaphoreType.DMA((2,)),
        ],
        compiler_params=limit(62),
        cost_estimate=cost(0.1),
    )(in_hbm(own), from_prev, from_next, *extra)


def along(value, axis, step):
    count = lax.axis_size(axis)
    return lax.ppermute(value, axis, [(i, (i + step) % count) for i in range(count)])


def both_ways(up, down, axis):
    return along(up, axis, 1), along(down, axis, -1)


def on_device(voltages, input_flags, channel_order, beam_weights):
    size_b, size_a = CHUNKS
    channels = size_a + size_b
    history = passed_along(voltages[:, :, voltages.shape[2] - (TAPS - 1) * NCH :], ("row", "col"), 1)
    row = lax.axis_index("row").astype(jnp.int32)
    col = lax.axis_index("col").astype(jnp.int32)
    place_a = jnp.stack([col, row])
    place_b = jnp.stack([row, col])
    weights = lax.all_gather(beam_weights, "col", axis=0)
    piece_b, piece_a = spectra(voltages, history, input_flags, channel_order, CHUNKS)

    def turn(piece, axis):
        return lax.all_to_all(piece, axis, split_axis=0, concat_axis=0, tiled=True)

    own_b = turn(piece_b, "chan")
    near_b = both_ways(own_b, own_b, "row")
    own_a = turn(piece_a, "chan")
    near_a = both_ways(own_a, own_a, "col")
    half_b = halves(*near_b, [own_a])
    far_b = both_ways(*half_b, "row")
    beam_b = own_beams(own_b, weights, half_b[:1])
    slots_b = (own_b, *near_b, *far_b)
    re_b, im_b = far_products(place_b, slots_b, True, [beam_b])
    got_b = both_ways(re_b, im_b, "col")
    half_a = halves(*near_a, [re_b])
    far_a = both_ways(*half_a, "col")
    slots_a = (own_a, *near_a, *far_a)
    mine_b, up_b, down_b = near_products(place_b, slots_b, True, after=[half_a[0]])
    sum_b = added(up_b, down_b, *got_b)
    sent_b = both_ways(*sum_b, "col")
    re_a, im_a = far_products(place_a, slots_a, False, [sum_b[0]])
    got_a = both_ways(re_a, im_a, "row")
    mine_a, up_a, down_a, power_a = near_products(place_a, slots_a, False, size_b, beam_weights)
    sum_a = added(up_a, down_a, *got_a)
    sent_a = both_ways(*sum_a, "row")

    power_b = jnp.transpose(turn(beam_b, "col"), (1, 0, 2, 3)).reshape(size_b, -1, beam_b.shape[3])
    out = finished(mine_b, *sent_b, 0, channels, None)
    visibility = finished(mine_a, *sent_a, size_b, channels, out)
    power = jnp.concatenate([power_b, power_a], axis=0)
    return (visibility, jnp.transpose(power, (0, 2, 1)))


def solution(mesh):
    placed = (P(None, "chan", ("row", "col")), P("chan"), P(), P(None, "chan", "col", None))
    return jax.shard_map(
        on_device,
        mesh=mesh,
        in_specs=placed,
        out_specs=(P(None, "chan", "row", "col"), P("chan", "col", "row")),
        check_vma=False,
    )
```

```python
import functools
import math

import jax
import jax.numpy as jnp
import numpy as np
from jax import lax
from jax.experimental import pallas as pl
from jax.experimental.pallas import tpu as pltpu
from jax.sharding import PartitionSpec as P

NCH = 128
TAPS = 4
INTEG = 8
CHUNKS = (5, 3)

F32 = jnp.float32
BF16 = jnp.bfloat16
VMEM = pl.BlockSpec(memory_space=pltpu.VMEM)
SMEM = pl.BlockSpec(memory_space=pltpu.SMEM)
ANY = pl.BlockSpec(memory_space=pl.ANY)
HBM = pl.BlockSpec(memory_space=pltpu.HBM)


def cost(micros):
    return pl.CostEstimate(flops=int(micros * 1.1e9), bytes_accessed=1, transcendentals=0)


def in_hbm(value):
    return pltpu.with_memory_space_constraint(value, pltpu.HBM)


def limit(mebibytes):
    return pltpu.CompilerParams(vmem_limit_bytes=mebibytes * 2**20)


def prototype(taps, length):
    position = np.arange(taps * length, dtype=np.float32) + np.float32(0.5)
    offset = position / np.float32(length) - np.float32(taps / 2.0)
    window = 0.5 - 0.5 * np.cos(2.0 * math.pi * position.astype(np.float64) / (taps * length))
    sinc = np.sin(math.pi * offset.astype(np.float64)) / (math.pi * offset.astype(np.float64))
    return (sinc * window).astype(np.float32).reshape(taps, length)


def dft_table(length):
    index = np.arange(length)
    angle = 2.0 * math.pi / length * (index[:, None] * index[None, :] % length)
    factor = 1.0 / math.sqrt(length)
    table = np.concatenate([np.cos(angle) * factor, np.sin(angle) * factor], axis=1)
    return table.astype(np.float32).astype(jnp.bfloat16)


def passed_along(value, axis, steps):
    count = lax.axis_size(axis)
    initial, last = (max(0, -steps), min(count, count - steps))
    return lax.ppermute(value, axis, [(source, source + steps) for source in range(initial, last)])


def flag_column(flags, inputs):
    eye = lax.broadcasted_iota(jnp.int32, (inputs, inputs), 0) == lax.broadcasted_iota(
        jnp.int32, (inputs, inputs), 1
    )
    held = jnp.where(eye, flags.astype(F32), 0.0)
    return jnp.broadcast_to(jnp.sum(held, axis=1, keepdims=True), (inputs, NCH))


def filter_kernel(v_hbm, flags_hbm, coeff_hbm, filt_ref, v_ref, flags_ref, coeff_ref, sems):
    copies = [
        pltpu.make_async_copy(src, dst, sems.at[n])
        for n, (src, dst) in enumerate(
            ((v_hbm, v_ref), (flags_hbm, flags_ref), (coeff_hbm, coeff_ref))
        )
    ]
    for copy in copies:
        copy.start()
    for copy in copies:
        copy.wait()
    inputs = v_ref.shape[1]
    frames = v_ref.shape[2] // NCH
    mask = flag_column(flags_ref[...], inputs)
    taps = [jnp.broadcast_to(coeff_ref[t : t + 1, :], (inputs, NCH)) * mask for t in range(TAPS)]
    for part in range(2):

        def frame_step(f, past, part=part):
            lanes = pl.ds(pl.multiple_of(f * NCH, NCH), NCH)
            window = past + (v_ref[part, :, lanes].astype(F32),)
            total = taps[0] * window[0]
            for t in range(1, TAPS):
                total = total + taps[t] * window[t]
            filt_ref[part, pl.ds(f, inputs, stride=frames), :] = total
            return window[1:]

        zero = v_ref[part, :, :NCH].astype(F32) * 0.0
        lax.fori_loop(0, frames, frame_step, (zero,) * (TAPS - 1), unroll=8)


def spectrum_kernel(chunks, filt_ref, halo_ref, flags_hbm, order_hbm, coeff_hbm, table_hbm, *rest):
    outs = rest[: len(chunks)]
    flags_ref, order_ref, coeff_ref, table_ref, corr_ref, spec_ref, sems = rest[len(chunks) :]
    copies = [
        pltpu.make_async_copy(src, dst, sems.at[n])
        for n, (src, dst) in enumerate(
            (
                (flags_hbm, flags_ref),
                (order_hbm, order_ref),
                (coeff_hbm, coeff_ref),
                (table_hbm, table_ref),
            )
        )
    ]
    for copy in copies:
        copy.start()
    for copy in copies:
        copy.wait()
    inputs = halo_ref.shape[1]
    frames = filt_ref.shape[1] // inputs
    rows = 8
    mask = flag_column(flags_ref[...], inputs)
    taps = [jnp.broadcast_to(coeff_ref[t : t + 1, :], (inputs, NCH)) * mask for t in range(TAPS)]
    for part in range(2):
        past = [halo_ref[part, :, t * NCH : (t + 1) * NCH].astype(F32) for t in range(TAPS - 1)]
        for f in range(rows):
            total = jnp.zeros((inputs, NCH), F32)
            for t in range(TAPS - 1 - f):
                total = total + taps[t] * past[f + t]
            corr_ref[part, pl.ds(f, inputs, stride=rows), :] = total
    onehot = lax.broadcasted_iota(jnp.int32, (NCH, NCH), 0) == jnp.broadcast_to(
        order_ref[...], (NCH, NCH)
    )
    table = lax.dot_general(
        onehot.astype(BF16), table_ref[...], (((0,), (0,)), ((), ())), preferred_element_type=F32
    ).astype(BF16)

    def input_step(pair, carry):
        blocks = []
        for which in range(2):
            i = pair * 2 + which
            both = []
            for part in range(2):
                block = filt_ref[part, pl.ds(pl.multiple_of(i * frames, frames), frames), :]
                extra = corr_ref[part, pl.ds(pl.multiple_of(i * rows, rows), rows), :]
                both.append(jnp.concatenate([block[:rows] + extra, block[rows:]], axis=0).astype(BF16))
            re, im = both
            blocks.append(jnp.concatenate([re, im], axis=1))
            blocks.append(jnp.concatenate([im, -re], axis=1))
        right = jnp.concatenate(blocks, axis=0)
        result = lax.dot_general(
            table, right, (((1,), (1,)), ((), ())), preferred_element_type=F32
        )
        for which in range(2):
            spec_ref[pl.ds(pair * 2 + which, NCH, stride=inputs), :] = result[
                :, which * NCH : (which + 1) * NCH
            ]
        return carry

    lax.fori_loop(0, inputs // 2, input_step, 0, unroll=4)
    per_block = sum(chunks)

    def copy_step(block, carry):
        first = 0
        for out, size in zip(outs, chunks):
            for k in range(size):
                at = pl.multiple_of((block * per_block + first + k) * inputs, inputs)
                out[block, k] = spec_ref[pl.ds(at, inputs), :].astype(BF16)
            first += size
        return carry

    lax.fori_loop(0, NCH // per_block, copy_step, 0)


def spectra(voltages, history, flags, order, chunks):
    inputs = voltages.shape[1]
    frames = voltages.shape[2] // NCH
    flags = flags.reshape(1, inputs)
    coeff = jnp.asarray(prototype(TAPS, NCH))
    filtered = pl.pallas_call(
        filter_kernel,
        out_shape=jax.ShapeDtypeStruct((2, inputs * frames, NCH), F32),
        in_specs=[HBM] * 3,
        out_specs=VMEM,
        scratch_shapes=[
            pltpu.VMEM(voltages.shape, BF16),
            pltpu.VMEM((1, inputs), jnp.int32),
            pltpu.VMEM((TAPS, NCH), F32),
            pltpu.SemaphoreType.DMA((3,)),
        ],
        compiler_params=limit(16),
        cost_estimate=cost(5),
    )(in_hbm(voltages), in_hbm(flags), in_hbm(coeff))
    blocks = NCH // sum(chunks)
    return pl.pallas_call(
        functools.partial(spectrum_kernel, chunks),
        out_shape=[jax.ShapeDtypeStruct((blocks, size, inputs, 2 * frames), BF16) for size in chunks],
        in_specs=[VMEM, VMEM] + [HBM] * 4,
        out_specs=[VMEM] * len(chunks),
        scratch_shapes=[
            pltpu.VMEM((1, inputs), jnp.int32),
            pltpu.VMEM((1, NCH), jnp.int32),
            pltpu.VMEM((TAPS, NCH), F32),
            pltpu.VMEM((NCH, 2 * NCH), BF16),
            pltpu.VMEM((2, inputs * 8, NCH), F32),
            pltpu.VMEM((NCH * inputs, 2 * frames), F32),
            pltpu.SemaphoreType.DMA((4,)),
        ],
        compiler_params=limit(16),
        cost_estimate=cost(6),
    )(
        filtered,
        history,
        *[in_hbm(x) for x in (flags, order.reshape(1, NCH), coeff, jnp.asarray(dft_table(NCH)))],
    )


def halves_kernel(low_ref, high_ref, *refs):
    low_out, high_out = refs[-2:]
    low_out[...] = low_ref[...]
    high_out[...] = high_ref[...]


def halves(low, high, after=()):
    blocks = low.shape[0] // 2
    block = (blocks // 2,) + low.shape[1:]
    first = pl.BlockSpec(block, lambda n: (n, 0, 0, 0))
    second = pl.BlockSpec(block, lambda n: (2 + n, 0, 0, 0))
    return pl.pallas_call(
        halves_kernel,
        out_shape=[pltpu.HBM((blocks,) + low.shape[1:], BF16)] * 2,
        grid=(2,),
        in_specs=[first, second] + [ANY] * len(after),
        out_specs=[first, first],
        compiler_params=limit(62),
        cost_estimate=cost(0.1),
    )(low, high, *after)


def turned_panel(panel, lanes, low_sign):
    first = lax.broadcasted_iota(jnp.int32, (panel.shape[0], lanes), 1) < lanes // 2
    parts = []
    for s in range(panel.shape[1] // lanes):
        part = pltpu.roll(panel[:, s * lanes : (s + 1) * lanes].astype(F32), lanes // 2, axis=1)
        parts.append(jnp.where(first, low_sign * part, -low_sign * part).astype(BF16))
    return jnp.concatenate(parts, axis=1)


def correlated(by_row, moving, fixed):
    panel = moving.shape[0]
    left, right = (fixed, moving) if by_row else (moving, fixed)
    result = lax.dot_general(
        left, right, (((1,), (1,)), ((), ())), preferred_element_type=F32
    ) * (1.0 / (NCH * 8))
    if by_row:
        return result[:panel], result[panel:]
    return result[:, :panel], result[:, panel:]


def stacked(by_row, panel, lanes):
    return jnp.concatenate([panel, turned_panel(panel, lanes, 1.0 if by_row else -1.0)], axis=0)


def far_kernel(by_row, place_ref, *refs):
    re_ref, im_ref = refs[-2:]
    lanes = refs[0].shape[3]

    def panel(parts, index):
        near = [part[:, 0].reshape(-1, lanes) for part in parts[:3]]
        low, high = [part[:, 0].reshape(-1, lanes) for part in parts[3:]]
        return jnp.concatenate(near + [jnp.where(index < 2, low, high)], axis=1)

    mine = panel(refs[:5], place_ref[0])
    other = panel(refs[5:10], lax.rem(place_ref[1] + 2, 4))
    re, im = correlated(by_row, other, stacked(by_row, mine, lanes))
    re_ref[0] = re.astype(BF16)
    im_ref[0] = im.astype(BF16)


def far_products(place, slots, by_row, after=()):
    own = slots[0]
    blocks, size, inputs, lanes = own.shape
    quarter = blocks // 4
    panel = quarter * inputs

    def fixed(k, c):
        return (c[0], k, 0, 0)

    def fixed_half(k, c):
        return (lax.rem(c[0], 2), k, 0, 0)

    def other(k, c):
        return (lax.rem(c[1] + 2, 4), k, 0, 0)

    def other_half(k, c):
        return (lax.rem(c[1], 2), k, 0, 0)

    def data(index):
        return pl.BlockSpec((quarter, 1, inputs, lanes), index)

    whole = pl.BlockSpec((1, panel, panel), lambda k, c: (k, 0, 0))
    slots = [in_hbm(slot) for slot in slots[:3]] + list(slots[3:])
    return pl.pallas_call(
        functools.partial(far_kernel, by_row),
        out_shape=[pltpu.HBM((size, panel, panel), BF16)] * 2,
        grid_spec=pltpu.PrefetchScalarGridSpec(
            num_scalar_prefetch=1,
            grid=(size,),
            in_specs=[data(fixed)] * 3
            + [data(fixed_half)] * 2
            + [data(other)] * 3
            + [data(other_half)] * 2
            + [ANY] * len(after),
            out_specs=[whole, whole],
        ),
        compiler_params=limit(62),
        cost_estimate=cost(0.1),
    )(place, *slots, *slots, *after)


def formed(parts, lanes):
    beams = parts.shape[0] // 2
    values = []
    low = lax.broadcasted_iota(jnp.int32, (beams, lanes), 1) < lanes // 2
    for s in range(parts.shape[1] // lanes):
        piece = parts[:, s * lanes : (s + 1) * lanes]
        turned = pltpu.roll(piece[beams:], lanes // 2, axis=1)
        value = piece[:beams] + jnp.where(low, -turned, turned)
        values.append(value * value)
    return jnp.concatenate(values, axis=1) if len(values) > 1 else values[0]


def pooled(power, lanes, bins, sources):
    width = power.shape[1]
    pools = []
    for source in sources:
        lane = lax.broadcasted_iota(jnp.int32, (bins, lanes), 1)
        place = lax.broadcasted_iota(jnp.int32, (bins, lanes), 0)
        wanted = source * (lanes // 2 // INTEG) + lax.rem(lane, lanes // 2) // INTEG
        pools.append(jnp.where(place == wanted, 1.0 / INTEG, 0.0).astype(BF16))
    pool = jnp.concatenate(pools, axis=1) if len(pools) > 1 else pools[0]
    high = power.astype(BF16)
    rest = power - high.astype(F32)
    middle = rest.astype(BF16)
    low = (rest - middle.astype(F32)).astype(BF16)
    total = jnp.zeros((bins, power.shape[0]), F32)
    for term in (low, middle, high):
        total = total + lax.dot_general(
            pool, term, (((1,), (1,)), ((), ())), preferred_element_type=F32
        )
    return total


def near_kernel(by_row, first, place_ref, own_ref, prev_ref, next_ref, low_ref, high_ref, *refs):
    fixed, ring = place_ref[0], place_ref[1]
    if by_row:
        out_ref, up_ref, down_ref, x_ref = refs[-4:]
    else:
        w_hbm = refs[0]
        out_ref, up_ref, down_ref, beam_ref, x_ref, w_ref, sem = refs[-7:]
        k = pl.program_id(0)
        copy = pltpu.make_async_copy(w_hbm.at[:, first : first + w_ref.shape[1]], w_ref, sem)

        @pl.when(k == 0)
        def _():
            copy.start()

    blocks, _, inputs, lanes = own_ref.shape
    half = blocks // 2 * inputs
    total = blocks * inputs
    panel = total // 4
    for s, ref in enumerate((own_ref, prev_ref, next_ref)):
        x_ref[:, s * lanes : (s + 1) * lanes] = ref[:, 0].reshape(total, lanes)
    x_ref[:half, 3 * lanes :] = low_ref[:, 0].reshape(half, lanes)
    x_ref[half:, 3 * lanes :] = high_ref[:, 0].reshape(half, lanes)

    def panel_of(index):
        return x_ref[pl.ds(pl.multiple_of(index * panel, panel), panel), :]

    stack = stacked(by_row, panel_of(fixed), lanes)
    for step, ref in ((1, up_ref), (3, down_ref), (0, out_ref)):
        re, im = correlated(by_row, panel_of(lax.rem(ring + step, 4)), stack)
        ref[0, 0] = re.astype(ref.dtype)
        ref[1, 0] = im.astype(ref.dtype)
    if by_row:
        return

    @pl.when(k == 0)
    def _():
        copy.wait()

    beams = w_ref.shape[2]
    weights = w_ref[:, k].reshape(2 * beams, total)
    parts = lax.dot_general(
        weights, x_ref[...], (((1,), (0,)), ((), ())), preferred_element_type=F32
    )
    bins = lanes // 2 // INTEG
    sources = [lax.rem(fixed + shift, 4) for shift in (0, 3, 1, 2)]
    beam_ref[0] = pooled(formed(parts, lanes), lanes, 4 * bins, sources)


def near_products(place, slots, by_row, first=0, weights=None, after=()):
    blocks, size, inputs, lanes = slots[0].shape
    total = blocks * inputs
    panel = total // 4

    def data(count):
        return pl.BlockSpec((count, 1, inputs, lanes), lambda k, c: (0, k, 0, 0))

    block = pl.BlockSpec((2, 1, panel, panel), lambda k, c: (0, k, 0, 0))
    shape = (2, size, panel, panel)
    shapes = [pltpu.HBM(shape, F32), pltpu.HBM(shape, BF16), pltpu.HBM(shape, BF16)]
    specs = [block] * 3
    args = [in_hbm(slot) for slot in slots[:3]] + list(slots[3:])
    scratch = [pltpu.VMEM((total, 4 * lanes), BF16)]
    if not by_row:
        beams = weights.shape[2]
        bins = 4 * (lanes // 2 // INTEG)
        shapes.append(jax.ShapeDtypeStruct((size, bins, beams), F32))
        specs.append(pl.BlockSpec((1, bins, beams), lambda k, c: (k, 0, 0)))
        args.append(in_hbm(weights))
        scratch += [pltpu.VMEM((2, size) + weights.shape[2:], BF16), pltpu.SemaphoreType.DMA]
    args += after
    return pl.pallas_call(
        functools.partial(near_kernel, by_row, first),
        out_shape=shapes,
        grid_spec=pltpu.PrefetchScalarGridSpec(
            num_scalar_prefetch=1,
            grid=(size,),
            in_specs=[data(blocks)] * 3 + [data(blocks // 2)] * 2 + [ANY] * (len(args) - 5),
            out_specs=specs,
            scratch_shapes=scratch,
        ),
        compiler_params=limit(62),
        cost_estimate=cost(10 if by_row else 0.1),
    )(place, *args)


def beam_kernel(own_ref, w_ref, *refs):
    out_ref = refs[-1]
    blocks, _, inputs, lanes = own_ref.shape
    owners, _, _, beams, total = w_ref.shape
    x = own_ref[:, 0].reshape(blocks * inputs, lanes)
    weights = jnp.concatenate(
        [w_ref[:, part, 0].reshape(owners * beams, total) for part in range(2)], axis=0
    )
    parts = lax.dot_general(weights, x, (((1,), (0,)), ((), ())), preferred_element_type=F32)
    power = pooled(formed(parts, lanes), lanes, lanes // 2 // INTEG, [0])
    for owner in range(owners):
        out_ref[owner, 0] = power[:, owner * beams : (owner + 1) * beams]


def own_beams(own, weights, after):
    blocks, size, inputs, lanes = own.shape
    owners, _, _, beams, total = weights.shape
    bins = lanes // 2 // INTEG
    return pl.pallas_call(
        beam_kernel,
        out_shape=jax.ShapeDtypeStruct((owners, size, bins, beams), F32),
        grid=(size,),
        in_specs=[
            pl.BlockSpec((blocks, 1, inputs, lanes), lambda k: (0, k, 0, 0)),
            pl.BlockSpec((owners, 2, 1, beams, total), lambda k: (0, 0, k, 0, 0)),
        ]
        + [ANY] * len(after),
        out_specs=pl.BlockSpec((owners, 1, bins, beams), lambda k: (0, k, 0, 0)),
        compiler_params=limit(62),
        cost_estimate=cost(0.1),
    )(in_hbm(own), in_hbm(weights), *after)


def add_kernel(up_ref, down_ref, low_ref, high_ref, *refs):
    up_out, down_out = refs[-2:]
    up_out[0] = (up_ref[0].astype(F32) + low_ref[...].astype(F32)).astype(BF16)
    down_out[0] = (down_ref[0].astype(F32) + high_ref[...].astype(F32)).astype(BF16)


def added(up, down, low, high, micros):
    _, size, panel, _ = up.shape
    real = pl.BlockSpec((1, size, panel, panel), lambda n: (0, 0, 0, 0))
    imag = pl.BlockSpec((1, size, panel, panel), lambda n: (1, 0, 0, 0))
    one = pl.BlockSpec((size, panel, panel), lambda n: (0, 0, 0))
    shape = pltpu.HBM(up.shape, BF16)
    return pl.pallas_call(
        add_kernel,
        out_shape=[shape, shape],
        grid=(1,),
        in_specs=[real, imag, one, one],
        out_specs=[real, imag],
        input_output_aliases={0: 0, 1: 1},
        compiler_params=limit(62),
        cost_estimate=cost(micros),
    )(up, down, low, high)


def final_kernel(first, own_ref, prev_ref, next_ref, *refs):
    out_hbm, held, sems = refs[-3:]
    size = own_ref.shape[1]
    p = pl.program_id(0)

    def copy(part):
        return pltpu.make_async_copy(
            held.at[part], out_hbm.at[part, first : first + size], sems.at[part]
        )

    for part in range(2):

        @pl.when(p == part)
        def _(part=part):
            held[part] = own_ref[0] + prev_ref[0].astype(F32) + next_ref[0].astype(F32)
            copy(part).start()

    @pl.when(p == 1)
    def _():
        copy(0).wait()
        copy(1).wait()


def finished(own, from_prev, from_next, first, channels, out):
    _, size, panel, _ = own.shape
    block = pl.BlockSpec((1, size, panel, panel), lambda p: (p, 0, 0, 0))
    extra = [] if out is None else [out]
    return pl.pallas_call(
        functools.partial(final_kernel, first),
        out_shape=jax.ShapeDtypeStruct((2, channels, panel, panel), F32),
        grid=(2,),
        in_specs=[block] * 3 + [ANY] * len(extra),
        out_specs=HBM,
        input_output_aliases={3: 0} if extra else {},
        scratch_shapes=[
            pltpu.VMEM((2, size, panel, panel), F32),
            pltpu.SemaphoreType.DMA((2,)),
        ],
        compiler_params=limit(62),
        cost_estimate=cost(0.1),
    )(in_hbm(own), from_prev, from_next, *extra)


def along(value, axis, step):
    count = lax.axis_size(axis)
    return lax.ppermute(value, axis, [(i, (i + step) % count) for i in range(count)])


def both_ways(up, down, axis):
    return along(up, axis, 1), along(down, axis, -1)


def on_device(voltages, input_flags, channel_order, beam_weights):
    size_b, size_a = CHUNKS
    channels = size_a + size_b
    history = passed_along(voltages[:, :, voltages.shape[2] - (TAPS - 1) * NCH :], ("row", "col"), 1)
    row = lax.axis_index("row").astype(jnp.int32)
    col = lax.axis_index("col").astype(jnp.int32)
    place_a = jnp.stack([col, row])
    place_b = jnp.stack([row, col])
    weights = lax.all_gather(beam_weights, "col", axis=0)
    piece_b, piece_a = spectra(voltages, history, input_flags, channel_order, CHUNKS)

    def turn(piece, axis):
        return lax.all_to_all(piece, axis, split_axis=0, concat_axis=0, tiled=True)

    own_b = turn(piece_b, "chan")
    near_b = both_ways(own_b, own_b, "row")
    own_a = turn(piece_a, "chan")
    near_a = both_ways(own_a, own_a, "col")
    half_b = halves(*near_b, [own_a])
    far_b = both_ways(*half_b, "row")
    beam_b = own_beams(own_b, weights, half_b[:1])
    half_a = halves(*near_a, [beam_b])
    far_a = both_ways(*half_a, "col")
    slots_b = (own_b, *near_b, *far_b)
    slots_a = (own_a, *near_a, *far_a)
    re_b, im_b = far_products(place_b, slots_b, True, [half_a[0]])
    got_b = both_ways(re_b, im_b, "col")
    re_a, im_a = far_products(place_a, slots_a, False, [re_b])
    got_a = both_ways(re_a, im_a, "row")
    mine_b, up_b, down_b = near_products(place_b, slots_b, True, after=[re_a])
    sum_b = added(up_b, down_b, *got_b, 0.1)
    sent_b = both_ways(*sum_b, "col")
    mine_a, up_a, down_a, power_a = near_products(
        place_a, slots_a, False, size_b, beam_weights, [sum_b[0]]
    )
    sum_a = added(up_a, down_a, *got_a, 20)
    sent_a = both_ways(*sum_a, "row")

    power_b = jnp.transpose(turn(beam_b, "col"), (1, 0, 2, 3)).reshape(size_b, -1, beam_b.shape[3])
    out = finished(mine_b, *sent_b, 0, channels, None)
    visibility = finished(mine_a, *sent_a, size_b, channels, out)
    power = jnp.concatenate([power_b, power_a], axis=0)
    return (visibility, jnp.transpose(power, (0, 2, 1)))


def solution(mesh):
    placed = (P(None, "chan", ("row", "col")), P("chan"), P(), P(None, "chan", "col", None))
    return jax.shard_map(
        on_device,
        mesh=mesh,
        in_specs=placed,
        out_specs=(P(None, "chan", "row", "col"), P("chan", "col", "row")),
        check_vma=False,
    )
```

```python
import functools
import math

import jax
import jax.numpy as jnp
import numpy as np
from jax import lax
from jax.experimental import pallas as pl
from jax.experimental.pallas import tpu as pltpu
from jax.sharding import PartitionSpec as P

NCH = 128
TAPS = 4
INTEG = 8
CHUNKS = (5, 3)

F32 = jnp.float32
BF16 = jnp.bfloat16
VMEM = pl.BlockSpec(memory_space=pltpu.VMEM)
SMEM = pl.BlockSpec(memory_space=pltpu.SMEM)
ANY = pl.BlockSpec(memory_space=pl.ANY)
HBM = pl.BlockSpec(memory_space=pltpu.HBM)


def cost(micros):
    return pl.CostEstimate(flops=int(micros * 1.1e9), bytes_accessed=1, transcendentals=0)


def in_hbm(value):
    return pltpu.with_memory_space_constraint(value, pltpu.HBM)


def limit(mebibytes):
    return pltpu.CompilerParams(vmem_limit_bytes=mebibytes * 2**20)


def prototype(taps, length):
    position = np.arange(taps * length, dtype=np.float32) + np.float32(0.5)
    offset = position / np.float32(length) - np.float32(taps / 2.0)
    window = 0.5 - 0.5 * np.cos(2.0 * math.pi * position.astype(np.float64) / (taps * length))
    sinc = np.sin(math.pi * offset.astype(np.float64)) / (math.pi * offset.astype(np.float64))
    return (sinc * window).astype(np.float32).reshape(taps, length)


def dft_table(length):
    index = np.arange(length)
    angle = 2.0 * math.pi / length * (index[:, None] * index[None, :] % length)
    factor = 1.0 / math.sqrt(length)
    table = np.concatenate([np.cos(angle) * factor, np.sin(angle) * factor], axis=1)
    return table.astype(np.float32).astype(jnp.bfloat16)


def passed_along(value, axis, steps):
    count = lax.axis_size(axis)
    initial, last = (max(0, -steps), min(count, count - steps))
    return lax.ppermute(value, axis, [(source, source + steps) for source in range(initial, last)])


def flag_column(flags, inputs):
    eye = lax.broadcasted_iota(jnp.int32, (inputs, inputs), 0) == lax.broadcasted_iota(
        jnp.int32, (inputs, inputs), 1
    )
    held = jnp.where(eye, flags.astype(F32), 0.0)
    return jnp.broadcast_to(jnp.sum(held, axis=1, keepdims=True), (inputs, NCH))


def filter_kernel(v_hbm, flags_hbm, coeff_hbm, filt_ref, v_ref, flags_ref, coeff_ref, sems):
    copies = [
        pltpu.make_async_copy(src, dst, sems.at[n])
        for n, (src, dst) in enumerate(
            ((v_hbm, v_ref), (flags_hbm, flags_ref), (coeff_hbm, coeff_ref))
        )
    ]
    for copy in copies:
        copy.start()
    for copy in copies:
        copy.wait()
    inputs = v_ref.shape[1]
    frames = v_ref.shape[2] // NCH
    mask = flag_column(flags_ref[...], inputs)
    taps = [jnp.broadcast_to(coeff_ref[t : t + 1, :], (inputs, NCH)) * mask for t in range(TAPS)]
    for part in range(2):

        def frame_step(f, past, part=part):
            lanes = pl.ds(pl.multiple_of(f * NCH, NCH), NCH)
            window = past + (v_ref[part, :, lanes].astype(F32),)
            total = taps[0] * window[0]
            for t in range(1, TAPS):
                total = total + taps[t] * window[t]
            filt_ref[part, pl.ds(f, inputs, stride=frames), :] = total
            return window[1:]

        zero = v_ref[part, :, :NCH].astype(F32) * 0.0
        lax.fori_loop(0, frames, frame_step, (zero,) * (TAPS - 1), unroll=8)


def spectrum_kernel(chunks, filt_ref, halo_ref, flags_hbm, order_hbm, coeff_hbm, table_hbm, *rest):
    outs = rest[: len(chunks)]
    flags_ref, order_ref, coeff_ref, table_ref, corr_ref, spec_ref, sems = rest[len(chunks) :]
    copies = [
        pltpu.make_async_copy(src, dst, sems.at[n])
        for n, (src, dst) in enumerate(
            (
                (flags_hbm, flags_ref),
                (order_hbm, order_ref),
                (coeff_hbm, coeff_ref),
                (table_hbm, table_ref),
            )
        )
    ]
    for copy in copies:
        copy.start()
    for copy in copies:
        copy.wait()
    inputs = halo_ref.shape[1]
    frames = filt_ref.shape[1] // inputs
    rows = 8
    mask = flag_column(flags_ref[...], inputs)
    taps = [jnp.broadcast_to(coeff_ref[t : t + 1, :], (inputs, NCH)) * mask for t in range(TAPS)]
    for part in range(2):
        past = [halo_ref[part, :, t * NCH : (t + 1) * NCH].astype(F32) for t in range(TAPS - 1)]
        for f in range(rows):
            total = jnp.zeros((inputs, NCH), F32)
            for t in range(TAPS - 1 - f):
                total = total + taps[t] * past[f + t]
            corr_ref[part, pl.ds(f, inputs, stride=rows), :] = total
    onehot = lax.broadcasted_iota(jnp.int32, (NCH, NCH), 0) == jnp.broadcast_to(
        order_ref[...], (NCH, NCH)
    )
    table = lax.dot_general(
        onehot.astype(BF16), table_ref[...], (((0,), (0,)), ((), ())), preferred_element_type=F32
    ).astype(BF16)

    def input_step(pair, carry):
        blocks = []
        for which in range(2):
            i = pair * 2 + which
            both = []
            for part in range(2):
                block = filt_ref[part, pl.ds(pl.multiple_of(i * frames, frames), frames), :]
                extra = corr_ref[part, pl.ds(pl.multiple_of(i * rows, rows), rows), :]
                both.append(jnp.concatenate([block[:rows] + extra, block[rows:]], axis=0).astype(BF16))
            re, im = both
            blocks.append(jnp.concatenate([re, im], axis=1))
            blocks.append(jnp.concatenate([im, -re], axis=1))
        right = jnp.concatenate(blocks, axis=0)
        result = lax.dot_general(
            table, right, (((1,), (1,)), ((), ())), preferred_element_type=F32
        )
        for which in range(2):
            spec_ref[pl.ds(pair * 2 + which, NCH, stride=inputs), :] = result[
                :, which * NCH : (which + 1) * NCH
            ]
        return carry

    lax.fori_loop(0, inputs // 2, input_step, 0, unroll=4)
    per_block = sum(chunks)

    def copy_step(block, carry):
        first = 0
        for out, size in zip(outs, chunks):
            for k in range(size):
                at = pl.multiple_of((block * per_block + first + k) * inputs, inputs)
                out[block, k] = spec_ref[pl.ds(at, inputs), :].astype(BF16)
            first += size
        return carry

    lax.fori_loop(0, NCH // per_block, copy_step, 0)


def spectra(voltages, history, flags, order, chunks):
    inputs = voltages.shape[1]
    frames = voltages.shape[2] // NCH
    flags = flags.reshape(1, inputs)
    coeff = jnp.asarray(prototype(TAPS, NCH))
    filtered = pl.pallas_call(
        filter_kernel,
        out_shape=jax.ShapeDtypeStruct((2, inputs * frames, NCH), F32),
        in_specs=[HBM] * 3,
        out_specs=VMEM,
        scratch_shapes=[
            pltpu.VMEM(voltages.shape, BF16),
            pltpu.VMEM((1, inputs), jnp.int32),
            pltpu.VMEM((TAPS, NCH), F32),
            pltpu.SemaphoreType.DMA((3,)),
        ],
        compiler_params=limit(16),
        cost_estimate=cost(5),
    )(in_hbm(voltages), in_hbm(flags), in_hbm(coeff))
    blocks = NCH // sum(chunks)
    return pl.pallas_call(
        functools.partial(spectrum_kernel, chunks),
        out_shape=[jax.ShapeDtypeStruct((blocks, size, inputs, 2 * frames), BF16) for size in chunks],
        in_specs=[VMEM, VMEM] + [HBM] * 4,
        out_specs=[VMEM] * len(chunks),
        scratch_shapes=[
            pltpu.VMEM((1, inputs), jnp.int32),
            pltpu.VMEM((1, NCH), jnp.int32),
            pltpu.VMEM((TAPS, NCH), F32),
            pltpu.VMEM((NCH, 2 * NCH), BF16),
            pltpu.VMEM((2, inputs * 8, NCH), F32),
            pltpu.VMEM((NCH * inputs, 2 * frames), F32),
            pltpu.SemaphoreType.DMA((4,)),
        ],
        compiler_params=limit(16),
        cost_estimate=cost(6),
    )(
        filtered,
        history,
        *[in_hbm(x) for x in (flags, order.reshape(1, NCH), coeff, jnp.asarray(dft_table(NCH)))],
    )


def halves_kernel(low_ref, high_ref, *refs):
    low_out, high_out = refs[-2:]
    low_out[...] = low_ref[...]
    high_out[...] = high_ref[...]


def halves(low, high, after=()):
    blocks = low.shape[0] // 2
    block = (blocks // 2,) + low.shape[1:]
    first = pl.BlockSpec(block, lambda n: (n, 0, 0, 0))
    second = pl.BlockSpec(block, lambda n: (2 + n, 0, 0, 0))
    return pl.pallas_call(
        halves_kernel,
        out_shape=[pltpu.HBM((blocks,) + low.shape[1:], BF16)] * 2,
        grid=(2,),
        in_specs=[first, second] + [ANY] * len(after),
        out_specs=[first, first],
        compiler_params=limit(62),
        cost_estimate=cost(0.1),
    )(low, high, *after)


def turned_panel(panel, lanes, low_sign):
    first = lax.broadcasted_iota(jnp.int32, (panel.shape[0], lanes), 1) < lanes // 2
    parts = []
    for s in range(panel.shape[1] // lanes):
        part = pltpu.roll(panel[:, s * lanes : (s + 1) * lanes].astype(F32), lanes // 2, axis=1)
        parts.append(jnp.where(first, low_sign * part, -low_sign * part).astype(BF16))
    return jnp.concatenate(parts, axis=1)


def correlated(by_row, moving, fixed):
    panel = moving.shape[0]
    left, right = (fixed, moving) if by_row else (moving, fixed)
    result = lax.dot_general(
        left, right, (((1,), (1,)), ((), ())), preferred_element_type=F32
    ) * (1.0 / (NCH * 8))
    if by_row:
        return result[:panel], result[panel:]
    return result[:, :panel], result[:, panel:]


def stacked(by_row, panel, lanes):
    return jnp.concatenate([panel, turned_panel(panel, lanes, 1.0 if by_row else -1.0)], axis=0)


def far_kernel(by_row, place_ref, *refs):
    re_ref, im_ref = refs[-2:]
    lanes = refs[0].shape[3]

    def panel(parts, index):
        near = [part[:, 0].reshape(-1, lanes) for part in parts[:3]]
        low, high = [part[:, 0].reshape(-1, lanes) for part in parts[3:]]
        return jnp.concatenate(near + [jnp.where(index < 2, low, high)], axis=1)

    mine = panel(refs[:5], place_ref[0])
    other = panel(refs[5:10], lax.rem(place_ref[1] + 2, 4))
    re, im = correlated(by_row, other, stacked(by_row, mine, lanes))
    re_ref[0] = re.astype(BF16)
    im_ref[0] = im.astype(BF16)


def far_products(place, slots, by_row, after=()):
    own = slots[0]
    blocks, size, inputs, lanes = own.shape
    quarter = blocks // 4
    panel = quarter * inputs

    def fixed(k, c):
        return (c[0], k, 0, 0)

    def fixed_half(k, c):
        return (lax.rem(c[0], 2), k, 0, 0)

    def other(k, c):
        return (lax.rem(c[1] + 2, 4), k, 0, 0)

    def other_half(k, c):
        return (lax.rem(c[1], 2), k, 0, 0)

    def data(index):
        return pl.BlockSpec((quarter, 1, inputs, lanes), index)

    whole = pl.BlockSpec((1, panel, panel), lambda k, c: (k, 0, 0))
    slots = [in_hbm(slot) for slot in slots[:3]] + list(slots[3:])
    return pl.pallas_call(
        functools.partial(far_kernel, by_row),
        out_shape=[pltpu.HBM((size, panel, panel), BF16)] * 2,
        grid_spec=pltpu.PrefetchScalarGridSpec(
            num_scalar_prefetch=1,
            grid=(size,),
            in_specs=[data(fixed)] * 3
            + [data(fixed_half)] * 2
            + [data(other)] * 3
            + [data(other_half)] * 2
            + [ANY] * len(after),
            out_specs=[whole, whole],
        ),
        compiler_params=limit(62),
        cost_estimate=cost(0.1),
    )(place, *slots, *slots, *after)


def formed(parts, lanes):
    beams = parts.shape[0] // 2
    values = []
    low = lax.broadcasted_iota(jnp.int32, (beams, lanes), 1) < lanes // 2
    for s in range(parts.shape[1] // lanes):
        piece = parts[:, s * lanes : (s + 1) * lanes]
        turned = pltpu.roll(piece[beams:], lanes // 2, axis=1)
        value = piece[:beams] + jnp.where(low, -turned, turned)
        values.append(value * value)
    return jnp.concatenate(values, axis=1) if len(values) > 1 else values[0]


def pooled(power, lanes, bins, sources):
    width = power.shape[1]
    pools = []
    for source in sources:
        lane = lax.broadcasted_iota(jnp.int32, (bins, lanes), 1)
        place = lax.broadcasted_iota(jnp.int32, (bins, lanes), 0)
        wanted = source * (lanes // 2 // INTEG) + lax.rem(lane, lanes // 2) // INTEG
        pools.append(jnp.where(place == wanted, 1.0 / INTEG, 0.0).astype(BF16))
    pool = jnp.concatenate(pools, axis=1) if len(pools) > 1 else pools[0]
    high = power.astype(BF16)
    rest = power - high.astype(F32)
    middle = rest.astype(BF16)
    low = (rest - middle.astype(F32)).astype(BF16)
    total = jnp.zeros((bins, power.shape[0]), F32)
    for term in (low, middle, high):
        total = total + lax.dot_general(
            pool, term, (((1,), (1,)), ((), ())), preferred_element_type=F32
        )
    return total


def near_kernel(by_row, first, place_ref, own_ref, prev_ref, next_ref, low_ref, high_ref, *refs):
    fixed, ring = place_ref[0], place_ref[1]
    if by_row:
        out_ref, up_ref, down_ref, x_ref = refs[-4:]
    else:
        w_hbm = refs[0]
        out_ref, up_ref, down_ref, beam_ref, x_ref, w_ref, sem = refs[-7:]
        k = pl.program_id(0)
        copy = pltpu.make_async_copy(w_hbm.at[:, first : first + w_ref.shape[1]], w_ref, sem)

        @pl.when(k == 0)
        def _():
            copy.start()

    blocks, _, inputs, lanes = own_ref.shape
    half = blocks // 2 * inputs
    total = blocks * inputs
    panel = total // 4
    for s, ref in enumerate((own_ref, prev_ref, next_ref)):
        x_ref[:, s * lanes : (s + 1) * lanes] = ref[:, 0].reshape(total, lanes)
    x_ref[:half, 3 * lanes :] = low_ref[:, 0].reshape(half, lanes)
    x_ref[half:, 3 * lanes :] = high_ref[:, 0].reshape(half, lanes)

    def panel_of(index):
        return x_ref[pl.ds(pl.multiple_of(index * panel, panel), panel), :]

    stack = stacked(by_row, panel_of(fixed), lanes)
    for step, ref in ((1, up_ref), (3, down_ref), (0, out_ref)):
        re, im = correlated(by_row, panel_of(lax.rem(ring + step, 4)), stack)
        ref[0, 0] = re.astype(ref.dtype)
        ref[1, 0] = im.astype(ref.dtype)
    if by_row:
        return

    @pl.when(k == 0)
    def _():
        copy.wait()

    beams = w_ref.shape[2]
    weights = w_ref[:, k].reshape(2 * beams, total)
    parts = lax.dot_general(
        weights, x_ref[...], (((1,), (0,)), ((), ())), preferred_element_type=F32
    )
    bins = lanes // 2 // INTEG
    sources = [lax.rem(fixed + shift, 4) for shift in (0, 3, 1, 2)]
    beam_ref[0] = pooled(formed(parts, lanes), lanes, 4 * bins, sources)


def near_products(place, slots, by_row, first=0, weights=None, after=()):
    blocks, size, inputs, lanes = slots[0].shape
    total = blocks * inputs
    panel = total // 4

    def data(count):
        return pl.BlockSpec((count, 1, inputs, lanes), lambda k, c: (0, k, 0, 0))

    block = pl.BlockSpec((2, 1, panel, panel), lambda k, c: (0, k, 0, 0))
    shape = (2, size, panel, panel)
    shapes = [pltpu.HBM(shape, F32), pltpu.HBM(shape, BF16), pltpu.HBM(shape, BF16)]
    specs = [block] * 3
    args = [in_hbm(slot) for slot in slots[:3]] + list(slots[3:])
    scratch = [pltpu.VMEM((total, 4 * lanes), BF16)]
    if not by_row:
        beams = weights.shape[2]
        bins = 4 * (lanes // 2 // INTEG)
        shapes.append(jax.ShapeDtypeStruct((size, bins, beams), F32))
        specs.append(pl.BlockSpec((1, bins, beams), lambda k, c: (k, 0, 0)))
        args.append(in_hbm(weights))
        scratch += [pltpu.VMEM((2, size) + weights.shape[2:], BF16), pltpu.SemaphoreType.DMA]
    args += after
    return pl.pallas_call(
        functools.partial(near_kernel, by_row, first),
        out_shape=shapes,
        grid_spec=pltpu.PrefetchScalarGridSpec(
            num_scalar_prefetch=1,
            grid=(size,),
            in_specs=[data(blocks)] * 3 + [data(blocks // 2)] * 2 + [ANY] * (len(args) - 5),
            out_specs=specs,
            scratch_shapes=scratch,
        ),
        compiler_params=limit(62),
        cost_estimate=cost(10 if by_row else 0.1),
    )(place, *args)


def beam_kernel(own_ref, w_ref, *refs):
    out_ref = refs[-1]
    blocks, _, inputs, lanes = own_ref.shape
    owners, _, _, beams, total = w_ref.shape
    x = own_ref[:, 0].reshape(blocks * inputs, lanes)
    weights = jnp.concatenate(
        [w_ref[:, part, 0].reshape(owners * beams, total) for part in range(2)], axis=0
    )
    parts = lax.dot_general(weights, x, (((1,), (0,)), ((), ())), preferred_element_type=F32)
    power = pooled(formed(parts, lanes), lanes, lanes // 2 // INTEG, [0])
    for owner in range(owners):
        out_ref[owner, 0] = power[:, owner * beams : (owner + 1) * beams]


def own_beams(own, weights, after):
    blocks, size, inputs, lanes = own.shape
    owners, _, _, beams, total = weights.shape
    bins = lanes // 2 // INTEG
    return pl.pallas_call(
        beam_kernel,
        out_shape=jax.ShapeDtypeStruct((owners, size, bins, beams), F32),
        grid=(size,),
        in_specs=[
            pl.BlockSpec((blocks, 1, inputs, lanes), lambda k: (0, k, 0, 0)),
            pl.BlockSpec((owners, 2, 1, beams, total), lambda k: (0, 0, k, 0, 0)),
        ]
        + [ANY] * len(after),
        out_specs=pl.BlockSpec((owners, 1, bins, beams), lambda k: (0, k, 0, 0)),
        compiler_params=limit(62),
        cost_estimate=cost(0.1),
    )(in_hbm(own), in_hbm(weights), *after)


def keep_kernel(col_ref, *refs):
    out_ref = refs[-1]
    count = len(refs) - 1
    col = col_ref[0]
    for step, ref in enumerate(refs[:-1]):
        bins = ref.shape[2]
        at = pl.multiple_of(lax.rem(col + count - step, count) * bins, bins)
        for k in range(ref.shape[1]):
            out_ref[k, pl.ds(at, bins), :] = ref[col, k]


def kept_beams(col, shared):
    owners, size, bins, beams = shared[0].shape
    return pl.pallas_call(
        keep_kernel,
        out_shape=jax.ShapeDtypeStruct((size, owners * bins, beams), F32),
        in_specs=[SMEM] + [VMEM] * len(shared),
        out_specs=VMEM,
        cost_estimate=cost(0.1),
    )(col, *shared)


def add_kernel(up_ref, down_ref, low_ref, high_ref, *refs):
    up_out, down_out = refs[-2:]
    up_out[0] = (up_ref[0].astype(F32) + low_ref[...].astype(F32)).astype(BF16)
    down_out[0] = (down_ref[0].astype(F32) + high_ref[...].astype(F32)).astype(BF16)


def added(up, down, low, high, micros, after=()):
    _, size, panel, _ = up.shape
    real = pl.BlockSpec((1, size, panel, panel), lambda n: (0, 0, 0, 0))
    imag = pl.BlockSpec((1, size, panel, panel), lambda n: (1, 0, 0, 0))
    one = pl.BlockSpec((size, panel, panel), lambda n: (0, 0, 0))
    shape = pltpu.HBM(up.shape, BF16)
    return pl.pallas_call(
        add_kernel,
        out_shape=[shape, shape],
        grid=(1,),
        in_specs=[real, imag, one, one] + [ANY] * len(after),
        out_specs=[real, imag],
        input_output_aliases={0: 0, 1: 1},
        compiler_params=limit(62),
        cost_estimate=cost(micros),
    )(up, down, low, high, *after)


def final_kernel(first, own_ref, prev_ref, next_ref, *refs):
    out_hbm, held, sems = refs[-3:]
    size = own_ref.shape[1]
    p = pl.program_id(0)

    def copy(part):
        return pltpu.make_async_copy(
            held.at[part], out_hbm.at[part, first : first + size], sems.at[part]
        )

    for part in range(2):

        @pl.when(p == part)
        def _(part=part):
            held[part] = own_ref[0] + prev_ref[0].astype(F32) + next_ref[0].astype(F32)
            copy(part).start()

    @pl.when(p == 1)
    def _():
        copy(0).wait()
        copy(1).wait()


def finished(own, from_prev, from_next, first, channels, out):
    _, size, panel, _ = own.shape
    block = pl.BlockSpec((1, size, panel, panel), lambda p: (p, 0, 0, 0))
    extra = [] if out is None else [out]
    return pl.pallas_call(
        functools.partial(final_kernel, first),
        out_shape=jax.ShapeDtypeStruct((2, channels, panel, panel), F32),
        grid=(2,),
        in_specs=[block] * 3 + [ANY] * len(extra),
        out_specs=HBM,
        input_output_aliases={3: 0} if extra else {},
        scratch_shapes=[
            pltpu.VMEM((2, size, panel, panel), F32),
            pltpu.SemaphoreType.DMA((2,)),
        ],
        compiler_params=limit(62),
        cost_estimate=cost(0.1),
    )(in_hbm(own), from_prev, from_next, *extra)


def along(value, axis, step):
    count = lax.axis_size(axis)
    return lax.ppermute(value, axis, [(i, (i + step) % count) for i in range(count)])


def both_ways(up, down, axis):
    return along(up, axis, 1), along(down, axis, -1)


def on_device(voltages, input_flags, channel_order, beam_weights):
    size_b, size_a = CHUNKS
    channels = size_a + size_b
    history = passed_along(voltages[:, :, voltages.shape[2] - (TAPS - 1) * NCH :], ("row", "col"), 1)
    row = lax.axis_index("row").astype(jnp.int32)
    col = lax.axis_index("col").astype(jnp.int32)
    place_a = jnp.stack([col, row])
    place_b = jnp.stack([row, col])
    weights = lax.all_gather(beam_weights, "col", axis=0)
    piece_b, piece_a = spectra(voltages, history, input_flags, channel_order, CHUNKS)

    def turn(piece, axis):
        return lax.all_to_all(piece, axis, split_axis=0, concat_axis=0, tiled=True)

    own_b = turn(piece_b, "chan")
    near_b = both_ways(own_b, own_b, "row")
    own_a = turn(piece_a, "chan")
    near_a = both_ways(own_a, own_a, "col")
    half_b = halves(*near_b, [own_a])
    far_b = both_ways(*half_b, "row")
    beam_b = own_beams(own_b, weights, half_b[:1])
    half_a = halves(*near_a, [beam_b])
    far_a = both_ways(*half_a, "col")
    slots_b = (own_b, *near_b, *far_b)
    slots_a = (own_a, *near_a, *far_a)
    re_b, im_b = far_products(place_b, slots_b, True, [half_a[0]])
    got_b = both_ways(re_b, im_b, "col")
    mine_b, up_b, down_b = near_products(place_b, slots_b, True, after=[re_b])
    re_a, im_a = far_products(place_a, slots_a, False, [mine_b])
    got_a = both_ways(re_a, im_a, "row")
    sum_b = added(up_b, down_b, *got_b, 0.1, [re_a])
    sent_b = both_ways(*sum_b, "col")
    mine_a, up_a, down_a, power_a = near_products(
        place_a, slots_a, False, size_b, beam_weights, [sum_b[0]]
    )
    sum_a = added(up_a, down_a, *got_a, 20)
    sent_a = both_ways(*sum_a, "row")

    shared = [beam_b] + [along(beam_b, "col", step) for step in (1, 2, 3)]
    power_b = kept_beams(col.reshape(1), shared)
    out = finished(mine_b, *sent_b, 0, channels, None)
    visibility = finished(mine_a, *sent_a, size_b, channels, out)
    power = jnp.concatenate([power_b, power_a], axis=0)
    return (visibility, jnp.transpose(power, (0, 2, 1)))


def solution(mesh):
    placed = (P(None, "chan", ("row", "col")), P("chan"), P(), P(None, "chan", "col", None))
    return jax.shard_map(
        on_device,
        mesh=mesh,
        in_specs=placed,
        out_specs=(P(None, "chan", "row", "col"), P("chan", "col", "row")),
        check_vma=False,
    )
```

```python
import functools
import math

import jax
import jax.numpy as jnp
import numpy as np
from jax import lax
from jax.experimental import pallas as pl
from jax.experimental.pallas import tpu as pltpu
from jax.sharding import PartitionSpec as P

NCH = 128
TAPS = 4
INTEG = 8
CHUNKS = (5, 3)

F32 = jnp.float32
BF16 = jnp.bfloat16
VMEM = pl.BlockSpec(memory_space=pltpu.VMEM)
SMEM = pl.BlockSpec(memory_space=pltpu.SMEM)
ANY = pl.BlockSpec(memory_space=pl.ANY)
HBM = pl.BlockSpec(memory_space=pltpu.HBM)


def cost(micros):
    return pl.CostEstimate(flops=int(micros * 1.1e9), bytes_accessed=1, transcendentals=0)


def in_hbm(value):
    return pltpu.with_memory_space_constraint(value, pltpu.HBM)


def limit(mebibytes):
    return pltpu.CompilerParams(vmem_limit_bytes=mebibytes * 2**20)


def prototype(taps, length):
    position = np.arange(taps * length, dtype=np.float32) + np.float32(0.5)
    offset = position / np.float32(length) - np.float32(taps / 2.0)
    window = 0.5 - 0.5 * np.cos(2.0 * math.pi * position.astype(np.float64) / (taps * length))
    sinc = np.sin(math.pi * offset.astype(np.float64)) / (math.pi * offset.astype(np.float64))
    return (sinc * window).astype(np.float32).reshape(taps, length)


def dft_table(length):
    index = np.arange(length)
    angle = 2.0 * math.pi / length * (index[:, None] * index[None, :] % length)
    factor = 1.0 / math.sqrt(length)
    table = np.concatenate([np.cos(angle) * factor, np.sin(angle) * factor], axis=1)
    return table.astype(np.float32).astype(jnp.bfloat16)


def passed_along(value, axis, steps):
    count = lax.axis_size(axis)
    initial, last = (max(0, -steps), min(count, count - steps))
    return lax.ppermute(value, axis, [(source, source + steps) for source in range(initial, last)])


def flag_column(flags, inputs):
    eye = lax.broadcasted_iota(jnp.int32, (inputs, inputs), 0) == lax.broadcasted_iota(
        jnp.int32, (inputs, inputs), 1
    )
    held = jnp.where(eye, flags.astype(F32), 0.0)
    return jnp.broadcast_to(jnp.sum(held, axis=1, keepdims=True), (inputs, NCH))


def filter_kernel(v_hbm, flags_hbm, coeff_hbm, filt_ref, v_ref, flags_ref, coeff_ref, sems):
    copies = [
        pltpu.make_async_copy(src, dst, sems.at[n])
        for n, (src, dst) in enumerate(
            ((v_hbm, v_ref), (flags_hbm, flags_ref), (coeff_hbm, coeff_ref))
        )
    ]
    for copy in copies:
        copy.start()
    for copy in copies:
        copy.wait()
    inputs = v_ref.shape[1]
    frames = v_ref.shape[2] // NCH
    mask = flag_column(flags_ref[...], inputs)
    taps = [jnp.broadcast_to(coeff_ref[t : t + 1, :], (inputs, NCH)) * mask for t in range(TAPS)]
    for part in range(2):

        def frame_step(group, past, part=part):
            totals = []
            for f in range(8):
                lanes = pl.ds(pl.multiple_of((group * 8 + f) * NCH, NCH), NCH)
                window = past + (v_ref[part, :, lanes].astype(F32),)
                total = taps[0] * window[0]
                for t in range(1, TAPS):
                    total = total + taps[t] * window[t]
                totals.append(total)
                past = window[1:]
            at = pl.ds(pl.multiple_of(group * 8, 8), 8)
            filt_ref[part, :, at, :] = jnp.transpose(jnp.stack(totals, axis=0), (1, 0, 2))
            return past

        zero = v_ref[part, :, :NCH].astype(F32) * 0.0
        lax.fori_loop(0, frames // 8, frame_step, (zero,) * (TAPS - 1))


def spectrum_kernel(chunks, filt_ref, halo_ref, flags_hbm, order_hbm, coeff_hbm, table_hbm, *rest):
    outs = rest[: len(chunks)]
    flags_ref, order_ref, coeff_ref, table_ref, corr_ref, spec_ref, sems = rest[len(chunks) :]
    copies = [
        pltpu.make_async_copy(src, dst, sems.at[n])
        for n, (src, dst) in enumerate(
            (
                (flags_hbm, flags_ref),
                (order_hbm, order_ref),
                (coeff_hbm, coeff_ref),
                (table_hbm, table_ref),
            )
        )
    ]
    for copy in copies:
        copy.start()
    for copy in copies:
        copy.wait()
    inputs = halo_ref.shape[1]
    frames = filt_ref.shape[2]
    rows = 8
    mask = flag_column(flags_ref[...], inputs)
    taps = [jnp.broadcast_to(coeff_ref[t : t + 1, :], (inputs, NCH)) * mask for t in range(TAPS)]
    for part in range(2):
        past = [halo_ref[part, :, t * NCH : (t + 1) * NCH].astype(F32) for t in range(TAPS - 1)]
        for f in range(rows):
            total = jnp.zeros((inputs, NCH), F32)
            for t in range(TAPS - 1 - f):
                total = total + taps[t] * past[f + t]
            corr_ref[part, pl.ds(f, inputs, stride=rows), :] = total
    onehot = lax.broadcasted_iota(jnp.int32, (NCH, NCH), 0) == jnp.broadcast_to(
        order_ref[...], (NCH, NCH)
    )
    table = lax.dot_general(
        onehot.astype(BF16), table_ref[...], (((0,), (0,)), ((), ())), preferred_element_type=F32
    ).astype(BF16)

    def input_step(group, carry):
        results = []
        for pair in range(4):
            blocks = []
            for which in range(2):
                i = group * 8 + pair * 2 + which
                both = []
                for part in range(2):
                    block = filt_ref[part, i]
                    extra = corr_ref[part, pl.ds(pl.multiple_of(i * rows, rows), rows), :]
                    both.append(
                        jnp.concatenate([block[:rows] + extra, block[rows:]], axis=0).astype(BF16)
                    )
                re, im = both
                blocks.append(jnp.concatenate([re, im], axis=1))
                blocks.append(jnp.concatenate([im, -re], axis=1))
            right = jnp.concatenate(blocks, axis=0)
            result = lax.dot_general(
                table, right, (((1,), (1,)), ((), ())), preferred_element_type=F32
            )
            results += [result[:, :NCH], result[:, NCH:]]
        at = pl.ds(pl.multiple_of(group * 8, 8), 8)
        spec_ref[:, at, :] = jnp.transpose(jnp.stack(results, axis=0), (1, 0, 2))
        return carry

    lax.fori_loop(0, inputs // 8, input_step, 0)
    per_block = sum(chunks)

    def copy_step(block, carry):
        first = 0
        for out, size in zip(outs, chunks):
            for k in range(size):
                out[block, k] = spec_ref[block * per_block + first + k].astype(BF16)
            first += size
        return carry

    lax.fori_loop(0, NCH // per_block, copy_step, 0)


def spectra(voltages, history, flags, order, chunks):
    inputs = voltages.shape[1]
    frames = voltages.shape[2] // NCH
    flags = flags.reshape(1, inputs)
    coeff = jnp.asarray(prototype(TAPS, NCH))
    filtered = pl.pallas_call(
        filter_kernel,
        out_shape=jax.ShapeDtypeStruct((2, inputs, frames, NCH), F32),
        in_specs=[HBM] * 3,
        out_specs=VMEM,
        scratch_shapes=[
            pltpu.VMEM(voltages.shape, BF16),
            pltpu.VMEM((1, inputs), jnp.int32),
            pltpu.VMEM((TAPS, NCH), F32),
            pltpu.SemaphoreType.DMA((3,)),
        ],
        compiler_params=limit(16),
        cost_estimate=cost(5),
    )(in_hbm(voltages), in_hbm(flags), in_hbm(coeff))
    blocks = NCH // sum(chunks)
    return pl.pallas_call(
        functools.partial(spectrum_kernel, chunks),
        out_shape=[jax.ShapeDtypeStruct((blocks, size, inputs, 2 * frames), BF16) for size in chunks],
        in_specs=[VMEM, VMEM] + [HBM] * 4,
        out_specs=[VMEM] * len(chunks),
        scratch_shapes=[
            pltpu.VMEM((1, inputs), jnp.int32),
            pltpu.VMEM((1, NCH), jnp.int32),
            pltpu.VMEM((TAPS, NCH), F32),
            pltpu.VMEM((NCH, 2 * NCH), BF16),
            pltpu.VMEM((2, inputs * 8, NCH), F32),
            pltpu.VMEM((NCH, inputs, 2 * frames), F32),
            pltpu.SemaphoreType.DMA((4,)),
        ],
        compiler_params=limit(16),
        cost_estimate=cost(6),
    )(
        filtered,
        history,
        *[in_hbm(x) for x in (flags, order.reshape(1, NCH), coeff, jnp.asarray(dft_table(NCH)))],
    )


def halves_kernel(low_ref, high_ref, *refs):
    low_out, high_out = refs[-2:]
    low_out[...] = low_ref[...]
    high_out[...] = high_ref[...]


def halves(low, high, after=()):
    blocks = low.shape[0] // 2
    block = (blocks // 2,) + low.shape[1:]
    first = pl.BlockSpec(block, lambda n: (n, 0, 0, 0))
    second = pl.BlockSpec(block, lambda n: (2 + n, 0, 0, 0))
    return pl.pallas_call(
        halves_kernel,
        out_shape=[pltpu.HBM((blocks,) + low.shape[1:], BF16)] * 2,
        grid=(2,),
        in_specs=[first, second] + [ANY] * len(after),
        out_specs=[first, first],
        compiler_params=limit(62),
        cost_estimate=cost(0.1),
    )(low, high, *after)


def turned_panel(panel, lanes, low_sign):
    first = lax.broadcasted_iota(jnp.int32, (panel.shape[0], lanes), 1) < lanes // 2
    parts = []
    for s in range(panel.shape[1] // lanes):
        part = pltpu.roll(panel[:, s * lanes : (s + 1) * lanes].astype(F32), lanes // 2, axis=1)
        parts.append(jnp.where(first, low_sign * part, -low_sign * part).astype(BF16))
    return jnp.concatenate(parts, axis=1)


def correlated(by_row, moving, fixed):
    panel = moving.shape[0]
    left, right = (fixed, moving) if by_row else (moving, fixed)
    result = lax.dot_general(
        left, right, (((1,), (1,)), ((), ())), preferred_element_type=F32
    ) * (1.0 / (NCH * 8))
    if by_row:
        return result[:panel], result[panel:]
    return result[:, :panel], result[:, panel:]


def stacked(by_row, panel, lanes):
    return jnp.concatenate([panel, turned_panel(panel, lanes, 1.0 if by_row else -1.0)], axis=0)


def far_kernel(by_row, place_ref, *refs):
    re_ref, im_ref = refs[-2:]
    lanes = refs[0].shape[3]

    def panel(parts, index):
        near = [part[:, 0].reshape(-1, lanes) for part in parts[:3]]
        low, high = [part[:, 0].reshape(-1, lanes) for part in parts[3:]]
        return jnp.concatenate(near + [jnp.where(index < 2, low, high)], axis=1)

    mine = panel(refs[:5], place_ref[0])
    other = panel(refs[5:10], lax.rem(place_ref[1] + 2, 4))
    re, im = correlated(by_row, other, stacked(by_row, mine, lanes))
    re_ref[0] = re.astype(BF16)
    im_ref[0] = im.astype(BF16)


def far_products(place, slots, by_row, after=()):
    own = slots[0]
    blocks, size, inputs, lanes = own.shape
    quarter = blocks // 4
    panel = quarter * inputs

    def fixed(k, c):
        return (c[0], k, 0, 0)

    def fixed_half(k, c):
        return (lax.rem(c[0], 2), k, 0, 0)

    def other(k, c):
        return (lax.rem(c[1] + 2, 4), k, 0, 0)

    def other_half(k, c):
        return (lax.rem(c[1], 2), k, 0, 0)

    def data(index):
        return pl.BlockSpec((quarter, 1, inputs, lanes), index)

    whole = pl.BlockSpec((1, panel, panel), lambda k, c: (k, 0, 0))
    slots = [in_hbm(slot) for slot in slots[:3]] + list(slots[3:])
    return pl.pallas_call(
        functools.partial(far_kernel, by_row),
        out_shape=[pltpu.HBM((size, panel, panel), BF16)] * 2,
        grid_spec=pltpu.PrefetchScalarGridSpec(
            num_scalar_prefetch=1,
            grid=(size,),
            in_specs=[data(fixed)] * 3
            + [data(fixed_half)] * 2
            + [data(other)] * 3
            + [data(other_half)] * 2
            + [ANY] * len(after),
            out_specs=[whole, whole],
        ),
        compiler_params=limit(62),
        cost_estimate=cost(0.1),
    )(place, *slots, *slots, *after)


def formed(parts, lanes):
    beams = parts.shape[0] // 2
    values = []
    low = lax.broadcasted_iota(jnp.int32, (beams, lanes), 1) < lanes // 2
    for s in range(parts.shape[1] // lanes):
        piece = parts[:, s * lanes : (s + 1) * lanes]
        turned = pltpu.roll(piece[beams:], lanes // 2, axis=1)
        value = piece[:beams] + jnp.where(low, -turned, turned)
        values.append(value * value)
    return jnp.concatenate(values, axis=1) if len(values) > 1 else values[0]


def pooled(power, lanes, bins, sources):
    width = power.shape[1]
    pools = []
    for source in sources:
        lane = lax.broadcasted_iota(jnp.int32, (bins, lanes), 1)
        place = lax.broadcasted_iota(jnp.int32, (bins, lanes), 0)
        wanted = source * (lanes // 2 // INTEG) + lax.rem(lane, lanes // 2) // INTEG
        pools.append(jnp.where(place == wanted, 1.0 / INTEG, 0.0).astype(BF16))
    pool = jnp.concatenate(pools, axis=1) if len(pools) > 1 else pools[0]
    high = power.astype(BF16)
    rest = power - high.astype(F32)
    middle = rest.astype(BF16)
    low = (rest - middle.astype(F32)).astype(BF16)
    total = jnp.zeros((bins, power.shape[0]), F32)
    for term in (low, middle, high):
        total = total + lax.dot_general(
            pool, term, (((1,), (1,)), ((), ())), preferred_element_type=F32
        )
    return total


def near_kernel(by_row, first, place_ref, own_ref, prev_ref, next_ref, low_ref, high_ref, *refs):
    fixed, ring = place_ref[0], place_ref[1]
    if by_row:
        out_ref, up_ref, down_ref, x_ref = refs[-4:]
    else:
        w_hbm = refs[0]
        out_ref, up_ref, down_ref, beam_ref, x_ref, w_ref, sem = refs[-7:]
        k = pl.program_id(0)
        copy = pltpu.make_async_copy(w_hbm.at[:, first : first + w_ref.shape[1]], w_ref, sem)

        @pl.when(k == 0)
        def _():
            copy.start()

    blocks, _, inputs, lanes = own_ref.shape
    half = blocks // 2 * inputs
    total = blocks * inputs
    panel = total // 4
    for s, ref in enumerate((own_ref, prev_ref, next_ref)):
        x_ref[:, s * lanes : (s + 1) * lanes] = ref[:, 0].reshape(total, lanes)
    x_ref[:half, 3 * lanes :] = low_ref[:, 0].reshape(half, lanes)
    x_ref[half:, 3 * lanes :] = high_ref[:, 0].reshape(half, lanes)

    def panel_of(index):
        return x_ref[pl.ds(pl.multiple_of(index * panel, panel), panel), :]

    stack = stacked(by_row, panel_of(fixed), lanes)
    for step, ref in ((1, up_ref), (3, down_ref), (0, out_ref)):
        re, im = correlated(by_row, panel_of(lax.rem(ring + step, 4)), stack)
        ref[0, 0] = re.astype(ref.dtype)
        ref[1, 0] = im.astype(ref.dtype)
    if by_row:
        return

    @pl.when(k == 0)
    def _():
        copy.wait()

    beams = w_ref.shape[2]
    weights = w_ref[:, k].reshape(2 * beams, total)
    parts = lax.dot_general(
        weights, x_ref[...], (((1,), (0,)), ((), ())), preferred_element_type=F32
    )
    bins = lanes // 2 // INTEG
    sources = [lax.rem(fixed + shift, 4) for shift in (0, 3, 1, 2)]
    beam_ref[0] = pooled(formed(parts, lanes), lanes, 4 * bins, sources)


def near_products(place, slots, by_row, first=0, weights=None, after=()):
    blocks, size, inputs, lanes = slots[0].shape
    total = blocks * inputs
    panel = total // 4

    def data(count):
        return pl.BlockSpec((count, 1, inputs, lanes), lambda k, c: (0, k, 0, 0))

    block = pl.BlockSpec((2, 1, panel, panel), lambda k, c: (0, k, 0, 0))
    shape = (2, size, panel, panel)
    shapes = [pltpu.HBM(shape, F32), pltpu.HBM(shape, BF16), pltpu.HBM(shape, BF16)]
    specs = [block] * 3
    args = [in_hbm(slot) for slot in slots[:3]] + list(slots[3:])
    scratch = [pltpu.VMEM((total, 4 * lanes), BF16)]
    if not by_row:
        beams = weights.shape[2]
        bins = 4 * (lanes // 2 // INTEG)
        shapes.append(jax.ShapeDtypeStruct((size, bins, beams), F32))
        specs.append(pl.BlockSpec((1, bins, beams), lambda k, c: (k, 0, 0)))
        args.append(in_hbm(weights))
        scratch += [pltpu.VMEM((2, size) + weights.shape[2:], BF16), pltpu.SemaphoreType.DMA]
    args += after
    return pl.pallas_call(
        functools.partial(near_kernel, by_row, first),
        out_shape=shapes,
        grid_spec=pltpu.PrefetchScalarGridSpec(
            num_scalar_prefetch=1,
            grid=(size,),
            in_specs=[data(blocks)] * 3 + [data(blocks // 2)] * 2 + [ANY] * (len(args) - 5),
            out_specs=specs,
            scratch_shapes=scratch,
        ),
        compiler_params=limit(62),
        cost_estimate=cost(10 if by_row else 0.1),
    )(place, *args)


def beam_kernel(own_ref, w_ref, *refs):
    out_ref = refs[-1]
    blocks, _, inputs, lanes = own_ref.shape
    owners, _, _, beams, total = w_ref.shape
    x = own_ref[:, 0].reshape(blocks * inputs, lanes)
    weights = jnp.concatenate(
        [w_ref[:, part, 0].reshape(owners * beams, total) for part in range(2)], axis=0
    )
    parts = lax.dot_general(weights, x, (((1,), (0,)), ((), ())), preferred_element_type=F32)
    power = pooled(formed(parts, lanes), lanes, lanes // 2 // INTEG, [0])
    for owner in range(owners):
        out_ref[owner, 0] = power[:, owner * beams : (owner + 1) * beams]


def own_beams(own, weights, after):
    blocks, size, inputs, lanes = own.shape
    owners, _, _, beams, total = weights.shape
    bins = lanes // 2 // INTEG
    return pl.pallas_call(
        beam_kernel,
        out_shape=jax.ShapeDtypeStruct((owners, size, bins, beams), F32),
        grid=(size,),
        in_specs=[
            pl.BlockSpec((blocks, 1, inputs, lanes), lambda k: (0, k, 0, 0)),
            pl.BlockSpec((owners, 2, 1, beams, total), lambda k: (0, 0, k, 0, 0)),
        ]
        + [ANY] * len(after),
        out_specs=pl.BlockSpec((owners, 1, bins, beams), lambda k: (0, k, 0, 0)),
        compiler_params=limit(62),
        cost_estimate=cost(0.1),
    )(in_hbm(own), in_hbm(weights), *after)


def add_kernel(up_ref, down_ref, low_ref, high_ref, *refs):
    up_out, down_out = refs[-2:]
    up_out[0] = (up_ref[0].astype(F32) + low_ref[...].astype(F32)).astype(BF16)
    down_out[0] = (down_ref[0].astype(F32) + high_ref[...].astype(F32)).astype(BF16)


def added(up, down, low, high, micros):
    _, size, panel, _ = up.shape
    real = pl.BlockSpec((1, size, panel, panel), lambda n: (0, 0, 0, 0))
    imag = pl.BlockSpec((1, size, panel, panel), lambda n: (1, 0, 0, 0))
    one = pl.BlockSpec((size, panel, panel), lambda n: (0, 0, 0))
    shape = pltpu.HBM(up.shape, BF16)
    return pl.pallas_call(
        add_kernel,
        out_shape=[shape, shape],
        grid=(1,),
        in_specs=[real, imag, one, one],
        out_specs=[real, imag],
        input_output_aliases={0: 0, 1: 1},
        compiler_params=limit(62),
        cost_estimate=cost(micros),
    )(up, down, low, high)


def final_kernel(first, own_ref, prev_ref, next_ref, *refs):
    out_hbm, held, sems = refs[-3:]
    size = own_ref.shape[1]
    p = pl.program_id(0)

    def copy(part):
        return pltpu.make_async_copy(
            held.at[part], out_hbm.at[part, first : first + size], sems.at[part]
        )

    for part in range(2):

        @pl.when(p == part)
        def _(part=part):
            held[part] = own_ref[0] + prev_ref[0].astype(F32) + next_ref[0].astype(F32)
            copy(part).start()

    @pl.when(p == 1)
    def _():
        copy(0).wait()
        copy(1).wait()


def finished(own, from_prev, from_next, first, channels, out):
    _, size, panel, _ = own.shape
    block = pl.BlockSpec((1, size, panel, panel), lambda p: (p, 0, 0, 0))
    extra = [] if out is None else [out]
    return pl.pallas_call(
        functools.partial(final_kernel, first),
        out_shape=jax.ShapeDtypeStruct((2, channels, panel, panel), F32),
        grid=(2,),
        in_specs=[block] * 3 + [ANY] * len(extra),
        out_specs=HBM,
        input_output_aliases={3: 0} if extra else {},
        scratch_shapes=[
            pltpu.VMEM((2, size, panel, panel), F32),
            pltpu.SemaphoreType.DMA((2,)),
        ],
        compiler_params=limit(62),
        cost_estimate=cost(0.1),
    )(in_hbm(own), from_prev, from_next, *extra)


def along(value, axis, step):
    count = lax.axis_size(axis)
    return lax.ppermute(value, axis, [(i, (i + step) % count) for i in range(count)])


def both_ways(up, down, axis):
    return along(up, axis, 1), along(down, axis, -1)


def on_device(voltages, input_flags, channel_order, beam_weights):
    size_b, size_a = CHUNKS
    channels = size_a + size_b
    history = passed_along(voltages[:, :, voltages.shape[2] - (TAPS - 1) * NCH :], ("row", "col"), 1)
    row = lax.axis_index("row").astype(jnp.int32)
    col = lax.axis_index("col").astype(jnp.int32)
    place_a = jnp.stack([col, row])
    place_b = jnp.stack([row, col])
    weights = lax.all_gather(beam_weights, "col", axis=0)
    piece_b, piece_a = spectra(voltages, history, input_flags, channel_order, CHUNKS)

    def turn(piece, axis):
        return lax.all_to_all(piece, axis, split_axis=0, concat_axis=0, tiled=True)

    own_b = turn(piece_b, "chan")
    near_b = both_ways(own_b, own_b, "row")
    own_a = turn(piece_a, "chan")
    near_a = both_ways(own_a, own_a, "col")
    half_b = halves(*near_b, [own_a])
    far_b = both_ways(*half_b, "row")
    beam_b = own_beams(own_b, weights, half_b[:1])
    half_a = halves(*near_a, [beam_b])
    far_a = both_ways(*half_a, "col")
    slots_b = (own_b, *near_b, *far_b)
    slots_a = (own_a, *near_a, *far_a)
    re_b, im_b = far_products(place_b, slots_b, True, [half_a[0]])
    got_b = both_ways(re_b, im_b, "col")
    re_a, im_a = far_products(place_a, slots_a, False, [re_b])
    got_a = both_ways(re_a, im_a, "row")
    mine_b, up_b, down_b = near_products(place_b, slots_b, True, after=[re_a])
    sum_b = added(up_b, down_b, *got_b, 0.1)
    sent_b = both_ways(*sum_b, "col")
    mine_a, up_a, down_a, power_a = near_products(
        place_a, slots_a, False, size_b, beam_weights, [sum_b[0]]
    )
    sum_a = added(up_a, down_a, *got_a, 20)
    sent_a = both_ways(*sum_a, "row")

    power_b = jnp.transpose(turn(beam_b, "col"), (1, 0, 2, 3)).reshape(size_b, -1, beam_b.shape[3])
    out = finished(mine_b, *sent_b, 0, channels, None)
    visibility = finished(mine_a, *sent_a, size_b, channels, out)
    power = jnp.concatenate([power_b, power_a], axis=0)
    return (visibility, jnp.transpose(power, (0, 2, 1)))


def solution(mesh):
    placed = (P(None, "chan", ("row", "col")), P("chan"), P(), P(None, "chan", "col", None))
    return jax.shard_map(
        on_device,
        mesh=mesh,
        in_specs=placed,
        out_specs=(P(None, "chan", "row", "col"), P("chan", "col", "row")),
        check_vma=False,
    )
```

```python
import functools
import math

import jax
import jax.numpy as jnp
import numpy as np
from jax import lax
from jax.experimental import pallas as pl
from jax.experimental.pallas import tpu as pltpu
from jax.sharding import PartitionSpec as P

NCH = 128
TAPS = 4
INTEG = 8
CHUNKS = (5, 3)

F32 = jnp.float32
BF16 = jnp.bfloat16
VMEM = pl.BlockSpec(memory_space=pltpu.VMEM)
SMEM = pl.BlockSpec(memory_space=pltpu.SMEM)
ANY = pl.BlockSpec(memory_space=pl.ANY)
HBM = pl.BlockSpec(memory_space=pltpu.HBM)


def cost(micros):
    return pl.CostEstimate(flops=int(micros * 1.1e9), bytes_accessed=1, transcendentals=0)


def in_hbm(value):
    return pltpu.with_memory_space_constraint(value, pltpu.HBM)


def limit(mebibytes):
    return pltpu.CompilerParams(vmem_limit_bytes=mebibytes * 2**20)


def prototype(taps, length):
    position = np.arange(taps * length, dtype=np.float32) + np.float32(0.5)
    offset = position / np.float32(length) - np.float32(taps / 2.0)
    window = 0.5 - 0.5 * np.cos(2.0 * math.pi * position.astype(np.float64) / (taps * length))
    sinc = np.sin(math.pi * offset.astype(np.float64)) / (math.pi * offset.astype(np.float64))
    return (sinc * window).astype(np.float32).reshape(taps, length)


def dft_table(length):
    index = np.arange(length)
    angle = 2.0 * math.pi / length * (index[:, None] * index[None, :] % length)
    factor = 1.0 / math.sqrt(length)
    table = np.concatenate([np.cos(angle) * factor, np.sin(angle) * factor], axis=1)
    return table.astype(np.float32).astype(jnp.bfloat16)


def passed_along(value, axis, steps):
    count = lax.axis_size(axis)
    initial, last = (max(0, -steps), min(count, count - steps))
    return lax.ppermute(value, axis, [(source, source + steps) for source in range(initial, last)])


def flag_column(flags, inputs):
    eye = lax.broadcasted_iota(jnp.int32, (inputs, inputs), 0) == lax.broadcasted_iota(
        jnp.int32, (inputs, inputs), 1
    )
    held = jnp.where(eye, flags.astype(F32), 0.0)
    return jnp.broadcast_to(jnp.sum(held, axis=1, keepdims=True), (inputs, NCH))


def filter_kernel(v_hbm, flags_hbm, coeff_hbm, filt_ref, v_ref, flags_ref, coeff_ref, sems):
    copies = [
        pltpu.make_async_copy(src, dst, sems.at[n])
        for n, (src, dst) in enumerate(
            ((v_hbm, v_ref), (flags_hbm, flags_ref), (coeff_hbm, coeff_ref))
        )
    ]
    for copy in copies:
        copy.start()
    for copy in copies:
        copy.wait()
    inputs = v_ref.shape[1]
    frames = v_ref.shape[2] // NCH
    mask = flag_column(flags_ref[...], inputs)
    taps = [jnp.broadcast_to(coeff_ref[t : t + 1, :], (inputs, NCH)) * mask for t in range(TAPS)]
    for part in range(2):

        def frame_step(group, past, part=part):
            totals = []
            for f in range(8):
                lanes = pl.ds(pl.multiple_of((group * 8 + f) * NCH, NCH), NCH)
                window = past + (v_ref[part, :, lanes].astype(F32),)
                total = taps[0] * window[0]
                for t in range(1, TAPS):
                    total = total + taps[t] * window[t]
                totals.append(total)
                past = window[1:]
            at = pl.ds(pl.multiple_of(group * 8, 8), 8)
            filt_ref[part, :, at, :] = jnp.transpose(jnp.stack(totals, axis=0), (1, 0, 2))
            return past

        zero = v_ref[part, :, :NCH].astype(F32) * 0.0
        lax.fori_loop(0, frames // 8, frame_step, (zero,) * (TAPS - 1))


def spectrum_kernel(chunks, filt_ref, halo_ref, flags_hbm, order_hbm, coeff_hbm, table_hbm, *rest):
    outs = rest[: len(chunks)]
    flags_ref, order_ref, coeff_ref, table_ref, corr_ref, spec_ref, sems = rest[len(chunks) :]
    copies = [
        pltpu.make_async_copy(src, dst, sems.at[n])
        for n, (src, dst) in enumerate(
            (
                (flags_hbm, flags_ref),
                (order_hbm, order_ref),
                (coeff_hbm, coeff_ref),
                (table_hbm, table_ref),
            )
        )
    ]
    for copy in copies:
        copy.start()
    for copy in copies:
        copy.wait()
    inputs = halo_ref.shape[1]
    frames = filt_ref.shape[2]
    rows = 8
    mask = flag_column(flags_ref[...], inputs)
    taps = [jnp.broadcast_to(coeff_ref[t : t + 1, :], (inputs, NCH)) * mask for t in range(TAPS)]
    for part in range(2):
        past = [halo_ref[part, :, t * NCH : (t + 1) * NCH].astype(F32) for t in range(TAPS - 1)]
        for f in range(rows):
            total = jnp.zeros((inputs, NCH), F32)
            for t in range(TAPS - 1 - f):
                total = total + taps[t] * past[f + t]
            corr_ref[part, pl.ds(f, inputs, stride=rows), :] = total
    onehot = lax.broadcasted_iota(jnp.int32, (NCH, NCH), 0) == jnp.broadcast_to(
        order_ref[...], (NCH, NCH)
    )
    table = lax.dot_general(
        onehot.astype(BF16), table_ref[...], (((0,), (0,)), ((), ())), preferred_element_type=F32
    ).astype(BF16)

    def input_step(group, carry):
        results = []
        for pair in range(4):
            blocks = []
            for which in range(2):
                i = group * 8 + pair * 2 + which
                both = []
                for part in range(2):
                    block = filt_ref[part, i]
                    extra = corr_ref[part, pl.ds(pl.multiple_of(i * rows, rows), rows), :]
                    both.append(
                        jnp.concatenate([block[:rows] + extra, block[rows:]], axis=0).astype(BF16)
                    )
                re, im = both
                blocks.append(jnp.concatenate([re, im], axis=1))
                blocks.append(jnp.concatenate([im, -re], axis=1))
            right = jnp.concatenate(blocks, axis=0)
            result = lax.dot_general(
                table, right, (((1,), (1,)), ((), ())), preferred_element_type=F32
            )
            results += [result[:, :NCH], result[:, NCH:]]
        at = pl.ds(pl.multiple_of(group * 8, 8), 8)
        spec_ref[:, at, :] = jnp.transpose(jnp.stack(results, axis=0), (1, 0, 2))
        return carry

    lax.fori_loop(0, inputs // 8, input_step, 0)
    per_block = sum(chunks)

    def copy_step(block, carry):
        first = 0
        for out, size in zip(outs, chunks):
            for k in range(size):
                out[block, k] = spec_ref[block * per_block + first + k].astype(BF16)
            first += size
        return carry

    lax.fori_loop(0, NCH // per_block, copy_step, 0)


def spectra(voltages, history, flags, order, chunks):
    inputs = voltages.shape[1]
    frames = voltages.shape[2] // NCH
    flags = flags.reshape(1, inputs)
    coeff = jnp.asarray(prototype(TAPS, NCH))
    filtered = pl.pallas_call(
        filter_kernel,
        out_shape=jax.ShapeDtypeStruct((2, inputs, frames, NCH), F32),
        in_specs=[HBM] * 3,
        out_specs=VMEM,
        scratch_shapes=[
            pltpu.VMEM(voltages.shape, BF16),
            pltpu.VMEM((1, inputs), jnp.int32),
            pltpu.VMEM((TAPS, NCH), F32),
            pltpu.SemaphoreType.DMA((3,)),
        ],
        compiler_params=limit(16),
        cost_estimate=cost(5),
    )(in_hbm(voltages), in_hbm(flags), in_hbm(coeff))
    blocks = NCH // sum(chunks)
    return pl.pallas_call(
        functools.partial(spectrum_kernel, chunks),
        out_shape=[jax.ShapeDtypeStruct((blocks, size, inputs, 2 * frames), BF16) for size in chunks],
        in_specs=[VMEM, VMEM] + [HBM] * 4,
        out_specs=[VMEM] * len(chunks),
        scratch_shapes=[
            pltpu.VMEM((1, inputs), jnp.int32),
            pltpu.VMEM((1, NCH), jnp.int32),
            pltpu.VMEM((TAPS, NCH), F32),
            pltpu.VMEM((NCH, 2 * NCH), BF16),
            pltpu.VMEM((2, inputs * 8, NCH), F32),
            pltpu.VMEM((NCH, inputs, 2 * frames), F32),
            pltpu.SemaphoreType.DMA((4,)),
        ],
        compiler_params=limit(16),
        cost_estimate=cost(6),
    )(
        filtered,
        history,
        *[in_hbm(x) for x in (flags, order.reshape(1, NCH), coeff, jnp.asarray(dft_table(NCH)))],
    )


def halves_kernel(low_ref, high_ref, *refs):
    low_out, high_out = refs[-2:]
    low_out[...] = low_ref[...]
    high_out[...] = high_ref[...]


def halves(low, high, after=()):
    blocks = low.shape[0] // 2
    block = (blocks // 2,) + low.shape[1:]
    first = pl.BlockSpec(block, lambda n: (n, 0, 0, 0))
    second = pl.BlockSpec(block, lambda n: (2 + n, 0, 0, 0))
    return pl.pallas_call(
        halves_kernel,
        out_shape=[pltpu.HBM((blocks,) + low.shape[1:], BF16)] * 2,
        grid=(2,),
        in_specs=[first, second] + [ANY] * len(after),
        out_specs=[first, first],
        compiler_params=limit(62),
        cost_estimate=cost(0.1),
    )(low, high, *after)


def turned_panel(panel, lanes, low_sign):
    first = lax.broadcasted_iota(jnp.int32, (panel.shape[0], lanes), 1) < lanes // 2
    parts = []
    for s in range(panel.shape[1] // lanes):
        part = pltpu.roll(panel[:, s * lanes : (s + 1) * lanes].astype(F32), lanes // 2, axis=1)
        parts.append(jnp.where(first, low_sign * part, -low_sign * part).astype(BF16))
    return jnp.concatenate(parts, axis=1)


def correlated(by_row, moving, fixed):
    panel = moving.shape[0]
    left, right = (fixed, moving) if by_row else (moving, fixed)
    result = lax.dot_general(
        left, right, (((1,), (1,)), ((), ())), preferred_element_type=F32
    ) * (1.0 / (NCH * 8))
    if by_row:
        return result[:panel], result[panel:]
    return result[:, :panel], result[:, panel:]


def stacked(by_row, panel, lanes):
    return jnp.concatenate([panel, turned_panel(panel, lanes, 1.0 if by_row else -1.0)], axis=0)


def far_kernel(by_row, place_ref, *refs):
    re_ref, im_ref = refs[-2:]
    lanes = refs[0].shape[3]

    def panel(parts, index):
        near = [part[:, 0].reshape(-1, lanes) for part in parts[:3]]
        low, high = [part[:, 0].reshape(-1, lanes) for part in parts[3:]]
        return jnp.concatenate(near + [jnp.where(index < 2, low, high)], axis=1)

    mine = panel(refs[:5], place_ref[0])
    other = panel(refs[5:10], lax.rem(place_ref[1] + 2, 4))
    re, im = correlated(by_row, other, stacked(by_row, mine, lanes))
    re_ref[0] = re.astype(BF16)
    im_ref[0] = im.astype(BF16)


def far_products(place, slots, by_row, after=()):
    own = slots[0]
    blocks, size, inputs, lanes = own.shape
    quarter = blocks // 4
    panel = quarter * inputs

    def fixed(k, c):
        return (c[0], k, 0, 0)

    def fixed_half(k, c):
        return (lax.rem(c[0], 2), k, 0, 0)

    def other(k, c):
        return (lax.rem(c[1] + 2, 4), k, 0, 0)

    def other_half(k, c):
        return (lax.rem(c[1], 2), k, 0, 0)

    def data(index):
        return pl.BlockSpec((quarter, 1, inputs, lanes), index)

    whole = pl.BlockSpec((1, panel, panel), lambda k, c: (k, 0, 0))
    slots = [in_hbm(slot) for slot in slots[:3]] + list(slots[3:])
    return pl.pallas_call(
        functools.partial(far_kernel, by_row),
        out_shape=[pltpu.HBM((size, panel, panel), BF16)] * 2,
        grid_spec=pltpu.PrefetchScalarGridSpec(
            num_scalar_prefetch=1,
            grid=(size,),
            in_specs=[data(fixed)] * 3
            + [data(fixed_half)] * 2
            + [data(other)] * 3
            + [data(other_half)] * 2
            + [ANY] * len(after),
            out_specs=[whole, whole],
        ),
        compiler_params=limit(62),
        cost_estimate=cost(0.1),
    )(place, *slots, *slots, *after)


def formed(parts, lanes):
    beams = parts.shape[0] // 2
    values = []
    low = lax.broadcasted_iota(jnp.int32, (beams, lanes), 1) < lanes // 2
    for s in range(parts.shape[1] // lanes):
        piece = parts[:, s * lanes : (s + 1) * lanes]
        turned = pltpu.roll(piece[beams:], lanes // 2, axis=1)
        value = piece[:beams] + jnp.where(low, -turned, turned)
        values.append(value * value)
    return jnp.concatenate(values, axis=1) if len(values) > 1 else values[0]


def pooled(power, lanes, bins, sources):
    width = power.shape[1]
    pools = []
    for source in sources:
        lane = lax.broadcasted_iota(jnp.int32, (bins, lanes), 1)
        place = lax.broadcasted_iota(jnp.int32, (bins, lanes), 0)
        wanted = source * (lanes // 2 // INTEG) + lax.rem(lane, lanes // 2) // INTEG
        pools.append(jnp.where(place == wanted, 1.0 / INTEG, 0.0).astype(BF16))
    pool = jnp.concatenate(pools, axis=1) if len(pools) > 1 else pools[0]
    high = power.astype(BF16)
    rest = power - high.astype(F32)
    middle = rest.astype(BF16)
    low = (rest - middle.astype(F32)).astype(BF16)
    total = jnp.zeros((bins, power.shape[0]), F32)
    for term in (low, middle, high):
        total = total + lax.dot_general(
            pool, term, (((1,), (1,)), ((), ())), preferred_element_type=F32
        )
    return total


def near_kernel(by_row, first, place_ref, own_ref, prev_ref, next_ref, low_ref, high_ref, *refs):
    fixed, ring = place_ref[0], place_ref[1]
    if by_row:
        out_ref, up_ref, down_ref, x_ref = refs[-4:]
    else:
        w_hbm = refs[0]
        out_ref, up_ref, down_ref, beam_ref, x_ref, w_ref, sem = refs[-7:]
        k = pl.program_id(0)
        copy = pltpu.make_async_copy(w_hbm.at[:, first : first + w_ref.shape[1]], w_ref, sem)

        @pl.when(k == 0)
        def _():
            copy.start()

    blocks, _, inputs, lanes = own_ref.shape
    half = blocks // 2 * inputs
    total = blocks * inputs
    panel = total // 4
    for s, ref in enumerate((own_ref, prev_ref, next_ref)):
        x_ref[:, s * lanes : (s + 1) * lanes] = ref[:, 0].reshape(total, lanes)
    x_ref[:half, 3 * lanes :] = low_ref[:, 0].reshape(half, lanes)
    x_ref[half:, 3 * lanes :] = high_ref[:, 0].reshape(half, lanes)

    def panel_of(index):
        return x_ref[pl.ds(pl.multiple_of(index * panel, panel), panel), :]

    stack = stacked(by_row, panel_of(fixed), lanes)
    for step, ref in ((1, up_ref), (3, down_ref), (0, out_ref)):
        re, im = correlated(by_row, panel_of(lax.rem(ring + step, 4)), stack)
        ref[0, 0] = re.astype(ref.dtype)
        ref[1, 0] = im.astype(ref.dtype)
    if by_row:
        return

    @pl.when(k == 0)
    def _():
        copy.wait()

    beams = w_ref.shape[2]
    weights = w_ref[:, k].reshape(2 * beams, total)
    parts = lax.dot_general(
        weights, x_ref[...], (((1,), (0,)), ((), ())), preferred_element_type=F32
    )
    bins = lanes // 2 // INTEG
    sources = [lax.rem(fixed + shift, 4) for shift in (0, 3, 1, 2)]
    beam_ref[0] = pooled(formed(parts, lanes), lanes, 4 * bins, sources)


def near_products(place, slots, by_row, first=0, weights=None, after=()):
    blocks, size, inputs, lanes = slots[0].shape
    total = blocks * inputs
    panel = total // 4

    def data(count):
        return pl.BlockSpec((count, 1, inputs, lanes), lambda k, c: (0, k, 0, 0))

    block = pl.BlockSpec((2, 1, panel, panel), lambda k, c: (0, k, 0, 0))
    shape = (2, size, panel, panel)
    shapes = [pltpu.HBM(shape, F32), pltpu.HBM(shape, BF16), pltpu.HBM(shape, BF16)]
    specs = [block] * 3
    args = [in_hbm(slot) for slot in slots[:3]] + list(slots[3:])
    scratch = [pltpu.VMEM((total, 4 * lanes), BF16)]
    if not by_row:
        beams = weights.shape[2]
        bins = 4 * (lanes // 2 // INTEG)
        shapes.append(jax.ShapeDtypeStruct((size, bins, beams), F32))
        specs.append(pl.BlockSpec((1, bins, beams), lambda k, c: (k, 0, 0)))
        args.append(in_hbm(weights))
        scratch += [pltpu.VMEM((2, size) + weights.shape[2:], BF16), pltpu.SemaphoreType.DMA]
    args += after
    return pl.pallas_call(
        functools.partial(near_kernel, by_row, first),
        out_shape=shapes,
        grid_spec=pltpu.PrefetchScalarGridSpec(
            num_scalar_prefetch=1,
            grid=(size,),
            in_specs=[data(blocks)] * 3 + [data(blocks // 2)] * 2 + [ANY] * (len(args) - 5),
            out_specs=specs,
            scratch_shapes=scratch,
        ),
        compiler_params=limit(62),
        cost_estimate=cost(10),
    )(place, *args)


def beam_kernel(own_ref, w_ref, *refs):
    out_ref = refs[-1]
    blocks, _, inputs, lanes = own_ref.shape
    owners, _, _, beams, total = w_ref.shape
    x = own_ref[:, 0].reshape(blocks * inputs, lanes)
    weights = jnp.concatenate(
        [w_ref[:, part, 0].reshape(owners * beams, total) for part in range(2)], axis=0
    )
    parts = lax.dot_general(weights, x, (((1,), (0,)), ((), ())), preferred_element_type=F32)
    power = pooled(formed(parts, lanes), lanes, lanes // 2 // INTEG, [0])
    for owner in range(owners):
        out_ref[owner, 0] = power[:, owner * beams : (owner + 1) * beams]


def own_beams(own, weights, after):
    blocks, size, inputs, lanes = own.shape
    owners, _, _, beams, total = weights.shape
    bins = lanes // 2 // INTEG
    return pl.pallas_call(
        beam_kernel,
        out_shape=jax.ShapeDtypeStruct((owners, size, bins, beams), F32),
        grid=(size,),
        in_specs=[
            pl.BlockSpec((blocks, 1, inputs, lanes), lambda k: (0, k, 0, 0)),
            pl.BlockSpec((owners, 2, 1, beams, total), lambda k: (0, 0, k, 0, 0)),
        ]
        + [ANY] * len(after),
        out_specs=pl.BlockSpec((owners, 1, bins, beams), lambda k: (0, k, 0, 0)),
        compiler_params=limit(62),
        cost_estimate=cost(0.1),
    )(in_hbm(own), in_hbm(weights), *after)


def add_kernel(up_ref, down_ref, low_ref, high_ref, *refs):
    up_out, down_out = refs[-2:]
    up_out[0] = (up_ref[0].astype(F32) + low_ref[...].astype(F32)).astype(BF16)
    down_out[0] = (down_ref[0].astype(F32) + high_ref[...].astype(F32)).astype(BF16)


def added(up, down, low, high, micros):
    _, size, panel, _ = up.shape
    real = pl.BlockSpec((1, size, panel, panel), lambda n: (0, 0, 0, 0))
    imag = pl.BlockSpec((1, size, panel, panel), lambda n: (1, 0, 0, 0))
    one = pl.BlockSpec((size, panel, panel), lambda n: (0, 0, 0))
    shape = pltpu.HBM(up.shape, BF16)
    return pl.pallas_call(
        add_kernel,
        out_shape=[shape, shape],
        grid=(1,),
        in_specs=[real, imag, one, one],
        out_specs=[real, imag],
        input_output_aliases={0: 0, 1: 1},
        compiler_params=limit(62),
        cost_estimate=cost(micros),
    )(up, down, low, high)


def final_kernel(first, own_ref, prev_ref, next_ref, *refs):
    out_hbm, held, sems = refs[-3:]
    size = own_ref.shape[1]
    p = pl.program_id(0)

    def copy(part):
        return pltpu.make_async_copy(
            held.at[part], out_hbm.at[part, first : first + size], sems.at[part]
        )

    for part in range(2):

        @pl.when(p == part)
        def _(part=part):
            held[part] = own_ref[0] + prev_ref[0].astype(F32) + next_ref[0].astype(F32)
            copy(part).start()

    @pl.when(p == 1)
    def _():
        copy(0).wait()
        copy(1).wait()


def finished(own, from_prev, from_next, first, channels, out):
    _, size, panel, _ = own.shape
    block = pl.BlockSpec((1, size, panel, panel), lambda p: (p, 0, 0, 0))
    extra = [] if out is None else [out]
    return pl.pallas_call(
        functools.partial(final_kernel, first),
        out_shape=jax.ShapeDtypeStruct((2, channels, panel, panel), F32),
        grid=(2,),
        in_specs=[block] * 3 + [ANY] * len(extra),
        out_specs=HBM,
        input_output_aliases={3: 0} if extra else {},
        scratch_shapes=[
            pltpu.VMEM((2, size, panel, panel), F32),
            pltpu.SemaphoreType.DMA((2,)),
        ],
        compiler_params=limit(62),
        cost_estimate=cost(0.1),
    )(in_hbm(own), from_prev, from_next, *extra)


def along(value, axis, step):
    count = lax.axis_size(axis)
    return lax.ppermute(value, axis, [(i, (i + step) % count) for i in range(count)])


def both_ways(up, down, axis):
    return along(up, axis, 1), along(down, axis, -1)


def on_device(voltages, input_flags, channel_order, beam_weights):
    size_b, size_a = CHUNKS
    channels = size_a + size_b
    history = passed_along(voltages[:, :, voltages.shape[2] - (TAPS - 1) * NCH :], ("row", "col"), 1)
    row = lax.axis_index("row").astype(jnp.int32)
    col = lax.axis_index("col").astype(jnp.int32)
    place_a = jnp.stack([col, row])
    place_b = jnp.stack([row, col])
    weights = lax.all_gather(beam_weights, "col", axis=0)
    piece_b, piece_a = spectra(voltages, history, input_flags, channel_order, CHUNKS)

    def turn(piece, axis):
        return lax.all_to_all(piece, axis, split_axis=0, concat_axis=0, tiled=True)

    own_b = turn(piece_b, "chan")
    near_b = both_ways(own_b, own_b, "row")
    own_a = turn(piece_a, "chan")
    near_a = both_ways(own_a, own_a, "col")
    half_b = halves(*near_b, [own_a])
    far_b = both_ways(*half_b, "row")
    beam_b = own_beams(own_b, weights, half_b[:1])
    half_a = halves(*near_a, [beam_b])
    far_a = both_ways(*half_a, "col")
    slots_b = (own_b, *near_b, *far_b)
    slots_a = (own_a, *near_a, *far_a)
    re_b, im_b = far_products(place_b, slots_b, True, [half_a[0]])
    got_b = both_ways(re_b, im_b, "col")
    mine_b, up_b, down_b = near_products(place_b, slots_b, True, after=[re_b])
    sum_b = added(up_b, down_b, *got_b, 0.1)
    sent_b = both_ways(*sum_b, "col")
    re_a, im_a = far_products(place_a, slots_a, False, [sum_b[0]])
    got_a = both_ways(re_a, im_a, "row")
    mine_a, up_a, down_a, power_a = near_products(
        place_a, slots_a, False, size_b, beam_weights, [re_a]
    )
    sum_a = added(up_a, down_a, *got_a, 0.1)
    sent_a = both_ways(*sum_a, "row")

    power_b = jnp.transpose(turn(beam_b, "col"), (1, 0, 2, 3)).reshape(size_b, -1, beam_b.shape[3])
    out = finished(mine_b, *sent_b, 0, channels, None)
    visibility = finished(mine_a, *sent_a, size_b, channels, out)
    power = jnp.concatenate([power_b, power_a], axis=0)
    return (visibility, jnp.transpose(power, (0, 2, 1)))


def solution(mesh):
    placed = (P(None, "chan", ("row", "col")), P("chan"), P(), P(None, "chan", "col", None))
    return jax.shard_map(
        on_device,
        mesh=mesh,
        in_specs=placed,
        out_specs=(P(None, "chan", "row", "col"), P("chan", "col", "row")),
        check_vma=False,
    )
```
